32 devices in a mesh: dp: 16 (over z, y, x), head: 2 (over core).
Axes of the slice: x: 2, y: 2, z: 4, core: 2. Of those that a mesh axis runs over, the one named last changes fastest.
Arguments:
- tokens: bfloat16 [32768, 768], P(('dp', 'head')), may hold values from -6 to 6
- w_qkv: bfloat16 [768, 2304], replicated, may hold values from -0.21875 to 0.21875
- b_query: float32 [768], replicated, may hold values from -3 to 3
- b_value: float32 [768], replicated, may hold values from -0.3 to 0.3
- w_out: bfloat16 [768, 768], replicated, may hold values from -2.5 to 2.5
- b_out: float32 [768], replicated, may hold values from -2 to 2
- gain_attn: float32 [768], replicated, may hold values from 0.5 to 1.5
- shift_attn: float32 [768], replicated, may hold values from -2 to 2
- w_in: bfloat16 [768, 3072], replicated, may hold values from -0.21875 to 0.21875
- b_in: float32 [3072], replicated, may hold values from -2 to 2
- w_back: bfloat16 [3072, 768], replicated, may hold values from -0.109375 to 0.109375
- b_back: float32 [768], replicated, may hold values from -2 to 2
- gain_out: float32 [768], replicated, may hold values from 0.5 to 1.5
- shift_out: float32 [768], replicated, may hold values from -2 to 2
- grad_out: bfloat16 [32768, 768], P(('dp', 'head')), may hold values from -6 to 6
- masked: int32 [32768], P(('dp', 'head')), may hold values from 0 to 1, as said below
Outputs:
- layer_out: bfloat16 [32768, 768], P(('dp', 'head'))
- grad_tokens: float32 [32768, 768], P(('dp', 'head'))
- grad_w_qkv: float32 [768, 2304], P('dp', 'head')
- grad_b_query: float32 [768], replicated
- grad_b_value: float32 [768], replicated
- grad_w_out: float32 [768, 768], P('dp', 'head')
- grad_b_out: float32 [768], replicated
- grad_gain_attn: float32 [768], replicated
- grad_shift_attn: float32 [768], replicated
- grad_w_in: float32 [768, 3072], P('dp', 'head')
- grad_b_in: float32 [3072], replicated
- grad_w_back: float32 [3072, 768], P('dp', 'head')
- grad_b_back: float32 [768], replicated
- grad_gain_out: float32 [768], replicated
- grad_shift_out: float32 [768], replicated
The draws below stay inside these ranges and needn't reach their ends.
Inputs may be any that keep to these rules, and one draw needn't show every extreme that they name: `masked`: among the 1024 tokens of one device (aligned blocks of rows) at most 320 are marked and at least one; in every draw some device has exactly 320.
All inputs are finite; a program needn't handle non-finite values.
Results may differ from the reference program's by a relative error of at most 0.015.
Values may be sent and summed in bfloat16 or wider, within the bound.
No kernel may reach another device: no remote copies, remote signals or barrier semaphores. Data moves between devices by JAX's collectives and lax.ppermute only.
A program may use at most 192 MiB of HBM per device.

```python
import jax
import jax.numpy as jnp
from jax import lax

D = 768
HEADS = 12
HEAD_DIM = 64
FF = 3072
LEN = 512
SEQS_DP = 4
TOKENS = 32768
ROWS_DEV = 1024
CAP = 320
N_DP = 16


def draw_masked(key, part):
    key = jax.random.fold_in(key, 7)
    count_key, full_key, order_key = jax.random.split(key, 3)
    blocks = TOKENS // ROWS_DEV
    least = max(1, ROWS_DEV // 20)
    counts = jax.random.randint(count_key, (blocks,), least, CAP + 1)
    fullest = jax.random.randint(full_key, (), 0, blocks)
    counts = jnp.where(jnp.arange(blocks) == fullest, CAP, counts)
    scores = jax.random.randint(order_key, (blocks, ROWS_DEV), 0, ROWS_DEV) * ROWS_DEV + jnp.arange(ROWS_DEV)[None, :]
    ranks = jnp.argsort(jnp.argsort(scores, axis=1), axis=1)
    return (ranks < counts[:, None]).astype(jnp.int32).reshape(TOKENS)


def levels(stream_key, shape, shards, smallest, high):
    factor_of, own = 1.0, jax.random.fold_in(stream_key, 6)
    for dim, parts in shards:
        draws = jnp.exp(jax.random.uniform(jax.random.fold_in(own, dim), (parts,), jnp.float32, smallest / len(shards), high / len(shards)))
        factor_of = factor_of * jnp.repeat(draws, shape[dim] // parts).reshape([-1 if axis == dim else 1 for axis in range(len(shape))])
    return factor_of


def scatter_about(rng, shape, spread, bound, cuts=(), dtype=jnp.bfloat16):
    loudness = levels(rng, shape, cuts, -0.22, 0.18) if cuts else 1.0
    entries = jax.random.normal(rng, shape, jnp.float32) * spread * loudness
    return jnp.minimum(jnp.maximum(entries, -bound), bound).astype(dtype)


def setup_inputs(seed: int = 0) -> dict:
    keys = jax.random.split(jax.random.key(seed), 17)
    tokens = scatter_about(keys[0], (TOKENS, D), 1.0, 6.0, ((0, 32),))
    w_qkv = scatter_about(keys[1], (D, 3 * D), D ** -0.5, 0.21875)
    b_query = scatter_about(keys[2], (D,), 0.5, 3.0, (), jnp.float32)
    b_value = scatter_about(keys[3], (D,), 0.05, 0.3, (), jnp.float32)
    w_out = scatter_about(keys[4], (D, D), (D * 4 // LEN) ** -0.5, 2.5)
    b_out = scatter_about(keys[5], (D,), 0.3, 2.0, (), jnp.float32)
    gain_attn = jnp.clip(1.0 + 0.1 * jax.random.normal(keys[6], (D,), jnp.float32), 0.5, 1.5)
    shift_attn = scatter_about(keys[7], (D,), 0.3, 2.0, (), jnp.float32)
    w_in = scatter_about(keys[8], (D, FF), D ** -0.5, 0.21875)
    b_in = scatter_about(keys[9], (FF,), 0.3, 2.0, (), jnp.float32)
    w_back = scatter_about(keys[10], (FF, D), FF ** -0.5, 0.109375)
    b_back = scatter_about(keys[11], (D,), 0.3, 2.0, (), jnp.float32)
    gain_out = jnp.clip(1.0 + 0.1 * jax.random.normal(keys[12], (D,), jnp.float32), 0.5, 1.5)
    shift_out = scatter_about(keys[13], (D,), 0.3, 2.0, (), jnp.float32)
    grad_out = scatter_about(keys[14], (TOKENS, D), 1.0, 6.0, ((0, 32),))
    masked = draw_masked(jax.random.fold_in(keys[16], 71), 0)
    return {"tokens": tokens, "w_qkv": w_qkv, "b_query": b_query, "b_value": b_value, "w_out": w_out, "b_out": b_out, "gain_attn": gain_attn, "shift_attn": shift_attn, "w_in": w_in, "b_in": b_in, "w_back": w_back, "b_back": b_back, "gain_out": gain_out, "shift_out": shift_out, "grad_out": grad_out, "masked": masked}


epsilon = 1e-12
precise = lax.Precision.HIGHEST

@jax.custom_vjp
def low(v):
    return lax.optimization_barrier(v.astype(jnp.bfloat16)).astype(jnp.float32)

@jax.custom_vjp
def low_back(v):
    return v

def low_keep(v):
    return (low(v), None)

def low_pass(kept, grad):
    return (grad,)

def back_keep(v):
    return (v, None)

def back_low(kept, grad):
    return (low(grad),)
low.defvjp(low_keep, low_pass)
low_back.defvjp(back_keep, back_low)

def norm_rows(values, gain, shift):
    mean = lax.optimization_barrier(jnp.mean(values, axis=-1, keepdims=True))
    centred = values - mean
    variance = lax.optimization_barrier(jnp.mean(centred * centred, axis=-1, keepdims=True))
    return centred * lax.rsqrt(variance + epsilon) * gain + shift

def attend_one(triple):
    query, key_rows, value = triple
    scores = low_back(jnp.einsum('qhd,khd->hqk', query, key_rows, precision=precise) * HEAD_DIM ** (-0.5))
    probs = low(jax.nn.softmax(scores, axis=-1))
    context = jnp.einsum('hqk,khd->qhd', probs, value, precision=precise)
    return low(low_back(context))

def layer(block, w_qkv, b_query, b_value, w_out, b_out, gain_attn, shift_attn, w_in, b_in, w_back, b_back, gain_out, shift_out):
    count = block.shape[0]
    bias = jnp.concatenate([b_query, jnp.zeros_like(b_query), b_value])
    qkv = low(low_back(jnp.dot(block, w_qkv, precision=precise) + bias))
    qkv = qkv.reshape(count // LEN, LEN, 3, HEADS, HEAD_DIM)
    context = lax.map(jax.checkpoint(attend_one), (qkv[:, :, 0], qkv[:, :, 1], qkv[:, :, 2]))
    context = context.reshape(count, D)
    attn = low_back(jnp.dot(context, w_out, precision=precise) + b_out)
    hidden = norm_rows(block + attn, gain_attn, shift_attn)
    inner = low_back(jnp.dot(low(hidden), w_in, precision=precise) + b_in)
    active = low(jax.nn.gelu(inner, approximate=False))
    branch = low_back(jnp.dot(active, w_back, precision=precise) + b_back)
    return norm_rows(hidden + branch, gain_out, shift_out)

def reference(tokens, w_qkv, b_query, b_value, w_out, b_out, gain_attn, shift_attn, w_in, b_in, w_back, b_back, gain_out, shift_out, grad_out, masked):
    params = tuple((entry.astype(jnp.float32) for entry in (w_qkv, b_query, b_value, w_out, b_out, gain_attn, shift_attn, w_in, b_in, w_back, b_back, gain_out, shift_out)))
    group = SEQS_DP * LEN
    inputs = tokens.astype(jnp.float32).reshape(N_DP, group, D)
    flags = masked.astype(jnp.float32)[:, None]
    cotangents = (grad_out.astype(jnp.float32) * flags).reshape(N_DP, group, D)

    def advance(totals, entry):
        block, cotangent = entry
        result, pullback = jax.vjp(layer, block, *params)
        grads = pullback(cotangent)
        totals = jax.tree.map(jnp.add, totals, tuple(grads[1:]))
        return (totals, (result, grads[0]))
    zeros = tuple((jnp.zeros_like(entry) for entry in params))
    totals, (results, input_grads) = lax.scan(advance, zeros, (inputs, cotangents))
    layer_out = results.reshape(TOKENS, D).astype(jnp.bfloat16)
    grad_tokens = input_grads.reshape(TOKENS, D)
    return (layer_out, grad_tokens, totals[0], totals[1], totals[2], totals[3], totals[4], totals[5], totals[6], totals[7], totals[8], totals[9], totals[10], totals[11], totals[12])
```

```python
import functools

import jax
import jax.numpy as jnp
from jax import lax
from jax.experimental import pallas as pl
from jax.experimental.pallas import tpu as pltpu
from jax.sharding import PartitionSpec as P

HEADS = 12
HEAD_DIM = 64
LEN = 512
CAP = 320
TILE = 64
SLOTS = (CAP // TILE + 1) * TILE
QUAD = 4 * HEAD_DIM
VMEM_LIMIT = 60 * 1024 * 1024

epsilon = 1e-12
bf16 = jnp.bfloat16
f32 = jnp.float32


def mm(a, b):
    return jnp.dot(a, b, preferred_element_type=f32)


def mm_nt(a, b):
    return lax.dot_general(a, b, (((1,), (1,)), ((), ())), preferred_element_type=f32)


def mm_tn(a, b):
    return lax.dot_general(a, b, (((0,), (0,)), ((), ())), preferred_element_type=f32)


def colsum(v):
    return jnp.sum(v, axis=0, keepdims=True)


def rowmean(v):
    return jnp.sum(v, axis=-1, keepdims=True) * (1.0 / v.shape[-1])


def norm_parts(v):
    centred = v - rowmean(v)
    r = lax.rsqrt(rowmean(centred * centred) + epsilon)
    return centred * r, r


def norm_back(cot, nhat, r, gain):
    e = cot * gain
    return r * (e - rowmean(e) - nhat * rowmean(e * nhat))


def phi_parts(v):
    x = jnp.abs(v)
    t = 1.0 / (1.0 + (0.3275911 * 0.7071067811865476) * x)
    e = jnp.exp(v * v * -0.5)
    poly = 0.5 * 1.061405429 * t + 0.5 * -1.453152027
    poly = poly * t + 0.5 * 1.421413741
    poly = poly * t + 0.5 * -0.284496736
    poly = poly * t + 0.5 * 0.254829592
    tail = poly * t * e
    return jnp.where(v >= 0.0, 1.0 - tail, tail), e


def lane_masks(dtype):
    head = lax.broadcasted_iota(jnp.int32, (1, QUAD), 1) // HEAD_DIM
    return [(head == j).astype(f32).astype(dtype) for j in range(4)]


def spread(x, masks):
    return jnp.concatenate([x * m for m in masks], axis=0)


def gather_heads(x, masks):
    n = x.shape[0] // 4
    total = x[:n] * masks[0]
    for j in range(1, 4):
        total = total + x[j * n : (j + 1) * n] * masks[j]
    return total


def softmax_rows(scores):
    e = jnp.exp(scores - jnp.max(scores, axis=-1, keepdims=True))
    return (e * (1.0 / jnp.sum(e, axis=-1, keepdims=True))).astype(bf16)


class Mover:
    def __init__(self, sems):
        self.sems = sems
        self.count = 0

    def start(self, src, dst):
        copy = pltpu.make_async_copy(src, dst, self.sems.at[self.count])
        self.count += 1
        copy.start()
        return copy


def marked_forward_kernel(
    core_ref, m_ref, bq_ref, bv_ref, bo_ref, g1_ref, s1_ref, bi_ref, bb_ref, g2_ref,
    tok_h, gout_h, wqkv_h, wout_h, win_h, wback_h,
    sel_h, kv_h, tokc_h, qs_h, p_h, ctx_h, nhat_h, r_h, hl_h, act_h, bbr_h, bin_h, bsum_h, xsend_h, small_ref,
    tok, gout, wqkv, wout, win, wback,
    sel, kv, tokc, gc, qs, prob, ctx, nhat, rr, hidden, hl, act, gp, branch, bbr, bin_, bsum, bv, bi,
    sems,
):
    rows, width = tok.shape
    ff = win.shape[1]
    mover = Mover(sems)
    other = 1 - core_ref[0]
    c_tok = mover.start(tok_h, tok)
    c_wqkv = mover.start(wqkv_h, wqkv)
    c_gout = mover.start(gout_h, gout)
    c_wout = mover.start(wout_h, wout)
    c_win = mover.start(win_h, win)
    c_wback = mover.start(wback_h, wback)
    outs = []
    bv[...] = bv_ref[...].reshape(bv.shape)
    bi[...] = bi_ref[...].reshape(bi.shape)
    m8 = m_ref[...].astype(f32)
    groups = m8.shape[0]
    per_seq = LEN // 128
    tri = (
        lax.broadcasted_iota(jnp.int32, (128, 128), 0)
        <= lax.broadcasted_iota(jnp.int32, (128, 128), 1)
    ).astype(f32).astype(bf16)
    within = mm(m8.astype(bf16), tri)
    first = jnp.sum(m8[:per_seq], axis=(0, 1), keepdims=True)
    a0 = jnp.floor((first + (TILE - 1)) * (1.0 / TILE)) * TILE
    offset = jnp.zeros((1, 1), f32)
    slot_iota = lax.broadcasted_iota(jnp.int32, (SLOTS, 128), 0).astype(f32)
    for g in range(groups):
        if g == per_seq:
            offset = a0
        slot = jnp.where(m8[g : g + 1] > 0.0, offset + within[g : g + 1] - 1.0, -1.0)
        sel[:, 128 * g : 128 * (g + 1)] = (slot_iota == slot).astype(f32).astype(bf16)
        offset = offset + within[g : g + 1, 127:128]
    outs.append(mover.start(sel, sel_h))
    a0_scalar = jnp.sum(a0).astype(jnp.int32)

    c_tok.wait()
    tokc[...] = mm(sel[...], tok[...]).astype(bf16)
    outs.append(mover.start(tokc, tokc_h))
    c_wqkv.wait()

    @pl.loop(0, 2 * width // 256)
    def _(i):
        at = pl.multiple_of(i * 256, 256)
        bias = jnp.where(i >= width // 256, bv[:, pl.ds(pl.multiple_of(lax.rem(at, width), 256), 256)], 0.0)
        kv[:, pl.ds(at, 256)] = (
            mm(tok[...], wqkv[:, pl.ds(pl.multiple_of(width + at, 256), 256)]) + bias
        ).astype(bf16)

    outs.append(mover.start(kv, kv_h))
    qs[...] = (
        (mm(tokc[...], wqkv[:, :width]) + bq_ref[...]).astype(bf16).astype(f32) * HEAD_DIM**-0.5
    ).astype(bf16)
    outs.append(mover.start(qs, qs_h))

    masks = lane_masks(bf16)
    fmasks = lane_masks(f32)

    @pl.loop(0, SLOTS // TILE)
    def _(t):
        r0 = pl.multiple_of(t * TILE, TILE)
        k0 = pl.multiple_of(jnp.where(r0 >= a0_scalar, LEN, 0), LEN)
        for g in range(width // QUAD):
            lanes = slice(g * QUAD, (g + 1) * QUAD)
            q4 = spread(qs[pl.ds(r0, TILE), lanes], masks)
            scores = mm_nt(q4, kv[pl.ds(k0, LEN), lanes])
            p = softmax_rows(scores)
            prob[t * (width // QUAD) + g] = p
            o = mm(p, kv[pl.ds(k0, LEN), width + g * QUAD : width + (g + 1) * QUAD])
            ctx[pl.ds(r0, TILE), lanes] = gather_heads(o, fmasks).astype(bf16)

    outs.append(mover.start(prob, p_h))
    outs.append(mover.start(ctx, ctx_h))
    c_wout.wait()
    pre = mm(ctx[...], wout[...]) + bo_ref[...] + tokc[...].astype(f32)
    nh, r = norm_parts(pre)
    nhat[...] = nh
    rr[...] = jnp.broadcast_to(r, rr.shape)
    outs.append(mover.start(nhat, nhat_h))
    outs.append(mover.start(rr, r_h))
    hid = nh * g1_ref[...] + s1_ref[...]
    hidden[...] = hid
    hl[...] = hid.astype(bf16)
    outs.append(mover.start(hl, hl_h))
    outs.append(mover.start(hl, xsend_h.at[:, ff : ff + width]))
    c_gout.wait()
    gc[...] = mm(sel[...], gout[...]).astype(bf16)
    c_win.wait()
    c_wback.wait()

    @pl.loop(0, ff // 256)
    def _(i):
        at = pl.ds(pl.multiple_of(i * 256, 256), 256)
        v = mm(hl[...], win[:, at]) + bi[:, at]
        cdf, e = phi_parts(v)
        act[:, at] = (v * cdf).astype(bf16)
        gp[:, at] = cdf + v * (e * 0.3989422804014327)

    outs.append(mover.start(act, act_h))
    outs.append(mover.start(act, xsend_h.at[:, :ff]))

    @pl.loop(0, width // 256)
    def _(i):
        at = pl.ds(pl.multiple_of(i * 256, 256), 256)
        branch[:, at] = mm(act[...], wback[:, at])

    nh2, r2 = norm_parts(hidden[...] + branch[...] + bb_ref[...])
    cot = gc[...].astype(f32)
    bs = norm_back(cot, nh2, r2, g2_ref[...])
    bsum[...] = bs
    outs.append(mover.start(bsum, bsum_h))
    bl = bs.astype(bf16)
    bbr[...] = bl
    outs.append(mover.start(bbr, bbr_h))
    half = width // 2
    outs.append(
        mover.start(
            bbr.at[:, pl.ds(pl.multiple_of(other * half, half), half)],
            xsend_h.at[:, ff + width : ff + width + half],
        )
    )
    small_ref[:, :width] = colsum(cot * nh2)
    small_ref[:, width : 2 * width] = colsum(cot)
    small_ref[:, 2 * width : 3 * width] = colsum(bl.astype(f32))

    @pl.loop(0, ff // 256)
    def _(i):
        start = pl.multiple_of(i * 256, 256)
        at = pl.ds(start, 256)
        b = (mm_nt(bbr[...], wback[at, :]) * gp[:, at]).astype(bf16)
        bin_[:, at] = b
        small_ref[:, pl.ds(pl.multiple_of(3 * width + start, 256), 256)] = colsum(b.astype(f32))

    outs.append(mover.start(bin_, bin_h))
    outs.append(
        mover.start(
            bin_.at[:, pl.ds(pl.multiple_of(other * (ff // 2), ff // 2), ff // 2)],
            xsend_h.at[:, ff + width + half :],
        )
    )
    for copy in outs:
        copy.wait()


def marked_forward(core, m8, tokens, gout, w_qkv, b_query, b_value, w_out, b_out, g1, s1, w_in, b_in, w_back, b_back, g2):
    rows, width = tokens.shape
    ff = w_in.shape[1]
    tiles = SLOTS // TILE * (width // QUAD)
    row = lambda v: v
    outs = dict(
        sel=((SLOTS, rows), bf16), kv=((rows, 2 * width), bf16), tokc=((SLOTS, width), bf16),
        qs=((SLOTS, width), bf16), p=((tiles, 4 * TILE, LEN), bf16), ctx=((SLOTS, width), bf16),
        nhat=((SLOTS, width), f32), r=((SLOTS, 128), f32), hl=((SLOTS, width), bf16),
        act=((SLOTS, ff), bf16), bbr=((SLOTS, width), bf16), bin=((SLOTS, ff), bf16),
        bsum=((SLOTS, width), f32), xsend=((SLOTS, (ff + width) * 3 // 2), bf16), small=((1, 3 * width + ff), f32),
    )
    scratch = [
        ((rows, width), bf16), ((rows, width), bf16), (w_qkv.shape, bf16), (w_out.shape, bf16),
        (w_in.shape, bf16), (w_back.shape, bf16),
        outs["sel"], outs["kv"], outs["tokc"], ((SLOTS, width), bf16), outs["qs"], outs["p"], outs["ctx"],
        outs["nhat"], outs["r"], ((SLOTS, width), f32), outs["hl"], outs["act"], ((SLOTS, ff), f32),
        ((SLOTS, width), f32), outs["bbr"], outs["bin"], outs["bsum"], ((1, width), f32), ((1, ff), f32),
    ]
    vmem = pl.BlockSpec(memory_space=pltpu.VMEM)
    smem = pl.BlockSpec(memory_space=pltpu.SMEM)
    hbm = pl.BlockSpec(memory_space=pl.ANY)
    res = pl.pallas_call(
        marked_forward_kernel,
        out_shape=[jax.ShapeDtypeStruct(*o) for o in outs.values()],
        in_specs=[smem] + [vmem] * 9 + [hbm] * 6,
        out_specs=[hbm] * 14 + [vmem],
        scratch_shapes=[pltpu.VMEM(*s) for s in scratch] + [pltpu.SemaphoreType.DMA((28,))],
        compiler_params=pltpu.CompilerParams(vmem_limit_bytes=VMEM_LIMIT),
        cost_estimate=pl.CostEstimate(flops=12 * 10**9, bytes_accessed=40 * 10**6, transcendentals=0),
        name="marked_forward",
    )(core, m8, row(b_query), row(b_value), row(b_out), row(g1), row(s1), row(b_in), row(b_back), row(g2),
      tokens, gout, w_qkv, w_out, w_in, w_back)
    return dict(zip(outs, res))


def marked_backward_kernel(
    m_ref, g1_ref,
    win_h, wout_h, wqkv_h, bin_h, bsum_h, nhat_h, r_h, ctx_h, p_h, qs_h, kv_h,
    battn_h, bq_h, bkv_h, rc_h, small_ref,
    win, wout, wq, bin_, bsum, nhat, rr, ctx, prob, qs, kv,
    bh, bpre, battn, bctx, dk, dv, bq, bkv, rc,
    sems,
):
    rows, width = kv.shape[0], qs.shape[1]
    mover = Mover(sems)
    c_bin = mover.start(bin_h, bin_)
    c_win = mover.start(win_h, win)
    c_bsum = mover.start(bsum_h, bsum)
    c_nhat = mover.start(nhat_h, nhat)
    c_r = mover.start(r_h, rr)
    c_wout = mover.start(wout_h, wout)
    c_att = [mover.start(s, d) for s, d in ((ctx_h, ctx), (p_h, prob), (qs_h, qs), (kv_h, kv))]
    c_wq = mover.start(wqkv_h.at[:, :width], wq)
    outs = []
    per_seq = LEN // 128
    first = jnp.sum(m_ref[:per_seq].astype(f32), axis=(0, 1), keepdims=True)
    a0_scalar = jnp.sum(jnp.floor((first + (TILE - 1)) * (1.0 / TILE)) * TILE).astype(jnp.int32)
    dk[...] = jnp.zeros_like(dk)
    dv[...] = jnp.zeros_like(dv)
    for c in (c_bin, c_win, c_bsum):
        c.wait()

    @pl.loop(0, width // 256)
    def _(i):
        at = pl.ds(pl.multiple_of(i * 256, 256), 256)
        bh[:, at] = bsum[:, at] + mm_nt(bin_[...], win[at, :])

    c_nhat.wait()
    c_r.wait()
    back_hidden = bh[...]
    nh = nhat[...]
    bp = norm_back(back_hidden, nh, rr[:, :1], g1_ref[...])
    bpre[...] = bp
    bl = bp.astype(bf16)
    battn[...] = bl
    outs.append(mover.start(battn, battn_h))
    small_ref[:, :width] = colsum(bl.astype(f32))
    small_ref[:, width : 2 * width] = colsum(back_hidden * nh)
    small_ref[:, 2 * width : 3 * width] = colsum(back_hidden)
    c_wout.wait()
    bctx[...] = mm_nt(bl, wout[...]).astype(bf16)
    for c in c_att:
        c.wait()
    masks = lane_masks(bf16)
    fmasks = lane_masks(f32)

    @pl.loop(0, SLOTS // TILE)
    def _(t):
        r0 = pl.multiple_of(t * TILE, TILE)
        k0 = pl.multiple_of(jnp.where(r0 >= a0_scalar, LEN, 0), LEN)
        for g in range(width // QUAD):
            lanes = slice(g * QUAD, (g + 1) * QUAD)
            d = bctx[pl.ds(r0, TILE), lanes]
            d4 = spread(d, masks)
            q4 = spread(qs[pl.ds(r0, TILE), lanes], masks)
            prod = d.astype(f32) * ctx[pl.ds(r0, TILE), lanes].astype(f32)
            delta = jnp.concatenate(
                [jnp.sum(prod * m, axis=-1, keepdims=True) for m in fmasks], axis=0
            )
            p = prob[t * (width // QUAD) + g]
            dp = mm_nt(d4, kv[pl.ds(k0, LEN), width + g * QUAD : width + (g + 1) * QUAD])
            ds = (p.astype(f32) * (dp - delta)).astype(bf16)
            dv[pl.ds(k0, LEN), lanes] += mm_tn(p, d4)
            dk[pl.ds(k0, LEN), lanes] += mm_tn(ds, q4)
            o = mm(ds, kv[pl.ds(k0, LEN), lanes])
            bq[pl.ds(r0, TILE), lanes] = (gather_heads(o, fmasks) * HEAD_DIM**-0.5).astype(bf16)

    outs.append(mover.start(bq, bq_h))
    c_wq.wait()
    rc[...] = (bpre[...] + mm_nt(bq[...], wq[...])).astype(bf16)
    outs.append(mover.start(rc, rc_h))
    bkv[:, :width] = dk[...].astype(bf16)
    bvl = dv[...].astype(bf16)
    bkv[:, width:] = bvl
    outs.append(mover.start(bkv, bkv_h))
    small_ref[:, 3 * width : 4 * width] = colsum(bq[...].astype(f32))
    small_ref[:, 4 * width :] = colsum(bvl.astype(f32))
    for copy in outs:
        copy.wait()


def marked_backward(m8, g1, w_in, w_out, w_qkv, a):
    rows = a["sel"].shape[1]
    width, ff = w_in.shape
    outs = dict(
        battn=((SLOTS, width), bf16), bq=((SLOTS, width), bf16), bkv=((rows, 2 * width), bf16),
        rc=((SLOTS, width), bf16), small=((1, 5 * width), f32),
    )
    ins = [a[k] for k in ("bin", "bsum", "nhat", "r", "ctx", "p", "qs", "kv")]
    scratch = [(w_in.shape, bf16), (w_out.shape, bf16), ((width, width), bf16)]
    scratch += [(v.shape, v.dtype) for v in ins]
    scratch += [
        ((SLOTS, width), f32), ((SLOTS, width), f32), outs["battn"], ((SLOTS, width), bf16),
        ((rows, width), f32), ((rows, width), f32), outs["bq"], outs["bkv"], outs["rc"],
    ]
    vmem = pl.BlockSpec(memory_space=pltpu.VMEM)
    smem = pl.BlockSpec(memory_space=pltpu.SMEM)
    hbm = pl.BlockSpec(memory_space=pl.ANY)
    res = pl.pallas_call(
        marked_backward_kernel,
        out_shape=[jax.ShapeDtypeStruct(*o) for o in outs.values()],
        in_specs=[vmem] * 2 + [hbm] * 11,
        out_specs=[hbm] * 4 + [vmem],
        scratch_shapes=[pltpu.VMEM(*s) for s in scratch] + [pltpu.SemaphoreType.DMA((28,))],
        compiler_params=pltpu.CompilerParams(vmem_limit_bytes=VMEM_LIMIT),
        cost_estimate=pl.CostEstimate(flops=8 * 10**9, bytes_accessed=40 * 10**6, transcendentals=0),
        name="marked_backward",
    )(m8, g1, w_in, w_out, w_qkv, *ins)
    return dict(zip(outs, res))


BLOCK = 256


def layer_rows_kernel(
    which, bq_ref, bo_ref, g1_ref, s1_ref, bi_ref, bb_ref, g2_ref, s2_ref,
    tok_h, kv_h, wqkv_h, wout_h, win_h, wback_h, *rest,
):
    (out_h, tok, kv, wq, wout, win, wback, q, ctx, hl, hidden, act, branch, out, bi, sems) = rest[-16:]
    width = wq.shape[1]
    ff = win.shape[1]
    mover = Mover(sems)
    i = which[0]
    r0 = pl.multiple_of(i * BLOCK, BLOCK)
    k0 = pl.multiple_of(i // (LEN // BLOCK) * LEN, LEN)
    c_tok = mover.start(tok_h.at[pl.ds(r0, BLOCK), :], tok)
    c_wq = mover.start(wqkv_h.at[:, :width], wq)
    c_kv = mover.start(kv_h.at[pl.ds(k0, LEN), :], kv)
    c_wout = mover.start(wout_h, wout)
    c_win = mover.start(win_h, win)
    c_wback = mover.start(wback_h, wback)
    bi[...] = bi_ref[...].reshape(bi.shape)
    c_tok.wait()
    c_wq.wait()
    q[...] = ((mm(tok[...], wq[...]) + bq_ref[...]).astype(bf16).astype(f32) * HEAD_DIM**-0.5).astype(bf16)
    c_kv.wait()
    masks = lane_masks(bf16)
    fmasks = lane_masks(f32)

    @pl.loop(0, BLOCK // TILE)
    def _(t):
        at = pl.ds(pl.multiple_of(t * TILE, TILE), TILE)
        for g in range(width // QUAD):
            lanes = slice(g * QUAD, (g + 1) * QUAD)
            p = softmax_rows(mm_nt(spread(q[at, lanes], masks), kv[:, lanes]))
            o = mm(p, kv[:, width + g * QUAD : width + (g + 1) * QUAD])
            ctx[at, lanes] = gather_heads(o, fmasks).astype(bf16)

    c_wout.wait()
    nh, _ = norm_parts(mm(ctx[...], wout[...]) + bo_ref[...] + tok[...].astype(f32))
    hid = nh * g1_ref[...] + s1_ref[...]
    hidden[...] = hid
    hl[...] = hid.astype(bf16)
    c_win.wait()

    @pl.loop(0, ff // 256)
    def _(j):
        at = pl.ds(pl.multiple_of(j * 256, 256), 256)
        v = mm(hl[...], win[:, at]) + bi[:, at]
        act[:, at] = (v * phi_parts(v)[0]).astype(bf16)

    c_wback.wait()

    @pl.loop(0, width // 256)
    def _(j):
        at = pl.ds(pl.multiple_of(j * 256, 256), 256)
        branch[:, at] = mm(act[...], wback[:, at])

    nh2, _ = norm_parts(hidden[...] + branch[...] + bb_ref[...])
    out[...] = (nh2 * g2_ref[...] + s2_ref[...]).astype(bf16)
    mover.start(out, out_h.at[pl.ds(r0, BLOCK), :]).wait()


def layer_rows(which, previous, tokens, kv, w_qkv, b_query, w_out, b_out, g1, s1, w_in, b_in, w_back, b_back, g2, s2):
    rows, width = tokens.shape
    ff = w_in.shape[1]
    row = lambda v: v
    vmem = pl.BlockSpec(memory_space=pltpu.VMEM)
    smem = pl.BlockSpec(memory_space=pltpu.SMEM)
    hbm = pl.BlockSpec(memory_space=pl.ANY)
    scratch = [
        ((BLOCK, width), bf16), ((LEN, 2 * width), bf16), ((width, width), bf16), (w_out.shape, bf16),
        (w_in.shape, bf16), (w_back.shape, bf16), ((BLOCK, width), bf16), ((BLOCK, width), bf16),
        ((BLOCK, width), bf16), ((BLOCK, width), f32), ((BLOCK, ff), bf16), ((BLOCK, width), f32),
        ((BLOCK, width), bf16), ((1, ff), f32),
    ]
    extra = () if previous is None else (previous,)
    return pl.pallas_call(
        layer_rows_kernel,
        out_shape=jax.ShapeDtypeStruct((rows, width), bf16),
        in_specs=[smem] + [vmem] * 8 + [hbm] * (6 + len(extra)),
        out_specs=hbm,
        scratch_shapes=[pltpu.VMEM(*s) for s in scratch] + [pltpu.SemaphoreType.DMA((8,))],
        input_output_aliases={15: 0} if extra else {},
        compiler_params=pltpu.CompilerParams(vmem_limit_bytes=VMEM_LIMIT),
        cost_estimate=pl.CostEstimate(flops=3 * 10**9, bytes_accessed=20 * 10**6, transcendentals=0),
        name="layer_rows",
    )(jnp.full((1,), which, jnp.int32), row(b_query), row(b_out), row(g1), row(s1), row(b_in), row(b_back), row(g2), row(s2),
      tokens, kv, w_qkv, w_out, w_in, w_back, *extra)


def place(piece, own, order):
    bits = piece ^ own
    spot = 0
    for step in order:
        spot = spot * 2 + ((bits >> step) & 1)
    return spot


def store_pieces(ref, value, first, size, own, order, lanes):
    for k in range(value.shape[0] // size):
        at = pl.multiple_of(place(first + k, own, order) * size, size)
        ref[pl.ds(at, size), lanes] = value[k * size : (k + 1) * size]


def ffn_grads_kernel(
    where, act_h, hl_h, bbr_h, bin_h, x_h, keep1_h, send1_h, keep2_h, send2_h,
    act, hl, bbr, bin_, out1, out2, sems, *, pieces, orders,
):
    own, core = where[0], where[1]
    slots, ff = act_h.shape
    width = hl_h.shape[1]
    half = width // 2
    mover = Mover(sems)
    up, down = slice(0, slots), slice(slots, 2 * slots)
    mine = lambda n: pl.ds(pl.multiple_of(core * n, n), n)
    c1 = [
        mover.start(act_h, act.at[up, :]),
        mover.start(x_h.at[:, :ff], act.at[down, :]),
        mover.start(bbr_h.at[:, mine(half)], bbr.at[up, :]),
        mover.start(x_h.at[:, ff + width : ff + width + half], bbr.at[down, :]),
    ]
    c2 = [
        mover.start(hl_h, hl.at[up, :]),
        mover.start(x_h.at[:, ff : ff + width], hl.at[down, :]),
        mover.start(bin_h.at[:, mine(ff // 2)], bin_.at[up, :]),
        mover.start(x_h.at[:, ff + width + half :], bin_.at[down, :]),
    ]
    for c in c1:
        c.wait()
    size = ff // pieces
    step = 384

    @pl.loop(0, ff // step)
    def _(j):
        g = mm_tn(act[:, pl.ds(pl.multiple_of(j * step, step), step)], bbr[...]).astype(bf16)
        store_pieces(out1, g, j * (step // size), size, own, orders[0], slice(None))

    rows = ff // 2
    outs = [mover.start(out1.at[rows:, :], send1_h), mover.start(out1.at[:rows, :], keep1_h)]
    for c in c2:
        c.wait()
    size = width // pieces
    for i in range(width // step):
        hlt = hl[:, i * step : (i + 1) * step].T

        @pl.loop(0, ff // 2 // 512)
        def _(j):
            lanes = pl.ds(pl.multiple_of(j * 512, 512), 512)
            g = mm(hlt, bin_[:, lanes]).astype(bf16)
            store_pieces(out2, g, i * (step // size), size, own, orders[1], lanes)

    outs += [mover.start(out2.at[half:, :], send2_h), mover.start(out2.at[:half, :], keep2_h)]
    for c in outs:
        c.wait()


def ffn_grads(where, a, x, pieces, orders):
    slots, ff = a["act"].shape
    width = a["hl"].shape[1]
    smem = pl.BlockSpec(memory_space=pltpu.SMEM)
    hbm = pl.BlockSpec(memory_space=pl.ANY)
    one, two = (ff // 2, width // 2), (width // 2, ff // 2)
    scratch = [
        (2 * slots, ff), (2 * slots, width), (2 * slots, width // 2), (2 * slots, ff // 2),
        (ff, width // 2), (width, ff // 2),
    ]
    return pl.pallas_call(
        functools.partial(ffn_grads_kernel, pieces=pieces, orders=orders),
        out_shape=[jax.ShapeDtypeStruct(s, bf16) for s in (one, one, two, two)],
        in_specs=[smem] + [hbm] * 5,
        out_specs=[hbm] * 4,
        scratch_shapes=[pltpu.VMEM(s, bf16) for s in scratch] + [pltpu.SemaphoreType.DMA((12,))],
        compiler_params=pltpu.CompilerParams(vmem_limit_bytes=VMEM_LIMIT),
        cost_estimate=pl.CostEstimate(flops=4 * 10**9, bytes_accessed=15 * 10**6, transcendentals=0),
        name="ffn_grads",
    )(where, a["act"], a["hl"], a["bbr"], a["bin"], x)


def projection_grads_kernel(
    where, tokc_h, bq_h, ctx_h, battn_h, tok_h, bkv_h, keep_h, send_h,
    tokc, bq, ctx, battn, tok, bkv, tokt, out, sems, *, pieces, order,
):
    own, core = where[0], where[1]
    width = tok.shape[1]
    half = width // 2
    size = width // pieces
    mover = Mover(sems)
    c1 = [mover.start(tok_h, tok), mover.start(bkv_h, bkv)]
    c2 = [mover.start(tokc_h, tokc), mover.start(bq_h, bq)]
    c3 = [mover.start(ctx_h, ctx), mover.start(battn_h, battn)]

    def products(left, right, columns, first, lanes):
        for i in range(2):
            g = mm(left[i * half : (i + 1) * half, :], right[:, columns]).astype(bf16)
            for k in range(half // size):
                at = pl.multiple_of(place(i * (half // size) + k, own, order) * size, size)
                out[first, pl.ds(at, size), lanes] = g[k * size : (k + 1) * size]

    for c in c1:
        c.wait()
    tokt[...] = tok[...].T

    @pl.loop(2, 6)
    def _(j):
        columns = pl.ds(pl.multiple_of((j - 2) * half, half), half)
        lanes = pl.ds(pl.multiple_of(lax.rem(j, 3) * half, half), half)
        products(tokt, bkv, columns, (j // 3) ^ core, lanes)

    for c in c2:
        c.wait()
    tokt[:, : tokc.shape[0]] = tokc[...].T
    short = tokt.at[:, : tokc.shape[0]]
    for j in range(2):
        columns = slice(j * half, (j + 1) * half)
        products(short, bq, columns, core, columns)
    for c in c3:
        c.wait()
    tokt[:, : tokc.shape[0]] = ctx[...].T
    for j in range(2):
        products(short, battn, slice(j * half, (j + 1) * half), j ^ core, slice(3 * half, 4 * half))
    outs = [mover.start(out.at[1], send_h), mover.start(out.at[0], keep_h)]
    for c in outs:
        c.wait()


def projection_grads(where, tokens, a, b, pieces, order):
    rows, width = tokens.shape
    smem = pl.BlockSpec(memory_space=pltpu.SMEM)
    hbm = pl.BlockSpec(memory_space=pl.ANY)
    shape = (width, 2 * width)
    ins = [a["tokc"], b["bq"], a["ctx"], b["battn"], tokens, b["bkv"]]
    scratch = [v.shape for v in ins] + [(width, rows), (2,) + shape]
    return pl.pallas_call(
        functools.partial(projection_grads_kernel, pieces=pieces, order=order),
        out_shape=[jax.ShapeDtypeStruct(shape, bf16)] * 2,
        in_specs=[smem] + [hbm] * 6,
        out_specs=[hbm] * 2,
        scratch_shapes=[pltpu.VMEM(s, bf16) for s in scratch] + [pltpu.SemaphoreType.DMA((8,))],
        compiler_params=pltpu.CompilerParams(vmem_limit_bytes=VMEM_LIMIT),
        cost_estimate=pl.CostEstimate(flops=4 * 10**9, bytes_accessed=15 * 10**6, transcendentals=0),
        name="projection_grads",
    )(where, *ins)


def add_low(a, b):
    return (a.astype(f32) + b.astype(f32)).astype(bf16)


def swap(value, bit, n):
    return lax.ppermute(value, "dp", [(i, i ^ (1 << bit)) for i in range(n)])


def reduce_pieces(keep, send, order, n):
    for i, bit in enumerate(order):
        got = swap(send, bit, n)
        if i == len(order) - 1:
            return keep.astype(f32) + got.astype(f32)
        m = keep.shape[0] // 2
        send, keep = add_low(keep[m:], got[m:]), add_low(keep[:m], got[:m])


def body(
    tokens, w_qkv, b_query, b_value, w_out, b_out, gain_attn, shift_attn, w_in, b_in, w_back, b_back,
    gain_out, shift_out, grad_out, masked,
):
    rows, width = tokens.shape
    ff = w_in.shape[1]
    n = lax.axis_size("dp")
    core = lax.axis_index("head")
    steps = n.bit_length() - 1
    halving = n == 1 << steps and width // n % 16 == 0
    if halving:
        own = lax.axis_index("dp")
        orders = [tuple(range(steps)), (1, 0) + tuple(range(2, steps)), (2, 0, 1) + tuple(range(3, steps))]
        pieces = n
    else:
        own = jnp.int32(0)
        orders = [(2, 1, 0)] * 3
        pieces = 8
    where = jnp.stack([own, core]).astype(jnp.int32)
    m8 = masked.reshape(-1, 128)
    a = marked_forward(
        core.reshape(1).astype(jnp.int32), m8, tokens, grad_out, w_qkv, b_query, b_value, w_out, b_out,
        gain_attn, shift_attn, w_in, b_in, w_back, b_back, gain_out,
    )
    x = lax.ppermute(a["xsend"], "head", [(0, 1), (1, 0)])
    b = marked_backward(m8, gain_attn, w_in, w_out, w_qkv, a)
    keep1, send1, keep2, send2 = ffn_grads(where, a, x, pieces, orders)
    keep3, send3 = projection_grads(where, tokens, a, b, pieces, orders[2])
    got3 = lax.ppermute(send3, "head", [(0, 1), (1, 0)])
    m = width // 2
    if halving:
        grad_w_back = reduce_pieces(keep1, send1, orders[0], n)
        grad_w_in = reduce_pieces(keep2, send2, orders[1], n)
        send3, keep3 = add_low(keep3[m:], got3[m:]), add_low(keep3[:m], got3[:m])
        shares = reduce_pieces(keep3, send3, orders[2], n)
    else:
        total = lambda *parts: lax.psum_scatter(
            jnp.concatenate(parts), "dp", scatter_dimension=0, tiled=True
        ).astype(f32)
        grad_w_back = total(keep1, send1)
        grad_w_in = total(keep2, send2)
        shares = total(add_low(keep3, got3))
    small = jnp.concatenate([a["small"][0], b["small"][0]])
    small = jnp.sum(lax.all_gather(small.reshape(-1, 128), ("dp", "head")), axis=0).reshape(-1)
    small_a, small_b = small[: 3 * width + ff], small[3 * width + ff :]
    layer_out = None
    for i in range(rows // BLOCK):
        layer_out = layer_rows(
            i, layer_out, tokens, a["kv"], w_qkv, b_query, w_out, b_out, gain_attn, shift_attn, w_in, b_in,
            w_back, b_back, gain_out, shift_out,
        )
    grad_tokens = mm_tn(a["sel"], b["rc"]) + mm_nt(b["bkv"], w_qkv[:, width:])
    return (
        layer_out,
        grad_tokens,
        shares[:, : 3 * m],
        small_b[3 * width : 4 * width],
        small_b[4 * width :],
        shares[:, 3 * m :],
        small_b[:width],
        small_b[width : 2 * width],
        small_b[2 * width : 3 * width],
        grad_w_in,
        small_a[3 * width :],
        grad_w_back,
        small_a[2 * width : 3 * width],
        small_a[:width],
        small_a[width : 2 * width],
    )


def solution(mesh):
    rows = P(("dp", "head"), None)
    shard = P("dp", "head")
    return jax.shard_map(
        body,
        mesh=mesh,
        in_specs=(rows,) + (P(),) * 13 + (rows, P(("dp", "head"))),
        out_specs=(rows, rows, shard, P(), P(), shard, P(), P(), P(), shard, P(), shard, P(), P(), P()),
        check_vma=False,
    )
```

```python
import functools

import jax
import jax.numpy as jnp
from jax import lax
from jax.experimental import pallas as pl
from jax.experimental.pallas import tpu as pltpu
from jax.sharding import PartitionSpec as P

HEADS = 12
HEAD_DIM = 64
LEN = 512
CAP = 320
TILE = 64
SLOTS = (CAP // TILE + 1) * TILE
QUAD = 4 * HEAD_DIM
PARAMS = pltpu.CompilerParams(vmem_limit_bytes=60 * 1024 * 1024)
COST = pl.CostEstimate(flops=1000, bytes_accessed=1000, transcendentals=0)

epsilon = 1e-12
bf16 = jnp.bfloat16
f32 = jnp.float32


def mm(a, b):
    return jnp.dot(a, b, preferred_element_type=f32)


def mm_nt(a, b):
    return lax.dot_general(a, b, (((1,), (1,)), ((), ())), preferred_element_type=f32)


def mm_tn(a, b):
    return lax.dot_general(a, b, (((0,), (0,)), ((), ())), preferred_element_type=f32)


def colsum(v):
    return jnp.sum(v, axis=0, keepdims=True)


def rowmean(v):
    return jnp.sum(v, axis=-1, keepdims=True) * (1.0 / v.shape[-1])


def norm_parts(v):
    centred = v - rowmean(v)
    r = lax.rsqrt(rowmean(centred * centred) + epsilon)
    return centred * r, r


def norm_back(cot, nhat, r, gain):
    e = cot * gain
    return r * (e - rowmean(e) - nhat * rowmean(e * nhat))


def erf_tail(v):
    x = jnp.abs(v)
    t = 1.0 / (1.0 + (0.3275911 * 0.7071067811865476) * x)
    e = jnp.exp2(v * v * (-0.5 * 1.4426950408889634))
    poly = 0.5 * 1.061405429 * t + 0.5 * -1.453152027
    poly = poly * t + 0.5 * 1.421413741
    poly = poly * t + 0.5 * -0.284496736
    poly = poly * t + 0.5 * 0.254829592
    return x, (poly * t) * e, e


def lane_masks():
    head = lax.broadcasted_iota(jnp.int32, (1, QUAD), 1) // HEAD_DIM
    return [(head == j).astype(f32).astype(bf16) for j in range(4)]


def spread(x, masks):
    return jnp.concatenate([x * m for m in masks], axis=0)


def softmax_columns(scores):
    e = jnp.exp(scores - jnp.max(scores, axis=0, keepdims=True))
    return e, 1.0 / jnp.sum(e, axis=0, keepdims=True)


def join_tiles(first, second):
    low = lax.broadcasted_iota(jnp.int32, (HEAD_DIM, 2 * TILE), 1) < TILE
    top = jnp.where(low, first[:HEAD_DIM], pltpu.roll(second[:HEAD_DIM], TILE, 1))
    bottom = jnp.where(low, pltpu.roll(first[HEAD_DIM:], TILE, 1), second[HEAD_DIM:])
    return jnp.concatenate([top, bottom], axis=0)


def pipelined(count, early, middle, late):
    ahead = early(0)
    waiting = None
    for i in range(count):
        now, ahead = ahead, early(i + 1) if i + 1 < count else None
        if waiting is not None:
            late(i - 1, waiting)
        waiting = middle(i, now)
    late(count - 1, waiting)


class Mover:
    def __init__(self, sems):
        self.sems = sems
        self.count = 0

    def start(self, src, dst):
        copy = pltpu.make_async_copy(src, dst, self.sems.at[self.count])
        self.count += 1
        copy.start()
        return copy


def marked_forward_kernel(
    core_ref, m_ref, bq_ref, bv_ref, bo_ref, g1_ref, s1_ref, bi_ref, bb_ref, g2_ref,
    tok_h, gout_h, wqkv_h, wout_h, win_h, wback_h,
    sel_h, kv_h, tokc_h, qs_h, p_h, ctx_h, hl_h, act_h, bbr_h, bin_h, xsend_h, battn_h, bctx_h, bpre_h, small_ref,
    tok, gout, wqkv, wout, win, wback,
    sel, kv, tokc, gc, qs, prob, ctx, nhat, rr, hidden, hl, act, gp, branch, bbr, bin_, bsum, bv, bi, vt,
    battn, bctx, bpre,
    sems,
):
    rows, width = tok.shape
    ff = win.shape[1]
    quads = width // QUAD
    mover = Mover(sems)
    other = 1 - core_ref[0]
    c_tok = mover.start(tok_h, tok)
    c_wqkv = mover.start(wqkv_h, wqkv)
    c_gout = mover.start(gout_h, gout)
    c_wout = mover.start(wout_h, wout)
    c_win = mover.start(win_h, win)
    c_wback = mover.start(wback_h, wback)
    outs = []
    bv[...] = bv_ref[...].reshape(bv.shape)
    bi[...] = bi_ref[...].reshape(bi.shape)
    m8 = m_ref[...].astype(f32)
    groups = m8.shape[0]
    per_seq = LEN // 128
    tri = (
        lax.broadcasted_iota(jnp.int32, (128, 128), 0)
        <= lax.broadcasted_iota(jnp.int32, (128, 128), 1)
    ).astype(f32).astype(bf16)
    within = mm(m8.astype(bf16), tri)
    first = jnp.sum(m8[:per_seq], axis=(0, 1), keepdims=True)
    a0 = jnp.floor((first + (TILE - 1)) * (1.0 / TILE)) * TILE
    offset = jnp.zeros((1, 1), f32)
    slot_iota = lax.broadcasted_iota(jnp.int32, (SLOTS, 128), 0).astype(f32)
    for g in range(groups):
        if g == per_seq:
            offset = a0
        slot = jnp.where(m8[g : g + 1] > 0.0, offset + within[g : g + 1] - 1.0, -1.0)
        sel[:, 128 * g : 128 * (g + 1)] = (slot_iota == slot).astype(f32).astype(bf16)
        offset = offset + within[g : g + 1, 127:128]
    outs.append(mover.start(sel, sel_h))
    a0_scalar = jnp.sum(a0).astype(jnp.int32)

    c_tok.wait()
    tokc[...] = mm(sel[...], tok[...]).astype(bf16)
    outs.append(mover.start(tokc, tokc_h))
    c_wqkv.wait()
    for q in range(rows // LEN):
        for i in range(2 * width // QUAD):
            at = slice(i * QUAD, (i + 1) * QUAD)
            value = mm(tok[q * LEN : (q + 1) * LEN, :], wqkv[:, width + i * QUAD : width + (i + 1) * QUAD])
            if i >= quads:
                low = (value + bv[:, i * QUAD - width : (i + 1) * QUAD - width]).astype(bf16)
                vt[q, i * QUAD - width : (i + 1) * QUAD - width, :] = low.T
                kv[q, :, at] = low
            else:
                kv[q, :, at] = value.astype(bf16)
    outs.append(mover.start(kv, kv_h))
    qs[...] = (
        (mm(tokc[...], wqkv[:, :width]) + bq_ref[...]).astype(bf16).astype(f32) * HEAD_DIM**-0.5
    ).astype(bf16)
    outs.append(mover.start(qs, qs_h))

    masks = lane_masks()
    steps = [(t, g, w) for t in range(SLOTS // (2 * TILE)) for g in range(quads) for w in range(2)]
    kept = {}

    def place_of(i):
        t, g, w = steps[i]
        r0 = (2 * t + w) * TILE
        return r0, (r0 >= a0_scalar).astype(jnp.int32), slice(g * QUAD, (g + 1) * QUAD)

    def scores(i):
        r0, q, lanes = place_of(i)
        return mm_nt(kv[q, :, lanes], spread(qs[r0 : r0 + TILE, lanes], masks))

    def probabilities(i, s):
        t, g, w = steps[i]
        e, inv = softmax_columns(s)
        p = (e * inv).astype(bf16)
        prob[(2 * t + w) * quads + g] = p
        return p

    def values(i, p):
        t, g, w = steps[i]
        r0, q, lanes = place_of(i)
        kept[w] = mm(vt[q, lanes, :], p)
        if w == 1:
            for h in range(2):
                part = slice(128 * h, 128 * (h + 1))
                ctx[g * QUAD + 128 * h : g * QUAD + 128 * (h + 1), 128 * t : 128 * (t + 1)] = join_tiles(
                    kept[0][part, part], kept[1][part, part]
                ).astype(bf16)

    pipelined(len(steps), scores, probabilities, values)
    outs.append(mover.start(prob, p_h))
    outs.append(mover.start(ctx, ctx_h))
    c_wout.wait()
    pre = mm(ctx[...].T, wout[...]) + bo_ref[...] + tokc[...].astype(f32)
    nh, r = norm_parts(pre)
    nhat[...] = nh
    rr[...] = jnp.broadcast_to(r, rr.shape)
    hid = nh * g1_ref[...] + s1_ref[...]
    hidden[...] = hid
    hl[...] = hid.astype(bf16)
    outs.append(mover.start(hl, hl_h))
    outs.append(mover.start(hl, xsend_h.at[:, ff : ff + width]))
    c_gout.wait()
    gc[...] = mm(sel[...], gout[...]).astype(bf16)
    c_win.wait()

    def inner(i):
        return mm(hl[...], win[:, i * 256 : (i + 1) * 256])

    def gelu(i, v):
        at = slice(i * 256, (i + 1) * 256)
        v = v + bi[:, at]
        x, tail, e = erf_tail(v)
        act[:, at] = (jnp.maximum(v, 0.0) - x * tail).astype(bf16)
        gp[:, at] = jnp.where(v >= 0.0, 1.0 - tail, tail) + v * (e * 0.3989422804014327)

    pipelined(ff // 256, inner, gelu, lambda i, v: None)
    outs.append(mover.start(act, act_h))
    outs.append(mover.start(act, xsend_h.at[:, :ff]))
    c_wback.wait()
    for i in range(width // 256):
        at = slice(i * 256, (i + 1) * 256)
        branch[:, at] = mm(act[...], wback[:, at])
    nh2, r2 = norm_parts(hidden[...] + branch[...] + bb_ref[...])
    cot = gc[...].astype(f32)
    bs = norm_back(cot, nh2, r2, g2_ref[...])
    bsum[...] = bs
    bl = bs.astype(bf16)
    bbr[...] = bl
    outs.append(mover.start(bbr, bbr_h))
    half = width // 2
    outs.append(
        mover.start(
            bbr.at[:, pl.ds(pl.multiple_of(other * half, half), half)],
            xsend_h.at[:, ff + width : ff + width + half],
        )
    )
    small_ref[:, :width] = colsum(cot * nh2)
    small_ref[:, width : 2 * width] = colsum(cot)
    small_ref[:, 2 * width : 3 * width] = colsum(bl.astype(f32))

    def back_active(i):
        return mm_nt(bbr[...], wback[i * 256 : (i + 1) * 256, :])

    def back_gelu(i, v):
        at = slice(i * 256, (i + 1) * 256)
        b = (v * gp[:, at]).astype(bf16)
        bin_[:, at] = b
        small_ref[:, 3 * width + i * 256 : 3 * width + (i + 1) * 256] = colsum(b.astype(f32))

    pipelined(ff // 256, back_active, back_gelu, lambda i, v: None)
    outs.append(mover.start(bin_, bin_h))
    outs.append(
        mover.start(
            bin_.at[:, pl.ds(pl.multiple_of(other * (ff // 2), ff // 2), ff // 2)],
            xsend_h.at[:, ff + width + half :],
        )
    )
    for i in range(width // 256):
        at = slice(i * 256, (i + 1) * 256)
        branch[:, at] = bsum[:, at] + mm_nt(bin_[...], win[at, :])
    back_hidden = branch[...]
    nh = nhat[...]
    bp = norm_back(back_hidden, nh, rr[:, :1], g1_ref[...])
    bpre[...] = bp
    outs.append(mover.start(bpre, bpre_h))
    bl = bp.astype(bf16)
    battn[...] = bl
    outs.append(mover.start(battn, battn_h))
    bctx[...] = mm_nt(bl, wout[...]).astype(bf16)
    outs.append(mover.start(bctx, bctx_h))
    at = 3 * width + ff
    small_ref[:, at : at + width] = colsum(bl.astype(f32))
    small_ref[:, at + width : at + 2 * width] = colsum(back_hidden * nh)
    small_ref[:, at + 2 * width : at + 3 * width] = colsum(back_hidden)
    for copy in outs:
        copy.wait()


def marked_forward(core, m8, tokens, gout, w_qkv, b_query, b_value, w_out, b_out, g1, s1, w_in, b_in, w_back, b_back, g2):
    rows, width = tokens.shape
    ff = w_in.shape[1]
    tiles = SLOTS // TILE * (width // QUAD)
    outs = dict(
        sel=((SLOTS, rows), bf16), kv=((rows // LEN, LEN, 2 * width), bf16), tokc=((SLOTS, width), bf16),
        qs=((SLOTS, width), bf16), p=((tiles, LEN, 4 * TILE), bf16), ctx=((width, SLOTS), bf16),
        hl=((SLOTS, width), bf16),
        act=((SLOTS, ff), bf16), bbr=((SLOTS, width), bf16), bin=((SLOTS, ff), bf16),
        xsend=((SLOTS, (ff + width) * 3 // 2), bf16), battn=((SLOTS, width), bf16), bctx=((SLOTS, width), bf16),
        bpre=((SLOTS, width), f32), small=((1, 6 * width + ff), f32),
    )
    scratch = [
        ((rows, width), bf16), ((rows, width), bf16), (w_qkv.shape, bf16), (w_out.shape, bf16),
        (w_in.shape, bf16), (w_back.shape, bf16),
        outs["sel"], outs["kv"], outs["tokc"], ((SLOTS, width), bf16), outs["qs"], outs["p"], outs["ctx"],
        ((SLOTS, width), f32), ((SLOTS, 128), f32), ((SLOTS, width), f32), outs["hl"], outs["act"], ((SLOTS, ff), f32),
        ((SLOTS, width), f32), outs["bbr"], outs["bin"], ((SLOTS, width), f32), ((1, width), f32), ((1, ff), f32),
        ((rows // LEN, width, LEN), bf16), outs["battn"], outs["bctx"], outs["bpre"],
    ]
    vmem = pl.BlockSpec(memory_space=pltpu.VMEM)
    smem = pl.BlockSpec(memory_space=pltpu.SMEM)
    hbm = pl.BlockSpec(memory_space=pl.ANY)
    res = pl.pallas_call(
        marked_forward_kernel,
        out_shape=[jax.ShapeDtypeStruct(*o) for o in outs.values()],
        in_specs=[smem] + [vmem] * 9 + [hbm] * 6,
        out_specs=[hbm] * 14 + [vmem],
        scratch_shapes=[pltpu.VMEM(*s) for s in scratch] + [pltpu.SemaphoreType.DMA((32,))],
        compiler_params=PARAMS,
        cost_estimate=COST,
        name="marked_forward",
    )(core, m8, b_query, b_value, b_out, g1, s1, b_in, b_back, g2,
      tokens, gout, w_qkv, w_out, w_in, w_back)
    return dict(zip(outs, res))


def marked_backward_kernel(
    m_ref, wqkv_h, bpre_h, bctx_h, p_h, qs_h, kv_h,
    bq_h, bkv_h, rc_h, small_ref,
    wq, bpre, bctx, prob, qs, kv, dk, dv, bqt, bq, bkv, rc, kt,
    sems,
):
    slots, width = qs.shape
    quads = width // QUAD
    mover = Mover(sems)
    c_kv = [mover.start(kv_h, kv), mover.start(bctx_h, bctx), mover.start(qs_h, qs)]
    group = 2 * quads
    c_p = [
        mover.start(p_h.at[i : i + group], prob.at[i : i + group]) for i in range(0, prob.shape[0], group)
    ]
    c_wq = mover.start(wqkv_h.at[:, :width], wq)
    c_bpre = mover.start(bpre_h, bpre)
    outs = []
    per_seq = LEN // 128
    first = jnp.sum(m_ref[:per_seq].astype(f32), axis=(0, 1), keepdims=True)
    a0_scalar = jnp.sum(jnp.floor((first + (TILE - 1)) * (1.0 / TILE)) * TILE).astype(jnp.int32)
    dk[...] = jnp.zeros_like(dk)
    dv[...] = jnp.zeros_like(dv)
    for c in c_kv:
        c.wait()
    for q in range(kv.shape[0]):
        for g in range(quads):
            lanes = slice(g * QUAD, (g + 1) * QUAD)
            kt[q, lanes, :] = kv[q, :, lanes].T
    masks = lane_masks()
    steps = [(t, g, w) for t in range(slots // (2 * TILE)) for g in range(quads) for w in range(2)]
    kept = {}

    def place_of(i):
        t, g, w = steps[i]
        r0 = (2 * t + w) * TILE
        return r0, (r0 >= a0_scalar).astype(jnp.int32), slice(g * QUAD, (g + 1) * QUAD)

    def back_probs(i):
        t, g, w = steps[i]
        if g == 0 and w == 0:
            c_p[t].wait()
        r0, q, lanes = place_of(i)
        d4 = spread(bctx[r0 : r0 + TILE, lanes], masks)
        dp = mm_nt(kv[q, :, width + g * QUAD : width + (g + 1) * QUAD], d4)
        dv[q, :, lanes] += mm(prob[(2 * t + w) * quads + g], d4)
        return dp

    def back_scores(i, dp):
        t, g, w = steps[i]
        p = prob[(2 * t + w) * quads + g].astype(f32)
        weighted = p * dp
        return (weighted - p * colsum(weighted)).astype(bf16)

    def back_query_key(i, ds):
        t, g, w = steps[i]
        r0, q, lanes = place_of(i)
        dk[q, :, lanes] += mm(ds, spread(qs[r0 : r0 + TILE, lanes], masks))
        kept[w] = mm(kt[q, lanes, :], ds)
        if w == 1:
            for h in range(2):
                part = slice(128 * h, 128 * (h + 1))
                bqt[g * QUAD + 128 * h : g * QUAD + 128 * (h + 1), 128 * t : 128 * (t + 1)] = (
                    join_tiles(kept[0][part, part], kept[1][part, part]) * HEAD_DIM**-0.5
                ).astype(bf16)

    pipelined(len(steps), back_probs, back_scores, back_query_key)
    bq[...] = bqt[...].T
    outs.append(mover.start(bq, bq_h))
    bkv[:, :, :width] = dk[...].astype(bf16)
    bvl = dv[...].astype(bf16)
    bkv[:, :, width:] = bvl
    outs.append(mover.start(bkv, bkv_h))
    c_wq.wait()
    c_bpre.wait()
    rc[...] = (bpre[...] + mm_nt(bq[...], wq[...])).astype(bf16)
    outs.append(mover.start(rc, rc_h))
    small_ref[:, :width] = colsum(bq[...].astype(f32))
    small_ref[:, width:] = sum(colsum(bvl[q].astype(f32)) for q in range(kv.shape[0]))
    for copy in outs:
        copy.wait()


def marked_backward(m8, w_qkv, a):
    rows = a["sel"].shape[1]
    width = w_qkv.shape[0]
    outs = dict(
        bq=((SLOTS, width), bf16), bkv=((rows // LEN, LEN, 2 * width), bf16),
        rc=((SLOTS, width), bf16), small=((1, 2 * width), f32),
    )
    ins = [a[k] for k in ("bpre", "bctx", "p", "qs", "kv")]
    scratch = [((width, width), bf16)] + [(v.shape, v.dtype) for v in ins]
    scratch += [
        ((rows // LEN, LEN, width), f32), ((rows // LEN, LEN, width), f32), ((width, SLOTS), bf16),
        outs["bq"], outs["bkv"], outs["rc"], ((rows // LEN, width, LEN), bf16),
    ]
    vmem = pl.BlockSpec(memory_space=pltpu.VMEM)
    hbm = pl.BlockSpec(memory_space=pl.ANY)
    res = pl.pallas_call(
        marked_backward_kernel,
        out_shape=[jax.ShapeDtypeStruct(*o) for o in outs.values()],
        in_specs=[vmem] + [hbm] * 6,
        out_specs=[hbm] * 3 + [vmem],
        scratch_shapes=[pltpu.VMEM(*s) for s in scratch] + [pltpu.SemaphoreType.DMA((24,))],
        compiler_params=PARAMS,
        cost_estimate=COST,
        name="marked_backward",
    )(m8, w_qkv, *ins)
    return dict(zip(outs, res))


def attention_rows_kernel(
    which, bq_ref, bo_ref, g1_ref, s1_ref, tok_h, kv_h, wqkv_h, wout_h, hidden_h,
    tok, kv, wq, wout, q, ctx, hidden, vt, sems,
):
    width = wq.shape[1]
    quads = width // QUAD
    tile = 128
    mover = Mover(sems)
    i = which[0]
    r0 = pl.multiple_of(i * LEN, LEN)
    c_tok = mover.start(tok_h.at[pl.ds(r0, LEN), :], tok)
    c_wq = mover.start(wqkv_h.at[:, :width], wq)
    c_kv = mover.start(kv_h.at[i], kv)
    c_wout = mover.start(wout_h, wout)
    c_tok.wait()
    c_wq.wait()
    q[...] = ((mm(tok[...], wq[...]) + bq_ref[...]).astype(bf16).astype(f32) * HEAD_DIM**-0.5).astype(bf16)
    c_kv.wait()
    for g in range(quads):
        vt[g * QUAD : (g + 1) * QUAD, :] = kv[:, width + g * QUAD : width + (g + 1) * QUAD].T
    masks = lane_masks()
    steps = [(t, g) for t in range(LEN // tile) for g in range(quads)]

    def scores(i):
        t, g = steps[i]
        lanes = slice(g * QUAD, (g + 1) * QUAD)
        return mm_nt(kv[:, lanes], spread(q[t * tile : (t + 1) * tile, lanes], masks))

    def probabilities(i, s):
        e, inv = softmax_columns(s)
        return e.astype(bf16), inv

    def values(i, parts):
        t, g = steps[i]
        p, inv = parts
        for h in range(2):
            at = g * QUAD + 128 * h
            z = mm(vt[at : at + 128, :], p[:, h * 2 * tile : (h + 1) * 2 * tile])
            for u in range(2):
                tokens = slice((2 * h + u) * tile, (2 * h + u + 1) * tile)
                ctx[at + u * HEAD_DIM : at + (u + 1) * HEAD_DIM, t * tile : (t + 1) * tile] = (
                    z[u * HEAD_DIM : (u + 1) * HEAD_DIM, u * tile : (u + 1) * tile] * inv[:, tokens]
                ).astype(bf16)

    pipelined(len(steps), scores, probabilities, values)
    c_wout.wait()
    nh, _ = norm_parts(mm(ctx[...].T, wout[...]) + bo_ref[...] + tok[...].astype(f32))
    hid = nh * g1_ref[...] + s1_ref[...]
    hidden[...] = hid
    mover.start(hidden, hidden_h).wait()


def attention_rows(which, tokens, kv, w_qkv, b_query, w_out, b_out, g1, s1):
    width = tokens.shape[1]
    vmem = pl.BlockSpec(memory_space=pltpu.VMEM)
    smem = pl.BlockSpec(memory_space=pltpu.SMEM)
    hbm = pl.BlockSpec(memory_space=pl.ANY)
    scratch = [
        ((LEN, width), bf16), ((LEN, 2 * width), bf16), ((width, width), bf16), (w_out.shape, bf16),
        ((LEN, width), bf16), ((width, LEN), bf16), ((LEN, width), f32), ((width, LEN), bf16),
    ]
    return pl.pallas_call(
        attention_rows_kernel,
        out_shape=jax.ShapeDtypeStruct((LEN, width), f32),
        in_specs=[smem] + [vmem] * 4 + [hbm] * 4,
        out_specs=hbm,
        scratch_shapes=[pltpu.VMEM(*s) for s in scratch] + [pltpu.SemaphoreType.DMA((8,))],
        compiler_params=PARAMS,
        cost_estimate=COST,
        name="attention_rows",
    )(jnp.full((1,), which, jnp.int32), b_query, b_out, g1, s1, tokens, kv, w_qkv, w_out)


def ffn_rows_kernel(
    which, bi_ref, bb_ref, g2_ref, s2_ref, hidden_h, win_h, wback_h, *rest,
):
    (out_h, win, wback, hl, hidden, act, branch, out, bi, sems) = rest[-10:]
    width, ff = win.shape
    mover = Mover(sems)
    r0 = pl.multiple_of(which[0] * LEN, LEN)
    c_hidden = mover.start(hidden_h, hidden)
    part = ff // 4
    c_win = [mover.start(win_h.at[:, k : k + part], win.at[:, k : k + part]) for k in range(0, ff, part)]
    c_wback = mover.start(wback_h, wback)
    bi[...] = bi_ref[...].reshape(bi.shape)
    c_hidden.wait()
    hl[...] = hidden[...].astype(bf16)

    def inner(j):
        if j * 256 % part == 0:
            c_win[j * 256 // part].wait()
        return mm(hl[...], win[:, j * 256 : (j + 1) * 256])

    def gelu(j, v):
        at = slice(j * 256, (j + 1) * 256)
        v = v + bi[:, at]
        x, tail, _ = erf_tail(v)
        act[:, at] = (jnp.maximum(v, 0.0) - x * tail).astype(bf16)

    pipelined(ff // 256, inner, gelu, lambda i, v: None)
    c_wback.wait()
    for j in range(width // 256):
        at = slice(j * 256, (j + 1) * 256)
        branch[:, at] = mm(act[...], wback[:, at])
    nh2, _ = norm_parts(hidden[...] + branch[...] + bb_ref[...])
    out[...] = (nh2 * g2_ref[...] + s2_ref[...]).astype(bf16)
    mover.start(out, out_h.at[pl.ds(r0, LEN), :]).wait()


def ffn_rows(which, previous, rows, hidden, w_in, b_in, w_back, b_back, g2, s2):
    width, ff = w_in.shape
    vmem = pl.BlockSpec(memory_space=pltpu.VMEM)
    smem = pl.BlockSpec(memory_space=pltpu.SMEM)
    hbm = pl.BlockSpec(memory_space=pl.ANY)
    scratch = [
        (w_in.shape, bf16), (w_back.shape, bf16), ((LEN, width), bf16), ((LEN, width), f32), ((LEN, ff), bf16),
        ((LEN, width), f32), ((LEN, width), bf16), ((1, ff), f32),
    ]
    extra = () if previous is None else (previous,)
    return pl.pallas_call(
        ffn_rows_kernel,
        out_shape=jax.ShapeDtypeStruct((rows, width), bf16),
        in_specs=[smem] + [vmem] * 4 + [hbm] * (3 + len(extra)),
        out_specs=hbm,
        scratch_shapes=[pltpu.VMEM(*s) for s in scratch] + [pltpu.SemaphoreType.DMA((8,))],
        input_output_aliases={8: 0} if extra else {},
        compiler_params=PARAMS,
        cost_estimate=COST,
        name="ffn_rows",
    )(jnp.full((1,), which, jnp.int32), b_in, b_back, g2, s2, hidden, w_in, w_back, *extra)


def place(piece, own, core, orders):
    bits = piece ^ own
    spots = []
    for order in orders:
        spot = 0
        for step in order:
            spot = spot * 2 + ((bits >> step) & 1)
        spots.append(spot)
    return spots[core] if isinstance(core, int) else spots[0] + core * (spots[1] - spots[0])


def ffn_grads_kernel(
    where, act_h, hl_h, bbr_h, bin_h, x_h, keep1_h, send1_h, keep2_h, send2_h,
    act, hl, bbr, bin_, out1, out2, hlt, sems, *, pieces, orders,
):
    own, core = where[0], where[1]
    slots, ff = act_h.shape
    width = hl_h.shape[1]
    half = width // 2
    mover = Mover(sems)
    up, down = slice(0, slots), slice(slots, 2 * slots)
    mine = lambda n: pl.ds(pl.multiple_of(core * n, n), n)
    c1 = [
        mover.start(bbr_h.at[:, mine(half)], bbr.at[up, :]),
        mover.start(x_h.at[:, ff + width : ff + width + half], bbr.at[down, :]),
        mover.start(act_h, act.at[up, :]),
        mover.start(x_h.at[:, :ff], act.at[down, :]),
    ]
    c2 = [
        mover.start(hl_h, hl.at[up, :]),
        mover.start(x_h.at[:, ff : ff + width], hl.at[down, :]),
        mover.start(bin_h.at[:, mine(ff // 2)], bin_.at[up, :]),
        mover.start(x_h.at[:, ff + width + half :], bin_.at[down, :]),
    ]
    for c in c1:
        c.wait()
    size, block = ff // pieces, width // pieces
    for j in range(ff // half):
        g = mm_tn(act[:, j * half : (j + 1) * half], bbr[...]).astype(bf16)
        for k in range(half // size):
            at = place(j * (half // size) + k, own, core, orders[0]) * size
            out1[pl.ds(pl.multiple_of(at, size), size), :] = g[k * size : (k + 1) * size]
    rows = ff // 2
    outs = [mover.start(out1.at[rows:, :], send1_h), mover.start(out1.at[:rows, :], keep1_h)]
    for c in c2:
        c.wait()
    for i in range(2):
        hlt[...] = hl[:, i * half : (i + 1) * half].T
        for j in range(ff // width):
            g = mm(hlt[...], bin_[:, j * half : (j + 1) * half]).astype(bf16)
            for k in range(half // block):
                at = place(i * (half // block) + k, own, core, orders[1]) * size + j * block
                out2[pl.ds(pl.multiple_of(at, block), block), :] = g[k * block : (k + 1) * block]
    outs += [mover.start(out2.at[rows:, :], send2_h), mover.start(out2.at[:rows, :], keep2_h)]
    for c in outs:
        c.wait()


def ffn_grads(where, a, x, pieces, orders):
    slots, ff = a["act"].shape
    width = a["hl"].shape[1]
    half = width // 2
    smem = pl.BlockSpec(memory_space=pltpu.SMEM)
    hbm = pl.BlockSpec(memory_space=pl.ANY)
    scratch = [
        (2 * slots, ff), (2 * slots, width), (2 * slots, half), (2 * slots, ff // 2), (ff, half), (ff, half),
        (half, 2 * slots),
    ]
    return pl.pallas_call(
        functools.partial(ffn_grads_kernel, pieces=pieces, orders=orders),
        out_shape=[jax.ShapeDtypeStruct((ff // 2, half), bf16)] * 4,
        in_specs=[smem] + [hbm] * 5,
        out_specs=[hbm] * 4,
        scratch_shapes=[pltpu.VMEM(s, bf16) for s in scratch] + [pltpu.SemaphoreType.DMA((12,))],
        compiler_params=PARAMS,
        cost_estimate=COST,
        name="ffn_grads",
    )(where, a["act"], a["hl"], a["bbr"], a["bin"], x)


def projection_grads_kernel(
    where, tokc_h, bq_h, ctx_h, battn_h, tok_h, bkv_h, keep_h, send_h,
    tokc, bq, ctx, battn, tok, bkv, tokt, short, out, sems, *, pieces, orders,
):
    own, core = where[0], where[1]
    rows, width = tok.shape
    half = width // 2
    block = width // pieces
    size = 4 * block
    mover = Mover(sems)
    c1 = [mover.start(tok_h, tok)]
    c2 = [mover.start(tokc_h, tokc), mover.start(bq_h, bq)]
    c3 = [mover.start(ctx_h, ctx), mover.start(battn_h, battn)]
    c4 = [mover.start(bkv_h, bkv)]

    def products(left, right, j, owner, chunk):
        for i in range(2):
            g = mm(left[i * half : (i + 1) * half, :], right[:, j * half : (j + 1) * half]).astype(bf16)
            for k in range(half // block):
                at = place(i * (half // block) + k, own, owner, orders) * size + chunk * block
                out[owner ^ core, pl.ds(pl.multiple_of(at, block), block), :] = g[k * block : (k + 1) * block]

    for c in c1 + c2:
        c.wait()
    short[...] = tokc[...].T
    tokt[...] = tok[...].T
    for j in range(2):
        products(short, bq, j, 0, j)
    for c in c3:
        c.wait()
    for j in range(2):
        products(ctx, battn, j, j, 3)
    for c in c4:
        c.wait()
    for j in range(4):
        products(tokt, bkv, j, (j + 2) // 3, (j + 2) % 3)
    outs = [mover.start(out.at[1], send_h), mover.start(out.at[0], keep_h)]
    for c in outs:
        c.wait()


def projection_grads(where, tokens, a, b, pieces, orders):
    rows, width = tokens.shape
    smem = pl.BlockSpec(memory_space=pltpu.SMEM)
    hbm = pl.BlockSpec(memory_space=pl.ANY)
    shape = (4 * width, width // 2)
    ins = [a["tokc"], b["bq"], a["ctx"], a["battn"], tokens, b["bkv"].reshape(rows, 2 * width)]
    scratch = [v.shape for v in ins] + [(width, rows), (width, SLOTS), (2,) + shape]
    return pl.pallas_call(
        functools.partial(projection_grads_kernel, pieces=pieces, orders=orders),
        out_shape=[jax.ShapeDtypeStruct(shape, bf16)] * 2,
        in_specs=[smem] + [hbm] * 6,
        out_specs=[hbm] * 2,
        scratch_shapes=[pltpu.VMEM(s, bf16) for s in scratch] + [pltpu.SemaphoreType.DMA((8,))],
        compiler_params=PARAMS,
        cost_estimate=COST,
        name="projection_grads",
    )(where, *ins)


def add_low(a, b):
    return (a.astype(f32) + b.astype(f32)).astype(bf16)


def after(value, *others):
    return lax.optimization_barrier((value, others))[0]


class Reduction:
    def __init__(self, keep, send, orders, n):
        self.keep, self.send, self.orders, self.n = keep, send, orders, n
        self.step = 0
        self.start()

    def start(self):
        pairs = [
            (2 * i + core, 2 * (i ^ (1 << self.orders[core][self.step])) + core)
            for i in range(self.n)
            for core in range(2)
        ]
        self.got = lax.ppermute(self.send, ("dp", "head"), pairs)

    def advance(self, *others):
        keep, got = after((self.keep, self.got), *others)
        self.step += 1
        if self.step == len(self.orders[0]):
            self.share = keep.astype(f32) + got.astype(f32)
            return self.share
        m = keep.shape[0] // 2
        self.send = add_low(keep[m:], got[m:])
        self.start()
        self.keep = add_low(keep[:m], got[:m])
        return self.keep


def columns(share, count):
    rows = share.shape[0] // count
    return jnp.concatenate([share[i * rows : (i + 1) * rows] for i in range(count)], axis=1)


def body(
    tokens, w_qkv, b_query, b_value, w_out, b_out, gain_attn, shift_attn, w_in, b_in, w_back, b_back,
    gain_out, shift_out, grad_out, masked,
):
    rows, width = tokens.shape
    ff = w_in.shape[1]
    n = lax.axis_size("dp")
    core = lax.axis_index("head")
    steps = n.bit_length() - 1
    halving = n == 1 << steps and width // n % 16 == 0
    if halving:
        own = lax.axis_index("dp")
        rest = tuple(range(3, steps))
        plane_first = ((0, 1, 2) + rest, (1, 0, 2) + rest)
        line_first = ((2, 0, 1) + rest, (2, 1, 0) + rest)
        orders = [plane_first, line_first, plane_first]
        pieces = n
    else:
        own = jnp.int32(0)
        orders = [((3, 2, 1, 0),) * 2] * 3
        pieces = 16
    where = jnp.stack([own, core]).astype(jnp.int32)
    m8 = masked.reshape(-1, 128)
    swap_cores = lambda v: lax.ppermute(v, "head", [(0, 1), (1, 0)])

    a = marked_forward(
        core.reshape(1).astype(jnp.int32), m8, tokens, grad_out, w_qkv, b_query, b_value, w_out, b_out,
        gain_attn, shift_attn, w_in, b_in, w_back, b_back, gain_out,
    )
    x = swap_cores(a["xsend"])
    b = marked_backward(m8, w_qkv, a)
    small = jnp.concatenate([a["small"][0], b["small"][0]])
    small = lax.all_gather(small.reshape(-1, 128), ("dp", "head"))
    keep1, send1, keep2, send2 = ffn_grads(after(where, b["rc"]), a, x, pieces, orders[:2])
    if halving:
        r1 = Reduction(keep1, send1, orders[0], n)
        r2 = Reduction(keep2, send2, orders[1], n)
    keep3, send3 = projection_grads(after(where, keep1), tokens, a, b, pieces, orders[2])
    got3 = swap_cores(send3)
    sel, wkv = after((a["sel"], w_qkv[:, width:]), keep3)
    grad_tokens = mm_tn(sel, b["rc"]) + mm_nt(b["bkv"].reshape(rows, 2 * width), wkv)
    if halving:
        done = r1.advance(grad_tokens)
        keep3, got3 = after((keep3, got3), done)
        m = keep3.shape[0] // 2
        r3 = Reduction(add_low(keep3[:m], got3[:m]), add_low(keep3[m:], got3[m:]), orders[2], n)
        done = r3.keep
    else:
        both3 = done = add_low(keep3, got3)

    def attention(which, done):
        return attention_rows(which, after(tokens, done), a["kv"], w_qkv, b_query, w_out, b_out, gain_attn, shift_attn)

    def ffn(which, previous, hidden, done):
        return ffn_rows(which, previous, rows, after(hidden, done), w_in, b_in, w_back, b_back, gain_out, shift_out)

    hidden = attention(0, done)
    done = r1.advance(hidden) if halving else hidden
    layer_out = ffn(0, None, hidden, done)
    done = layer_out
    if halving:
        done = r1.advance(done)
        done = r2.advance(done)
    hidden = attention(1, done)
    done = hidden
    if halving:
        done = r1.advance(done)
        done = r2.advance(done)
        done = r3.advance(done)
    layer_out = ffn(1, layer_out, hidden, done)
    if halving:
        done = layer_out
        done = r2.advance(done)
        done = r3.advance(done)
        done = r2.advance(done)
        done = r3.advance(done)
        done = r3.advance(done)
        shares = [r1.share, r2.share, r3.share]
    else:
        total = lambda v: lax.psum_scatter(v, "dp", scatter_dimension=0, tiled=True).astype(f32)
        natural = lambda v, count: columns_of_blocks(v, count, pieces)
        shares = [
            total(jnp.concatenate([keep1, send1])),
            total(natural(jnp.concatenate([keep2, send2]), 4)),
            total(natural(both3, 4)),
        ]
    small = jnp.sum(small, axis=0).reshape(-1)
    names = (("gain_out", width), ("shift_out", width), ("b_back", width), ("b_in", ff), ("b_out", width),
             ("gain_attn", width), ("shift_attn", width), ("b_query", width), ("b_value", width))
    sums, at = {}, 0
    for name, size in names:
        sums[name] = small[at : at + size]
        at += size
    if halving:
        shares[1] = columns(shares[1], 4)
        shares[2] = columns(shares[2], 4)
    half3 = 3 * width // 2
    return (
        layer_out, grad_tokens, shares[2][:, :half3], sums["b_query"], sums["b_value"], shares[2][:, half3:],
        sums["b_out"], sums["gain_attn"], sums["shift_attn"], shares[1], sums["b_in"], shares[0],
        sums["b_back"], sums["gain_out"], sums["shift_out"],
    )


def columns_of_blocks(v, count, pieces):
    lanes = v.shape[1]
    v = v.reshape(pieces, count, -1, lanes)
    return jnp.moveaxis(v, 1, 2).reshape(-1, count * lanes)


def solution(mesh):
    rows = P(("dp", "head"), None)
    shard = P("dp", "head")
    return jax.shard_map(
        body,
        mesh=mesh,
        in_specs=(rows,) + (P(),) * 13 + (rows, P(("dp", "head"))),
        out_specs=(rows, rows, shard, P(), P(), shard, P(), P(), P(), shard, P(), shard, P(), P(), P()),
        check_vma=False,
    )
```

```python
import functools

import jax
import jax.numpy as jnp
from jax import lax
from jax.experimental import pallas as pl
from jax.experimental.pallas import tpu as pltpu
from jax.sharding import PartitionSpec as P

HEADS = 12
HEAD_DIM = 64
LEN = 512
CAP = 320
ROWS = 256
SMALL = 32
TILE = 64
SLOTS = (CAP // TILE + 1) * TILE
QUAD = 4 * HEAD_DIM
PARAMS = pltpu.CompilerParams(vmem_limit_bytes=60 * 1024 * 1024)
COST = pl.CostEstimate(flops=1000, bytes_accessed=1000, transcendentals=0)

epsilon = 1e-12
bf16 = jnp.bfloat16
f32 = jnp.float32


def mm(a, b):
    return jnp.dot(a, b, preferred_element_type=f32)


def mm_nt(a, b):
    return lax.dot_general(a, b, (((1,), (1,)), ((), ())), preferred_element_type=f32)


def mm_tn(a, b):
    return lax.dot_general(a, b, (((0,), (0,)), ((), ())), preferred_element_type=f32)


def colsum(v):
    return jnp.sum(v, axis=0, keepdims=True)


def rowmean(v):
    return jnp.sum(v, axis=-1, keepdims=True) * (1.0 / v.shape[-1])


def norm_parts(v):
    centred = v - rowmean(v)
    r = lax.rsqrt(rowmean(centred * centred) + epsilon)
    return centred * r, r


def norm_back(cot, nhat, r, gain):
    e = cot * gain
    return r * (e - rowmean(e) - nhat * rowmean(e * nhat))


def erf_of(v):
    return lax.erf(v * 0.7071067811865476)


def lane_masks():
    head = lax.broadcasted_iota(jnp.int32, (1, QUAD), 1) // HEAD_DIM
    return [(head == j).astype(f32).astype(bf16) for j in range(4)]


def spread(x, masks):
    return jnp.concatenate([x * m for m in masks], axis=0)


def softmax_columns(scores):
    e = jnp.exp(scores - jnp.max(scores, axis=0, keepdims=True))
    return e, 1.0 / jnp.sum(e, axis=0, keepdims=True)


def join_tiles(first, second):
    low = lax.broadcasted_iota(jnp.int32, (HEAD_DIM, 2 * TILE), 1) < TILE
    top = jnp.where(low, first[:HEAD_DIM], pltpu.roll(second[:HEAD_DIM], TILE, 1))
    bottom = jnp.where(low, pltpu.roll(first[HEAD_DIM:], TILE, 1), second[HEAD_DIM:])
    return jnp.concatenate([top, bottom], axis=0)


def nothing(i, value):
    pass


def pipelined(count, early, middle, late):
    ahead = early(0)
    waiting = None
    for i in range(count):
        now, ahead = ahead, early(i + 1) if i + 1 < count else None
        if waiting is not None:
            late(i - 1, waiting)
        waiting = middle(i, now)
    late(count - 1, waiting)


class Mover:
    def __init__(self, sems):
        self.sems = sems
        self.count = 0

    def start(self, src, dst):
        copy = pltpu.make_async_copy(src, dst, self.sems.at[self.count])
        self.count += 1
        copy.start()
        return copy


def marked_forward_kernel(
    core_ref, m_ref, bq_ref, bv_ref, bo_ref, g1_ref, s1_ref, bi_ref, bb_ref, g2_ref,
    tok_h, gout_h, wqkv_h, wout_h, win_h, wback_h,
    sel_h, kv_h, tokc_h, qs_h, p_h, ctx_h, hl_h, act_h, bbr_h, bin_h, xsend_h, battn_h, bctx_h, bpre_h, small_ref,
    tok, gout, wqkv, wout, win, wback,
    sel, kv, tokc, gc, qs, prob, ctx, nhat, rr, hidden, hl, act, gp, branch, bbr, bin_, bv, bi, vt,
    battn, bctx, bpre,
    sems,
):
    rows, width = tok.shape
    ff = win.shape[1]
    quads = width // QUAD
    mover = Mover(sems)
    other = 1 - core_ref[0]
    c_tok = mover.start(tok_h, tok)
    c_wqkv = mover.start(wqkv_h, wqkv)
    c_gout = mover.start(gout_h, gout)
    c_wout = mover.start(wout_h, wout)
    c_win = mover.start(win_h, win)
    c_wback = mover.start(wback_h, wback)
    outs = []
    bv[...] = bv_ref[...].reshape(bv.shape)
    bi[...] = bi_ref[...].reshape(bi.shape)
    m8 = m_ref[...].astype(f32)
    groups = m8.shape[0]
    per_seq = LEN // 128
    tri = (
        lax.broadcasted_iota(jnp.int32, (128, 128), 0)
        <= lax.broadcasted_iota(jnp.int32, (128, 128), 1)
    ).astype(f32).astype(bf16)
    within = mm(m8.astype(bf16), tri)
    first = jnp.sum(m8[:per_seq], axis=(0, 1), keepdims=True)
    a0 = jnp.floor((first + (TILE - 1)) * (1.0 / TILE)) * TILE
    offset = jnp.zeros((1, 1), f32)
    slot_iota = lax.broadcasted_iota(jnp.int32, (SLOTS, 128), 0).astype(f32)
    for g in range(groups):
        if g == per_seq:
            offset = a0
        slot = jnp.where(m8[g : g + 1] > 0.0, offset + within[g : g + 1] - 1.0, -1.0)
        sel[:, 128 * g : 128 * (g + 1)] = (slot_iota == slot).astype(f32).astype(bf16)
        offset = offset + within[g : g + 1, 127:128]
    outs.append(mover.start(sel, sel_h))
    a0_scalar = jnp.sum(a0).astype(jnp.int32)

    c_tok.wait()
    tokc[...] = mm(sel[...], tok[...]).astype(bf16)
    outs.append(mover.start(tokc, tokc_h))
    c_wqkv.wait()
    for q in range(rows // LEN):
        for i in range(2 * width // QUAD):
            at = slice(i * QUAD, (i + 1) * QUAD)
            value = mm(tok[q * LEN : (q + 1) * LEN, :], wqkv[:, width + i * QUAD : width + (i + 1) * QUAD])
            if i >= quads:
                low = (value + bv[:, i * QUAD - width : (i + 1) * QUAD - width]).astype(bf16)
                vt[q, i * QUAD - width : (i + 1) * QUAD - width, :] = low.T
                kv[q, :, at] = low
            else:
                kv[q, :, at] = value.astype(bf16)
    outs.append(mover.start(kv, kv_h))
    qs[...] = (
        (mm(tokc[...], wqkv[:, :width]) + bq_ref[...]).astype(bf16).astype(f32) * HEAD_DIM**-0.5
    ).astype(bf16)
    outs.append(mover.start(qs, qs_h))

    masks = lane_masks()
    steps = [(t, g, w) for t in range(SLOTS // (2 * TILE)) for g in range(quads) for w in range(2)]
    kept = {}

    def place_of(i):
        t, g, w = steps[i]
        r0 = (2 * t + w) * TILE
        return r0, (r0 >= a0_scalar).astype(jnp.int32), slice(g * QUAD, (g + 1) * QUAD)

    def scores(i):
        r0, q, lanes = place_of(i)
        return mm_nt(kv[q, :, lanes], spread(qs[r0 : r0 + TILE, lanes], masks))

    def probabilities(i, s):
        t, g, w = steps[i]
        e, inv = softmax_columns(s)
        p = (e * inv).astype(bf16)
        prob[(2 * t + w) * quads + g] = p
        return p

    def values(i, p):
        t, g, w = steps[i]
        r0, q, lanes = place_of(i)
        kept[w] = mm(vt[q, lanes, :], p)
        if w == 1:
            for h in range(2):
                part = slice(128 * h, 128 * (h + 1))
                ctx[g * QUAD + 128 * h : g * QUAD + 128 * (h + 1), 128 * t : 128 * (t + 1)] = join_tiles(
                    kept[0][part, part], kept[1][part, part]
                ).astype(bf16)

    pipelined(len(steps), scores, probabilities, values)
    outs.append(mover.start(prob, p_h))
    outs.append(mover.start(ctx, ctx_h))
    c_wout.wait()
    pre = mm(ctx[...].T, wout[...]) + bo_ref[...] + tokc[...].astype(f32)
    nh, r = norm_parts(pre)
    nhat[...] = nh
    rr[...] = jnp.broadcast_to(r, rr.shape)
    hid = nh * g1_ref[...] + s1_ref[...]
    hidden[...] = hid
    hl[...] = hid.astype(bf16)
    outs.append(mover.start(hl, hl_h))
    outs.append(mover.start(hl, xsend_h.at[:, ff : ff + width]))
    c_gout.wait()
    gc[...] = mm(sel[...], gout[...]).astype(bf16)
    c_win.wait()

    c_wback.wait()
    steps = [(j, m) for j in range(0, ff, 256) for m in range(0, SLOTS, SLOTS)]

    def inner(i):
        j, m = steps[i]
        return mm(hl[m : m + SLOTS, :], win[:, j : j + 256])

    def gelu(i, v):
        j, m = steps[i]
        v = v + bi[:, j : j + 256]
        cdf = 0.5 + 0.5 * erf_of(v)
        act[m : m + SLOTS, j : j + 256] = (v * cdf).astype(bf16)
        phi = jnp.exp2(v * v * (-0.5 * 1.4426950408889634)) * 0.3989422804014327
        gp[m : m + SLOTS, j : j + 256] = cdf + v * phi

    pipelined(len(steps), inner, gelu, nothing)
    outs.append(mover.start(act, act_h))
    outs.append(mover.start(act, xsend_h.at[:, :ff]))
    for m in range(0, SLOTS, SLOTS):
        for k in range(0, width, 256):
            branch[m : m + SLOTS, k : k + 256] = mm(act[m : m + SLOTS, :], wback[:, k : k + 256])
    nh2, r2 = norm_parts(hidden[...] + branch[...] + bb_ref[...])
    cot = gc[...].astype(f32)
    bs = norm_back(cot, nh2, r2, g2_ref[...])
    bl = bs.astype(bf16)
    bbr[...] = bl
    outs.append(mover.start(bbr, bbr_h))
    half = width // 2
    outs.append(
        mover.start(
            bbr.at[:, pl.ds(pl.multiple_of(other * half, half), half)],
            xsend_h.at[:, ff + width : ff + width + half],
        )
    )
    small_ref[:, :width] = colsum(cot * nh2)
    small_ref[:, width : 2 * width] = colsum(cot)
    small_ref[:, 2 * width : 3 * width] = colsum(bl.astype(f32))

    branch[...] = bs

    def back_active(i):
        j, m = steps[i]
        return mm_nt(bbr[m : m + SLOTS, :], wback[j : j + 256, :])

    def back_gelu(i, v):
        j, m = steps[i]
        b = (v * gp[m : m + SLOTS, j : j + 256]).astype(bf16)
        bin_[m : m + SLOTS, j : j + 256] = b
        part = colsum(b.astype(f32))
        at = slice(3 * width + j, 3 * width + j + 256)
        small_ref[:, at] = part if m == 0 else small_ref[:, at] + part

    pipelined(len(steps), back_active, back_gelu, nothing)
    outs.append(mover.start(bin_, bin_h))
    outs.append(
        mover.start(
            bin_.at[:, pl.ds(pl.multiple_of(other * (ff // 2), ff // 2), ff // 2)],
            xsend_h.at[:, ff + width + half :],
        )
    )
    for m in range(0, SLOTS, SLOTS):
        for k in range(0, width, 256):
            branch[m : m + SLOTS, k : k + 256] += mm_nt(bin_[m : m + SLOTS, :], win[k : k + 256, :])
    back_hidden = branch[...]
    nh = nhat[...]
    bp = norm_back(back_hidden, nh, rr[:, :1], g1_ref[...])
    bpre[...] = bp
    outs.append(mover.start(bpre, bpre_h))
    bl = bp.astype(bf16)
    battn[...] = bl
    outs.append(mover.start(battn, battn_h))
    bctx[...] = mm_nt(bl, wout[...]).astype(bf16)
    outs.append(mover.start(bctx, bctx_h))
    at = 3 * width + ff
    small_ref[:, at : at + width] = colsum(bl.astype(f32))
    small_ref[:, at + width : at + 2 * width] = colsum(back_hidden * nh)
    small_ref[:, at + 2 * width : at + 3 * width] = colsum(back_hidden)
    for copy in outs:
        copy.wait()


def marked_forward(core, m8, tokens, gout, w_qkv, b_query, b_value, w_out, b_out, g1, s1, w_in, b_in, w_back, b_back, g2):
    rows, width = tokens.shape
    ff = w_in.shape[1]
    tiles = SLOTS // TILE * (width // QUAD)
    outs = dict(
        sel=((SLOTS, rows), bf16), kv=((rows // LEN, LEN, 2 * width), bf16), tokc=((SLOTS, width), bf16),
        qs=((SLOTS, width), bf16), p=((tiles, LEN, 4 * TILE), bf16), ctx=((width, SLOTS), bf16),
        hl=((SLOTS, width), bf16),
        act=((SLOTS, ff), bf16), bbr=((SLOTS, width), bf16), bin=((SLOTS, ff), bf16),
        xsend=((SLOTS, (ff + width) * 3 // 2), bf16), battn=((SLOTS, width), bf16), bctx=((SLOTS, width), bf16),
        bpre=((SLOTS, width), f32), small=((1, 6 * width + ff), f32),
    )
    scratch = [
        ((rows, width), bf16), ((rows, width), bf16), (w_qkv.shape, bf16), (w_out.shape, bf16),
        (w_in.shape, bf16), (w_back.shape, bf16),
        outs["sel"], outs["kv"], outs["tokc"], ((SLOTS, width), bf16), outs["qs"], outs["p"], outs["ctx"],
        ((SLOTS, width), f32), ((SLOTS, 128), f32), ((SLOTS, width), f32), outs["hl"], outs["act"], ((SLOTS, ff), f32),
        ((SLOTS, width), f32), outs["bbr"], outs["bin"], ((1, width), f32), ((1, ff), f32),
        ((rows // LEN, width, LEN), bf16), outs["battn"], outs["bctx"], outs["bpre"],
    ]
    vmem = pl.BlockSpec(memory_space=pltpu.VMEM)
    smem = pl.BlockSpec(memory_space=pltpu.SMEM)
    hbm = pl.BlockSpec(memory_space=pl.ANY)
    res = pl.pallas_call(
        marked_forward_kernel,
        out_shape=[jax.ShapeDtypeStruct(*o) for o in outs.values()],
        in_specs=[smem] + [vmem] * 9 + [hbm] * 6,
        out_specs=[hbm] * 14 + [vmem],
        scratch_shapes=[pltpu.VMEM(*s) for s in scratch] + [pltpu.SemaphoreType.DMA((32,))],
        compiler_params=PARAMS,
        cost_estimate=COST,
        name="marked_forward",
    )(core, m8, b_query, b_value, b_out, g1, s1, b_in, b_back, g2,
      tokens, gout, w_qkv, w_out, w_in, w_back)
    return dict(zip(outs, res))


def place(piece, own, core, orders):
    bits = piece ^ own
    spots = []
    for order in orders:
        spot = 0
        for step in order:
            spot = spot * 2 + ((bits >> step) & 1)
        spots.append(spot)
    return spots[core] if isinstance(core, int) else spots[0] + core * (spots[1] - spots[0])


def marked_backward_kernel(
    where, m_ref, small_a, wqkv_h, bpre_h, bctx_h, p_h, qs_h, kv_h, tok_h, tokc_h, ctx_h, battn_h,
    bkv_h, rc_h, keep_h, send_h, small_h,
    wq, bpre, bctx, prob, qs, kv, tok, tokc, ctx, battn, dk, dv, bqt, bq, bkv, rc, kt, tokt, short, out, small, low,
    sems, *, pieces, orders,
):
    slots, width = qs.shape
    rows = tok.shape[0]
    quads = width // QUAD
    half = width // 2
    own, core = where[0], where[1]
    block = width // pieces
    size = 4 * block
    mover = Mover(sems)
    c_first = [mover.start(ctx_h, ctx), mover.start(battn_h, battn)]
    c_kv = [mover.start(kv_h, kv), mover.start(bctx_h, bctx), mover.start(qs_h, qs)]
    group = 2 * quads
    c_p = [
        mover.start(p_h.at[i : i + group], prob.at[i : i + group]) for i in range(0, prob.shape[0], group)
    ]
    c_tok = [mover.start(tok_h, tok), mover.start(tokc_h, tokc)]
    c_wq = mover.start(wqkv_h.at[:, :width], wq)
    c_bpre = mover.start(bpre_h, bpre)
    per_seq = LEN // 128
    first = jnp.sum(m_ref[:per_seq].astype(f32), axis=(0, 1), keepdims=True)
    a0_scalar = jnp.sum(jnp.floor((first + (TILE - 1)) * (1.0 / TILE)) * TILE).astype(jnp.int32)
    dk[...] = jnp.zeros_like(dk)
    dv[...] = jnp.zeros_like(dv)

    def products(left, right, chunks):
        for m in range(0, width, half):
            g = mm(left[m : m + half, :], right).astype(bf16)
            for c, (owner, chunk) in enumerate(chunks):
                for k in range(half // block):
                    at = place(m // block + k, own, owner, orders) * size + chunk * block
                    out[owner ^ core, pl.ds(pl.multiple_of(at, block), block), :] = g[
                        k * block : (k + 1) * block, c * half : (c + 1) * half
                    ]

    for c in c_first:
        c.wait()
    products(ctx, battn[...], ((0, 3), (1, 3)))
    for c in c_kv:
        c.wait()
    for q in range(kv.shape[0]):
        for g in range(quads):
            lanes = slice(g * QUAD, (g + 1) * QUAD)
            kt[q, lanes, :] = kv[q, :, lanes].T
    masks = lane_masks()
    steps = [(t, g, w) for t in range(slots // (2 * TILE)) for g in range(quads) for w in range(2)]
    kept = {}

    def place_of(i):
        t, g, w = steps[i]
        r0 = (2 * t + w) * TILE
        return r0, (r0 >= a0_scalar).astype(jnp.int32), slice(g * QUAD, (g + 1) * QUAD)

    def back_probs(i):
        t, g, w = steps[i]
        if g == 0 and w == 0:
            c_p[t].wait()
        r0, q, lanes = place_of(i)
        d4 = spread(bctx[r0 : r0 + TILE, lanes], masks)
        dp = mm_nt(kv[q, :, width + g * QUAD : width + (g + 1) * QUAD], d4)
        dv[q, :, lanes] += mm(prob[(2 * t + w) * quads + g], d4)
        return dp

    def back_scores(i, dp):
        t, g, w = steps[i]
        p = prob[(2 * t + w) * quads + g].astype(f32)
        weighted = p * dp
        return (weighted - p * colsum(weighted)).astype(bf16)

    def back_query_key(i, ds):
        t, g, w = steps[i]
        r0, q, lanes = place_of(i)
        dk[q, :, lanes] += mm(ds, spread(qs[r0 : r0 + TILE, lanes], masks))
        kept[w] = mm(kt[q, lanes, :], ds)
        if w == 1:
            for h in range(2):
                part = slice(128 * h, 128 * (h + 1))
                bqt[g * QUAD + 128 * h : g * QUAD + 128 * (h + 1), 128 * t : 128 * (t + 1)] = (
                    join_tiles(kept[0][part, part], kept[1][part, part]) * HEAD_DIM**-0.5
                ).astype(bf16)

    pipelined(len(steps), back_probs, back_scores, back_query_key)
    for q in range(kv.shape[0]):
        at = slice(q * LEN, (q + 1) * LEN)
        bkv[at, :width] = dk[q].astype(bf16)
        bkv[at, width:] = dv[q].astype(bf16)
    outs = [mover.start(bkv, bkv_h)]
    bq[...] = bqt[...].T
    for c in c_tok:
        c.wait()
    tokt[...] = tok[...].T
    short[...] = tokc[...].T
    products(short, bq[...], ((0, 0), (0, 1)))
    products(tokt, bkv[:, :width], ((0, 2), (1, 0)))
    products(tokt, bkv[:, width:], ((1, 1), (1, 2)))
    first_rows = small_a.shape[1] // half
    small[...] = jnp.zeros_like(small)
    for i in range(first_rows):
        small[i : i + 1, :] = small_a[:, i * half : (i + 1) * half]
    for i, lanes in enumerate((slice(0, half), slice(half, width))):
        small[first_rows + i : first_rows + i + 1, :] = colsum(bq[:, lanes].astype(f32))
        small[first_rows + 2 + i : first_rows + 3 + i, :] = colsum(
            bkv[:, width + i * half : width + (i + 1) * half].astype(f32)
        )
    high = small[...].astype(bf16)
    low[:SMALL] = high
    low[SMALL:] = (small[...] - high.astype(f32)).astype(bf16)
    outs += [
        mover.start(out.at[1], send_h.at[: 4 * width, :]),
        mover.start(low, send_h.at[4 * width :, :]),
        mover.start(out.at[0], keep_h),
        mover.start(small, small_h),
    ]
    c_wq.wait()
    c_bpre.wait()
    rc[...] = (bpre[...] + mm_nt(bq[...], wq[...])).astype(bf16)
    outs.append(mover.start(rc, rc_h))
    for copy in outs:
        copy.wait()


def marked_backward(where, m8, tokens, w_qkv, a, pieces, orders):
    rows, width = tokens.shape
    half = width // 2
    outs = dict(
        bkv=((rows, 2 * width), bf16), rc=((SLOTS, width), bf16), keep=((4 * width, half), bf16),
        send=((4 * width + 2 * SMALL, half), bf16), small=((SMALL, half), f32),
    )
    ins = [a["bpre"], a["bctx"], a["p"], a["qs"], a["kv"], tokens, a["tokc"], a["ctx"], a["battn"]]
    scratch = [((width, width), bf16)] + [(v.shape, v.dtype) for v in ins]
    scratch += [
        ((rows // LEN, LEN, width), f32), ((rows // LEN, LEN, width), f32), ((width, SLOTS), bf16),
        ((SLOTS, width), bf16), outs["bkv"], outs["rc"], ((rows // LEN, width, LEN), bf16), ((width, rows), bf16),
        ((width, SLOTS), bf16), ((2, 4 * width, half), bf16), outs["small"], ((2 * SMALL, half), bf16),
    ]
    vmem = pl.BlockSpec(memory_space=pltpu.VMEM)
    smem = pl.BlockSpec(memory_space=pltpu.SMEM)
    hbm = pl.BlockSpec(memory_space=pl.ANY)
    res = pl.pallas_call(
        functools.partial(marked_backward_kernel, pieces=pieces, orders=orders),
        out_shape=[jax.ShapeDtypeStruct(*o) for o in outs.values()],
        in_specs=[smem, vmem, vmem] + [hbm] * 10,
        out_specs=[hbm] * 5,
        scratch_shapes=[pltpu.VMEM(*s) for s in scratch] + [pltpu.SemaphoreType.DMA((24,))],
        compiler_params=PARAMS,
        cost_estimate=COST,
        name="marked_backward",
    )(where, m8, a["small"], w_qkv, *ins)
    return dict(zip(outs, res))


def attention_rows_kernel(
    which, bq_ref, bo_ref, g1_ref, s1_ref, tok_h, kv_h, wqkv_h, wout_h, hidden_h,
    tok, kv, wq, wout, q, ctx, hidden, vt, sems,
):
    width = wq.shape[1]
    quads = width // QUAD
    tile = 128
    mover = Mover(sems)
    i = which[0]
    r0 = pl.multiple_of(i * LEN, LEN)
    c_tok = mover.start(tok_h.at[pl.ds(r0, LEN), :], tok)
    c_wq = mover.start(wqkv_h.at[:, :width], wq)
    c_kv = mover.start(kv_h.at[i], kv)
    c_wout = mover.start(wout_h, wout)
    c_tok.wait()
    c_wq.wait()
    q[...] = ((mm(tok[...], wq[...]) + bq_ref[...]).astype(bf16).astype(f32) * HEAD_DIM**-0.5).astype(bf16)
    c_kv.wait()
    for g in range(quads):
        vt[g * QUAD : (g + 1) * QUAD, :] = kv[:, width + g * QUAD : width + (g + 1) * QUAD].T
    masks = lane_masks()
    steps = [(t, g) for t in range(LEN // tile) for g in range(quads)]

    def scores(i):
        t, g = steps[i]
        lanes = slice(g * QUAD, (g + 1) * QUAD)
        return mm_nt(kv[:, lanes], spread(q[t * tile : (t + 1) * tile, lanes], masks))

    def probabilities(i, s):
        e, inv = softmax_columns(s)
        return e.astype(bf16), inv

    def values(i, parts):
        t, g = steps[i]
        p, inv = parts
        for h in range(2):
            at = g * QUAD + 128 * h
            z = mm(vt[at : at + 128, :], p[:, h * 2 * tile : (h + 1) * 2 * tile])
            for u in range(2):
                tokens = slice((2 * h + u) * tile, (2 * h + u + 1) * tile)
                ctx[at + u * HEAD_DIM : at + (u + 1) * HEAD_DIM, t * tile : (t + 1) * tile] = (
                    z[u * HEAD_DIM : (u + 1) * HEAD_DIM, u * tile : (u + 1) * tile] * inv[:, tokens]
                ).astype(bf16)

    pipelined(len(steps), scores, probabilities, values)
    c_wout.wait()
    nh, _ = norm_parts(mm(ctx[...].T, wout[...]) + bo_ref[...] + tok[...].astype(f32))
    hid = nh * g1_ref[...] + s1_ref[...]
    hidden[...] = hid
    mover.start(hidden, hidden_h).wait()


def attention_rows(which, tokens, kv, w_qkv, b_query, w_out, b_out, g1, s1):
    width = tokens.shape[1]
    vmem = pl.BlockSpec(memory_space=pltpu.VMEM)
    smem = pl.BlockSpec(memory_space=pltpu.SMEM)
    hbm = pl.BlockSpec(memory_space=pl.ANY)
    scratch = [
        ((LEN, width), bf16), ((LEN, 2 * width), bf16), ((width, width), bf16), (w_out.shape, bf16),
        ((LEN, width), bf16), ((width, LEN), bf16), ((LEN, width), f32), ((width, LEN), bf16),
    ]
    return pl.pallas_call(
        attention_rows_kernel,
        out_shape=jax.ShapeDtypeStruct((LEN, width), f32),
        in_specs=[smem] + [vmem] * 4 + [hbm] * 4,
        out_specs=hbm,
        scratch_shapes=[pltpu.VMEM(*s) for s in scratch] + [pltpu.SemaphoreType.DMA((8,))],
        compiler_params=PARAMS,
        cost_estimate=COST,
        name="attention_rows",
    )(jnp.full((1,), which, jnp.int32), b_query, b_out, g1, s1, tokens, kv, w_qkv, w_out)


def ffn_rows_kernel(
    which, bi_ref, bb_ref, g2_ref, s2_ref, hidden_h, win_h, wback_h, *rest,
):
    (out_h, win, wback, hl, hidden, act, branch, out, bi, sems) = rest[-10:]
    width, ff = win.shape
    mover = Mover(sems)
    r0 = pl.multiple_of(which[0] * LEN, LEN)
    c_hidden = mover.start(hidden_h, hidden)
    part = ff // 4
    c_win = [mover.start(win_h.at[:, k : k + part], win.at[:, k : k + part]) for k in range(0, ff, part)]
    c_wback = mover.start(wback_h, wback)
    bi[...] = bi_ref[...].reshape(bi.shape)
    c_hidden.wait()
    hl[...] = hidden[...].astype(bf16)
    steps = [(j, m) for j in range(0, ff, 256) for m in range(0, LEN, ROWS)]

    def inner(i):
        j, m = steps[i]
        if j % part == 0 and m == 0:
            c_win[j // part].wait()
        return mm(hl[m : m + ROWS, :], win[:, j : j + 256])

    def gelu(i, v):
        j, m = steps[i]
        v = v + bi[:, j : j + 256]
        h = v * 0.5
        act[m : m + ROWS, j : j + 256] = (h + h * erf_of(v)).astype(bf16)

    pipelined(len(steps), inner, gelu, nothing)
    c_wback.wait()
    for m in range(0, LEN, 256):
        for k in range(0, width, 256):
            branch[m : m + 256, k : k + 256] = mm(act[m : m + 256, :], wback[:, k : k + 256])
    nh2, _ = norm_parts(hidden[...] + branch[...] + bb_ref[...])
    out[...] = (nh2 * g2_ref[...] + s2_ref[...]).astype(bf16)
    mover.start(out, out_h.at[pl.ds(r0, LEN), :]).wait()


def ffn_rows(which, previous, rows, hidden, w_in, b_in, w_back, b_back, g2, s2):
    width, ff = w_in.shape
    vmem = pl.BlockSpec(memory_space=pltpu.VMEM)
    smem = pl.BlockSpec(memory_space=pltpu.SMEM)
    hbm = pl.BlockSpec(memory_space=pl.ANY)
    scratch = [
        (w_in.shape, bf16), (w_back.shape, bf16), ((LEN, width), bf16), ((LEN, width), f32), ((LEN, ff), bf16),
        ((LEN, width), f32), ((LEN, width), bf16), ((1, ff), f32),
    ]
    extra = () if previous is None else (previous,)
    return pl.pallas_call(
        ffn_rows_kernel,
        out_shape=jax.ShapeDtypeStruct((rows, width), bf16),
        in_specs=[smem] + [vmem] * 4 + [hbm] * (3 + len(extra)),
        out_specs=hbm,
        scratch_shapes=[pltpu.VMEM(*s) for s in scratch] + [pltpu.SemaphoreType.DMA((12,))],
        input_output_aliases={8: 0} if extra else {},
        compiler_params=PARAMS,
        cost_estimate=COST,
        name="ffn_rows",
    )(jnp.full((1,), which, jnp.int32), b_in, b_back, g2, s2, hidden, w_in, w_back, *extra)


def ffn_grads_kernel(
    where, act_h, hl_h, bbr_h, bin_h, x_h, keep1_h, send1_h, keep2_h, send2_h,
    act, hl, bbr, bin_, out1, out2, hlt, sems, *, pieces, orders,
):
    own, core = where[0], where[1]
    slots, ff = act_h.shape
    width = hl_h.shape[1]
    half = width // 2
    mover = Mover(sems)
    up, down = slice(0, slots), slice(slots, 2 * slots)
    mine = lambda n: pl.ds(pl.multiple_of(core * n, n), n)
    c1 = [
        mover.start(bbr_h.at[:, mine(half)], bbr.at[up, :]),
        mover.start(x_h.at[:, ff + width : ff + width + half], bbr.at[down, :]),
        mover.start(act_h, act.at[up, :]),
        mover.start(x_h.at[:, :ff], act.at[down, :]),
    ]
    c2 = [
        mover.start(hl_h, hl.at[up, :]),
        mover.start(x_h.at[:, ff : ff + width], hl.at[down, :]),
        mover.start(bin_h.at[:, mine(ff // 2)], bin_.at[up, :]),
        mover.start(x_h.at[:, ff + width + half :], bin_.at[down, :]),
    ]
    for c in c1:
        c.wait()
    size, block = ff // pieces, width // pieces
    for j in range(ff // half):
        g = mm_tn(act[:, j * half : (j + 1) * half], bbr[...]).astype(bf16)
        for k in range(half // size):
            at = place(j * (half // size) + k, own, core, orders[0]) * size
            out1[pl.ds(pl.multiple_of(at, size), size), :] = g[k * size : (k + 1) * size]
    rows = ff // 2
    outs = [mover.start(out1.at[rows:, :], send1_h), mover.start(out1.at[:rows, :], keep1_h)]
    for c in c2:
        c.wait()
    for i in range(2):
        hlt[...] = hl[:, i * half : (i + 1) * half].T
        for j in range(ff // width):
            g = mm(hlt[...], bin_[:, j * half : (j + 1) * half]).astype(bf16)
            for k in range(half // block):
                at = place(i * (half // block) + k, own, core, orders[1]) * size + j * block
                out2[pl.ds(pl.multiple_of(at, block), block), :] = g[k * block : (k + 1) * block]
    outs += [mover.start(out2.at[rows:, :], send2_h), mover.start(out2.at[:rows, :], keep2_h)]
    for c in outs:
        c.wait()


def ffn_grads(where, a, x, pieces, orders):
    slots, ff = a["act"].shape
    width = a["hl"].shape[1]
    half = width // 2
    smem = pl.BlockSpec(memory_space=pltpu.SMEM)
    hbm = pl.BlockSpec(memory_space=pl.ANY)
    scratch = [
        (2 * slots, ff), (2 * slots, width), (2 * slots, half), (2 * slots, ff // 2), (ff, half), (ff, half),
        (half, 2 * slots),
    ]
    return pl.pallas_call(
        functools.partial(ffn_grads_kernel, pieces=pieces, orders=orders),
        out_shape=[jax.ShapeDtypeStruct((ff // 2, half), bf16)] * 4,
        in_specs=[smem] + [hbm] * 5,
        out_specs=[hbm] * 4,
        scratch_shapes=[pltpu.VMEM(s, bf16) for s in scratch] + [pltpu.SemaphoreType.DMA((12,))],
        compiler_params=PARAMS,
        cost_estimate=COST,
        name="ffn_grads",
    )(where, a["act"], a["hl"], a["bbr"], a["bin"], x)


def add_low(a, b):
    return (a.astype(f32) + b.astype(f32)).astype(bf16)


def after(value, *others):
    return lax.optimization_barrier((value, others))[0]


def two_parts(v):
    high = lax.reduce_precision(v, 8, 7)
    return [high.astype(bf16), (v - high).astype(bf16)]


def one_part(v):
    return v[:SMALL].astype(f32) + v[SMALL:].astype(f32)


class Reduction:
    def __init__(self, keep, send, orders, n, small=None):
        self.keep, self.send, self.orders, self.n, self.small = keep, send, orders, n, small
        self.step = 0
        self.start()

    def start(self):
        pairs = [
            (2 * i + core, 2 * (i ^ (1 << self.orders[core][self.step])) + core)
            for i in range(self.n)
            for core in range(2)
        ]
        send = self.send
        if self.small is not None:
            send = jnp.concatenate([send] + two_parts(self.small))
        self.got = lax.ppermute(send, ("dp", "head"), pairs)

    def advance(self, *others):
        keep, got, small = after((self.keep, self.got, self.small), *others)
        self.step += 1
        rows = keep.shape[0]
        if small is not None:
            self.small = small + one_part(got[rows:])
            got = got[:rows]
        if self.step == len(self.orders[0]):
            self.share = keep.astype(f32) + got.astype(f32)
            return self.share
        m = rows // 2
        self.send = add_low(keep[m:], got[m:])
        self.start()
        self.keep = add_low(keep[:m], got[:m])
        return self.keep


def columns(share, count):
    rows = share.shape[0] // count
    return jnp.concatenate([share[i * rows : (i + 1) * rows] for i in range(count)], axis=1)


def body(
    tokens, w_qkv, b_query, b_value, w_out, b_out, gain_attn, shift_attn, w_in, b_in, w_back, b_back,
    gain_out, shift_out, grad_out, masked,
):
    rows, width = tokens.shape
    ff = w_in.shape[1]
    n = lax.axis_size("dp")
    core = lax.axis_index("head")
    steps = n.bit_length() - 1
    halving = n == 1 << steps and width // n % 16 == 0
    if halving:
        own = lax.axis_index("dp")
        rest = tuple(range(3, steps))
        plane_first = ((0, 1, 2) + rest, (1, 0, 2) + rest)
        line_first = ((2, 0, 1) + rest, (2, 1, 0) + rest)
        orders = [plane_first, line_first, plane_first]
        pieces = n
    else:
        own = jnp.int32(0)
        orders = [((3, 2, 1, 0),) * 2] * 3
        pieces = 16
    where = jnp.stack([own, core]).astype(jnp.int32)
    m8 = masked.reshape(-1, 128)
    swap_cores = lambda v: lax.ppermute(v, "head", [(0, 1), (1, 0)])

    a = marked_forward(
        core.reshape(1).astype(jnp.int32), m8, tokens, grad_out, w_qkv, b_query, b_value, w_out, b_out,
        gain_attn, shift_attn, w_in, b_in, w_back, b_back, gain_out,
    )
    x = swap_cores(a["xsend"])
    b = marked_backward(where, m8, tokens, w_qkv, a, pieces, orders[2])
    got3 = swap_cores(b["send"])
    keep1, send1, keep2, send2 = ffn_grads(after(where, b["rc"]), a, x, pieces, orders[:2])
    keep3, got3, small = after((b["keep"], got3, b["small"]), keep1)
    small = small + one_part(got3[4 * width :])
    m = 2 * width
    if halving:
        r1 = Reduction(keep1, send1, orders[0], n)
        r2 = Reduction(keep2, send2, orders[1], n)
        r3 = Reduction(
            add_low(keep3[:m], got3[:m]), add_low(keep3[m:], got3[m : 2 * m]), orders[2], n, small
        )
        done = r3.keep
    else:
        r1 = r2 = r3 = None
        both3 = done = add_low(keep3, got3[: 2 * m])

    def attention(which, done):
        return attention_rows(which, after(tokens, done), a["kv"], w_qkv, b_query, w_out, b_out, gain_attn, shift_attn)

    def ffn(which, previous, hidden, done):
        return ffn_rows(which, previous, rows, after(hidden, done), w_in, b_in, w_back, b_back, gain_out, shift_out)

    def turn(done, *chains):
        if halving:
            for chain in chains:
                done = chain.advance(done)
        return done

    hidden = attention(0, done)
    layer_out = ffn(0, None, hidden, hidden)
    done = turn(layer_out, r1)
    hidden = attention(1, done)
    done = turn(hidden, r1, r2, r3)
    layer_out = ffn(1, layer_out, hidden, done)
    done = turn(layer_out, r3, r2, r1)
    sel, wkv = after((a["sel"], w_qkv[:, width:]), done)
    grad_tokens = mm_tn(sel, b["rc"]) + mm_nt(b["bkv"], wkv)
    done = turn(grad_tokens, r3, r2, r1)
    done = turn(done, r3, r2)
    if halving:
        shares = [r1.share, r2.share, r3.share]
        small = r3.small
    else:
        total = lambda v: lax.psum_scatter(v, "dp", scatter_dimension=0, tiled=True).astype(f32)
        natural = lambda v, count: columns_of_blocks(v, count, pieces)
        small = lax.psum(small, "dp")
        shares = [
            total(jnp.concatenate([keep1, send1])),
            total(natural(jnp.concatenate([keep2, send2]), 4)),
            total(natural(both3, 4)),
        ]
    small = small.reshape(-1)
    names = (("gain_out", width), ("shift_out", width), ("b_back", width), ("b_in", ff), ("b_out", width),
             ("gain_attn", width), ("shift_attn", width), ("b_query", width), ("b_value", width))
    sums, at = {}, 0
    for name, size in names:
        sums[name] = small[at : at + size]
        at += size
    if halving:
        shares[1] = columns(shares[1], 4)
        shares[2] = columns(shares[2], 4)
    half3 = 3 * width // 2
    return (
        layer_out, grad_tokens, shares[2][:, :half3], sums["b_query"], sums["b_value"], shares[2][:, half3:],
        sums["b_out"], sums["gain_attn"], sums["shift_attn"], shares[1], sums["b_in"], shares[0],
        sums["b_back"], sums["gain_out"], sums["shift_out"],
    )


def columns_of_blocks(v, count, pieces):
    lanes = v.shape[1]
    v = v.reshape(pieces, count, -1, lanes)
    return jnp.moveaxis(v, 1, 2).reshape(-1, count * lanes)


def solution(mesh):
    rows = P(("dp", "head"), None)
    shard = P("dp", "head")
    return jax.shard_map(
        body,
        mesh=mesh,
        in_specs=(rows,) + (P(),) * 13 + (rows, P(("dp", "head"))),
        out_specs=(rows, rows, shard, P(), P(), shard, P(), P(), P(), shard, P(), shard, P(), P(), P()),
        check_vma=False,
    )
```

```python
import functools

import jax
import jax.numpy as jnp
from jax import lax
from jax.experimental import pallas as pl
from jax.experimental.pallas import tpu as pltpu
from jax.sharding import PartitionSpec as P

HEADS = 12
HEAD_DIM = 64
LEN = 512
CAP = 320
TALL = 384
ROWS = 256
SMALL = 32
TILE = 64
SLOTS = (CAP // TILE + 1) * TILE
QUAD = 4 * HEAD_DIM
COST = pl.CostEstimate(flops=1000, bytes_accessed=1000, transcendentals=0)

epsilon = 1e-12
bf16 = jnp.bfloat16
f32 = jnp.float32


def params(mib):
    return pltpu.CompilerParams(vmem_limit_bytes=mib * 1024 * 1024)


def mm(a, b):
    return jnp.dot(a, b, preferred_element_type=f32)


def mm_nt(a, b):
    return lax.dot_general(a, b, (((1,), (1,)), ((), ())), preferred_element_type=f32)


def mm_tn(a, b):
    return lax.dot_general(a, b, (((0,), (0,)), ((), ())), preferred_element_type=f32)


def colsum(v):
    return jnp.sum(v, axis=0, keepdims=True)


def rowmean(v):
    return jnp.sum(v, axis=-1, keepdims=True) * (1.0 / v.shape[-1])


def norm_parts(v):
    centred = v - rowmean(v)
    r = lax.rsqrt(rowmean(centred * centred) + epsilon)
    return centred * r, r


def norm_back(cot, nhat, r, gain):
    e = cot * gain
    return r * (e - rowmean(e) - nhat * rowmean(e * nhat))


def erf_of(v):
    return lax.erf(v * 0.7071067811865476)


def lane_masks():
    head = lax.broadcasted_iota(jnp.int32, (1, QUAD), 1) // HEAD_DIM
    return [(head == j).astype(f32).astype(bf16) for j in range(4)]


def spread(x, masks):
    return jnp.concatenate([x * m for m in masks], axis=0)


def softmax_columns(scores):
    e = jnp.exp(scores - jnp.max(scores, axis=0, keepdims=True))
    return e, 1.0 / jnp.sum(e, axis=0, keepdims=True)


def join_tiles(first, second):
    low = lax.broadcasted_iota(jnp.int32, (HEAD_DIM, 2 * TILE), 1) < TILE
    top = jnp.where(low, first[:HEAD_DIM], pltpu.roll(second[:HEAD_DIM], TILE, 1))
    bottom = jnp.where(low, pltpu.roll(first[HEAD_DIM:], TILE, 1), second[HEAD_DIM:])
    return jnp.concatenate([top, bottom], axis=0)


def nothing(i, value):
    pass


def pipelined(count, early, middle, late):
    ahead = early(0)
    waiting = None
    for i in range(count):
        now, ahead = ahead, early(i + 1) if i + 1 < count else None
        if waiting is not None:
            late(i - 1, waiting)
        waiting = middle(i, now)
    late(count - 1, waiting)


class Mover:
    def __init__(self, sems):
        self.sems = sems
        self.count = 0

    def start(self, src, dst):
        copy = pltpu.make_async_copy(src, dst, self.sems.at[self.count])
        self.count += 1
        copy.start()
        return copy


def marked_forward_kernel(
    core_ref, m_ref, bq_ref, bv_ref, bo_ref, g1_ref, s1_ref, bi_ref, bb_ref, g2_ref,
    tok_h, gout_h, wqkv_h, wout_h, win_h, wback_h,
    sel_h, kv_h, tokc_h, qs_h, p_h, ctx_h, hl_h, act_h, bbr_h, bin_h, xsend_h, battn_h, bctx_h, bpre_h, small_ref,
    tok, gout, wqkv, wout, win, wback,
    sel, kv, tokc, gc, qs, prob, ctx, nhat, rr, hidden, hl, act, gp, branch, bbr, bin_, bv, bi, vt,
    battn, bctx, bpre,
    sems,
):
    rows, width = tok.shape
    ff = win.shape[1]
    quads = width // QUAD
    mover = Mover(sems)
    other = 1 - core_ref[0]
    c_tok = mover.start(tok_h, tok)
    c_wqkv = mover.start(wqkv_h, wqkv)
    c_gout = mover.start(gout_h, gout)
    c_wout = mover.start(wout_h, wout)
    c_win = mover.start(win_h, win)
    c_wback = mover.start(wback_h, wback)
    outs = []
    bv[...] = bv_ref[...].reshape(bv.shape)
    bi[...] = bi_ref[...].reshape(bi.shape)
    m8 = m_ref[...].astype(f32)
    groups = m8.shape[0]
    per_seq = LEN // 128
    tri = (
        lax.broadcasted_iota(jnp.int32, (128, 128), 0)
        <= lax.broadcasted_iota(jnp.int32, (128, 128), 1)
    ).astype(f32).astype(bf16)
    within = mm(m8.astype(bf16), tri)
    first = jnp.sum(m8[:per_seq], axis=(0, 1), keepdims=True)
    a0 = jnp.floor((first + (TILE - 1)) * (1.0 / TILE)) * TILE
    offset = jnp.zeros((1, 1), f32)
    slot_iota = lax.broadcasted_iota(jnp.int32, (SLOTS, 128), 0).astype(f32)
    for g in range(groups):
        if g == per_seq:
            offset = a0
        slot = jnp.where(m8[g : g + 1] > 0.0, offset + within[g : g + 1] - 1.0, -1.0)
        sel[:, 128 * g : 128 * (g + 1)] = (slot_iota == slot).astype(f32).astype(bf16)
        offset = offset + within[g : g + 1, 127:128]
    outs.append(mover.start(sel, sel_h))
    a0_scalar = jnp.sum(a0).astype(jnp.int32)

    c_tok.wait()
    tokc[...] = mm(sel[...], tok[...]).astype(bf16)
    outs.append(mover.start(tokc, tokc_h))
    c_wqkv.wait()
    for q in range(rows // LEN):
        for i in range(2 * width // QUAD):
            at = slice(i * QUAD, (i + 1) * QUAD)
            value = mm(tok[q * LEN : (q + 1) * LEN, :], wqkv[:, width + i * QUAD : width + (i + 1) * QUAD])
            if i >= quads:
                low = (value + bv[:, i * QUAD - width : (i + 1) * QUAD - width]).astype(bf16)
                vt[q, i * QUAD - width : (i + 1) * QUAD - width, :] = low.T
                kv[q, :, at] = low
            else:
                kv[q, :, at] = value.astype(bf16)
    outs.append(mover.start(kv, kv_h))
    qs[...] = (
        (mm(tokc[...], wqkv[:, :width]) + bq_ref[...]).astype(bf16).astype(f32) * HEAD_DIM**-0.5
    ).astype(bf16)
    outs.append(mover.start(qs, qs_h))

    masks = lane_masks()
    steps = [(t, g, w) for t in range(SLOTS // (2 * TILE)) for g in range(quads) for w in range(2)]
    kept = {}

    def place_of(i):
        t, g, w = steps[i]
        r0 = (2 * t + w) * TILE
        return r0, (r0 >= a0_scalar).astype(jnp.int32), slice(g * QUAD, (g + 1) * QUAD)

    def scores(i):
        r0, q, lanes = place_of(i)
        return mm_nt(kv[q, :, lanes], spread(qs[r0 : r0 + TILE, lanes], masks))

    def probabilities(i, s):
        t, g, w = steps[i]
        e, inv = softmax_columns(s)
        p = (e * inv).astype(bf16)
        prob[(2 * t + w) * quads + g] = p
        return p

    def values(i, p):
        t, g, w = steps[i]
        r0, q, lanes = place_of(i)
        kept[w] = mm(vt[q, lanes, :], p)
        if w == 1:
            for h in range(2):
                part = slice(128 * h, 128 * (h + 1))
                ctx[g * QUAD + 128 * h : g * QUAD + 128 * (h + 1), 128 * t : 128 * (t + 1)] = join_tiles(
                    kept[0][part, part], kept[1][part, part]
                ).astype(bf16)

    pipelined(len(steps), scores, probabilities, values)
    outs.append(mover.start(prob, p_h))
    outs.append(mover.start(ctx, ctx_h))
    c_wout.wait()
    pre = mm(ctx[...].T, wout[...]) + bo_ref[...] + tokc[...].astype(f32)
    nh, r = norm_parts(pre)
    nhat[...] = nh
    rr[...] = jnp.broadcast_to(r, rr.shape)
    hid = nh * g1_ref[...] + s1_ref[...]
    hidden[...] = hid
    hl[...] = hid.astype(bf16)
    outs.append(mover.start(hl, hl_h))
    outs.append(mover.start(hl, xsend_h.at[:, ff : ff + width]))
    c_gout.wait()
    gc[...] = mm(sel[...], gout[...]).astype(bf16)
    c_win.wait()

    c_wback.wait()
    steps = [(j, m) for j in range(0, ff, 256) for m in range(0, SLOTS, SLOTS)]

    def inner(i):
        j, m = steps[i]
        return mm(hl[m : m + SLOTS, :], win[:, j : j + 256])

    def gelu(i, v):
        j, m = steps[i]
        v = v + bi[:, j : j + 256]
        cdf = 0.5 + 0.5 * erf_of(v)
        act[m : m + SLOTS, j : j + 256] = (v * cdf).astype(bf16)
        phi = jnp.exp2(v * v * (-0.5 * 1.4426950408889634)) * 0.3989422804014327
        gp[m : m + SLOTS, j : j + 256] = cdf + v * phi

    pipelined(len(steps), inner, gelu, nothing)
    outs.append(mover.start(act, act_h))
    outs.append(mover.start(act, xsend_h.at[:, :ff]))
    for m in range(0, SLOTS, SLOTS):
        for k in range(0, width, 256):
            branch[m : m + SLOTS, k : k + 256] = mm(act[m : m + SLOTS, :], wback[:, k : k + 256])
    nh2, r2 = norm_parts(hidden[...] + branch[...] + bb_ref[...])
    cot = gc[...].astype(f32)
    bs = norm_back(cot, nh2, r2, g2_ref[...])
    bl = bs.astype(bf16)
    bbr[...] = bl
    outs.append(mover.start(bbr, bbr_h))
    half = width // 2
    outs.append(
        mover.start(
            bbr.at[:, pl.ds(pl.multiple_of(other * half, half), half)],
            xsend_h.at[:, ff + width : ff + width + half],
        )
    )
    small_ref[:, :width] = colsum(cot * nh2)
    small_ref[:, width : 2 * width] = colsum(cot)
    small_ref[:, 2 * width : 3 * width] = colsum(bl.astype(f32))

    branch[...] = bs

    def back_active(i):
        j, m = steps[i]
        return mm_nt(bbr[m : m + SLOTS, :], wback[j : j + 256, :])

    def back_gelu(i, v):
        j, m = steps[i]
        b = (v * gp[m : m + SLOTS, j : j + 256]).astype(bf16)
        bin_[m : m + SLOTS, j : j + 256] = b
        part = colsum(b.astype(f32))
        at = slice(3 * width + j, 3 * width + j + 256)
        small_ref[:, at] = part if m == 0 else small_ref[:, at] + part

    pipelined(len(steps), back_active, back_gelu, nothing)
    outs.append(mover.start(bin_, bin_h))
    outs.append(
        mover.start(
            bin_.at[:, pl.ds(pl.multiple_of(other * (ff // 2), ff // 2), ff // 2)],
            xsend_h.at[:, ff + width + half :],
        )
    )
    for m in range(0, SLOTS, SLOTS):
        for k in range(0, width, 256):
            branch[m : m + SLOTS, k : k + 256] += mm_nt(bin_[m : m + SLOTS, :], win[k : k + 256, :])
    back_hidden = branch[...]
    nh = nhat[...]
    bp = norm_back(back_hidden, nh, rr[:, :1], g1_ref[...])
    bpre[...] = bp
    outs.append(mover.start(bpre, bpre_h))
    bl = bp.astype(bf16)
    battn[...] = bl
    outs.append(mover.start(battn, battn_h))
    bctx[...] = mm_nt(bl, wout[...]).astype(bf16)
    outs.append(mover.start(bctx, bctx_h))
    at = 3 * width + ff
    small_ref[:, at : at + width] = colsum(bl.astype(f32))
    small_ref[:, at + width : at + 2 * width] = colsum(back_hidden * nh)
    small_ref[:, at + 2 * width : at + 3 * width] = colsum(back_hidden)
    for copy in outs:
        copy.wait()


def marked_forward(core, m8, tokens, gout, w_qkv, b_query, b_value, w_out, b_out, g1, s1, w_in, b_in, w_back, b_back, g2):
    rows, width = tokens.shape
    ff = w_in.shape[1]
    tiles = SLOTS // TILE * (width // QUAD)
    outs = dict(
        sel=((SLOTS, rows), bf16), kv=((rows // LEN, LEN, 2 * width), bf16), tokc=((SLOTS, width), bf16),
        qs=((SLOTS, width), bf16), p=((tiles, LEN, 4 * TILE), bf16), ctx=((width, SLOTS), bf16),
        hl=((SLOTS, width), bf16),
        act=((SLOTS, ff), bf16), bbr=((SLOTS, width), bf16), bin=((SLOTS, ff), bf16),
        xsend=((SLOTS, (ff + width) * 3 // 2), bf16), battn=((SLOTS, width), bf16), bctx=((SLOTS, width), bf16),
        bpre=((SLOTS, width), f32), small=((1, 6 * width + ff), f32),
    )
    scratch = [
        ((rows, width), bf16), ((rows, width), bf16), (w_qkv.shape, bf16), (w_out.shape, bf16),
        (w_in.shape, bf16), (w_back.shape, bf16),
        outs["sel"], outs["kv"], outs["tokc"], ((SLOTS, width), bf16), outs["qs"], outs["p"], outs["ctx"],
        ((SLOTS, width), f32), ((SLOTS, 128), f32), ((SLOTS, width), f32), outs["hl"], outs["act"], ((SLOTS, ff), f32),
        ((SLOTS, width), f32), outs["bbr"], outs["bin"], ((1, width), f32), ((1, ff), f32),
        ((rows // LEN, width, LEN), bf16), outs["battn"], outs["bctx"], outs["bpre"],
    ]
    vmem = pl.BlockSpec(memory_space=pltpu.VMEM)
    smem = pl.BlockSpec(memory_space=pltpu.SMEM)
    hbm = pl.BlockSpec(memory_space=pl.ANY)
    res = pl.pallas_call(
        marked_forward_kernel,
        out_shape=[jax.ShapeDtypeStruct(*o) for o in outs.values()],
        in_specs=[smem] + [vmem] * 9 + [hbm] * 6,
        out_specs=[hbm] * 14 + [vmem],
        scratch_shapes=[pltpu.VMEM(*s) for s in scratch] + [pltpu.SemaphoreType.DMA((32,))],
        compiler_params=params(60),
        cost_estimate=COST,
        name="marked_forward",
    )(core, m8, b_query, b_value, b_out, g1, s1, b_in, b_back, g2,
      tokens, gout, w_qkv, w_out, w_in, w_back)
    return dict(zip(outs, res))


def place(piece, own, core, orders):
    bits = piece ^ own
    spots = []
    for order in orders:
        spot = 0
        for step in order:
            spot = spot * 2 + ((bits >> step) & 1)
        spots.append(spot)
    return spots[core] if isinstance(core, int) else spots[0] + core * (spots[1] - spots[0])


def marked_backward_kernel(
    where, m_ref, small_a, wqkv_h, bpre_h, bctx_h, p_h, qs_h, kv_h, tok_h, tokc_h, ctx_h, battn_h,
    bkv_h, rc_h, keep_h, send_h, small_h,
    wq, bpre, bctx, prob, qs, kv, tok, tokc, ctx, battn, dk, dv, bqt, bq, bkv, rc, kt, tokt, short, out, small, low,
    sems, *, pieces, orders,
):
    slots, width = qs.shape
    rows = tok.shape[0]
    quads = width // QUAD
    half = width // 2
    own, core = where[0], where[1]
    block = width // pieces
    size = 4 * block
    mover = Mover(sems)
    c_first = [mover.start(ctx_h, ctx), mover.start(battn_h, battn)]
    c_kv = [mover.start(kv_h, kv), mover.start(bctx_h, bctx), mover.start(qs_h, qs)]
    group = 2 * quads
    c_p = [
        mover.start(p_h.at[i : i + group], prob.at[i : i + group]) for i in range(0, prob.shape[0], group)
    ]
    c_tok = [mover.start(tok_h, tok), mover.start(tokc_h, tokc)]
    c_wq = mover.start(wqkv_h.at[:, :width], wq)
    c_bpre = mover.start(bpre_h, bpre)
    per_seq = LEN // 128
    first = jnp.sum(m_ref[:per_seq].astype(f32), axis=(0, 1), keepdims=True)
    a0_scalar = jnp.sum(jnp.floor((first + (TILE - 1)) * (1.0 / TILE)) * TILE).astype(jnp.int32)
    dk[...] = jnp.zeros_like(dk)
    dv[...] = jnp.zeros_like(dv)

    def products(left, right, chunks):
        for m in range(0, width, half):
            g = mm(left[m : m + half, :], right).astype(bf16)
            for c, (owner, chunk) in enumerate(chunks):
                for k in range(half // block):
                    at = place(m // block + k, own, owner, orders) * size + chunk * block
                    out[owner ^ core, pl.ds(pl.multiple_of(at, block), block), :] = g[
                        k * block : (k + 1) * block, c * half : (c + 1) * half
                    ]

    for c in c_first:
        c.wait()
    products(ctx, battn[...], ((0, 3), (1, 3)))
    for c in c_kv:
        c.wait()
    for q in range(kv.shape[0]):
        for g in range(quads):
            lanes = slice(g * QUAD, (g + 1) * QUAD)
            kt[q, lanes, :] = kv[q, :, lanes].T
    masks = lane_masks()
    steps = [(t, g, w) for t in range(slots // (2 * TILE)) for g in range(quads) for w in range(2)]
    kept = {}

    def place_of(i):
        t, g, w = steps[i]
        r0 = (2 * t + w) * TILE
        return r0, (r0 >= a0_scalar).astype(jnp.int32), slice(g * QUAD, (g + 1) * QUAD)

    def back_probs(i):
        t, g, w = steps[i]
        if g == 0 and w == 0:
            c_p[t].wait()
        r0, q, lanes = place_of(i)
        d4 = spread(bctx[r0 : r0 + TILE, lanes], masks)
        dp = mm_nt(kv[q, :, width + g * QUAD : width + (g + 1) * QUAD], d4)
        dv[q, :, lanes] += mm(prob[(2 * t + w) * quads + g], d4)
        return dp

    def back_scores(i, dp):
        t, g, w = steps[i]
        p = prob[(2 * t + w) * quads + g].astype(f32)
        weighted = p * dp
        return (weighted - p * colsum(weighted)).astype(bf16)

    def back_query_key(i, ds):
        t, g, w = steps[i]
        r0, q, lanes = place_of(i)
        dk[q, :, lanes] += mm(ds, spread(qs[r0 : r0 + TILE, lanes], masks))
        kept[w] = mm(kt[q, lanes, :], ds)
        if w == 1:
            for h in range(2):
                part = slice(128 * h, 128 * (h + 1))
                bqt[g * QUAD + 128 * h : g * QUAD + 128 * (h + 1), 128 * t : 128 * (t + 1)] = (
                    join_tiles(kept[0][part, part], kept[1][part, part]) * HEAD_DIM**-0.5
                ).astype(bf16)

    pipelined(len(steps), back_probs, back_scores, back_query_key)
    for q in range(kv.shape[0]):
        at = slice(q * LEN, (q + 1) * LEN)
        bkv[at, :width] = dk[q].astype(bf16)
        bkv[at, width:] = dv[q].astype(bf16)
    outs = [mover.start(bkv, bkv_h)]
    bq[...] = bqt[...].T
    for c in c_tok:
        c.wait()
    tokt[...] = tok[...].T
    short[...] = tokc[...].T
    products(short, bq[...], ((0, 0), (0, 1)))
    products(tokt, bkv[:, :width], ((0, 2), (1, 0)))
    products(tokt, bkv[:, width:], ((1, 1), (1, 2)))
    first_rows = small_a.shape[1] // half
    small[...] = jnp.zeros_like(small)
    for i in range(first_rows):
        small[i : i + 1, :] = small_a[:, i * half : (i + 1) * half]
    for i, lanes in enumerate((slice(0, half), slice(half, width))):
        small[first_rows + i : first_rows + i + 1, :] = colsum(bq[:, lanes].astype(f32))
        small[first_rows + 2 + i : first_rows + 3 + i, :] = colsum(
            bkv[:, width + i * half : width + (i + 1) * half].astype(f32)
        )
    high = small[...].astype(bf16)
    low[:SMALL] = high
    low[SMALL:] = (small[...] - high.astype(f32)).astype(bf16)
    outs += [
        mover.start(out.at[1], send_h.at[: 4 * width, :]),
        mover.start(low, send_h.at[4 * width :, :]),
        mover.start(out.at[0], keep_h),
        mover.start(small, small_h),
    ]
    c_wq.wait()
    c_bpre.wait()
    rc[...] = (bpre[...] + mm_nt(bq[...], wq[...])).astype(bf16)
    outs.append(mover.start(rc, rc_h))
    for copy in outs:
        copy.wait()


def marked_backward(where, m8, tokens, w_qkv, a, pieces, orders):
    rows, width = tokens.shape
    half = width // 2
    outs = dict(
        bkv=((rows, 2 * width), bf16), rc=((SLOTS, width), bf16), keep=((4 * width, half), bf16),
        send=((4 * width + 2 * SMALL, half), bf16), small=((SMALL, half), f32),
    )
    ins = [a["bpre"], a["bctx"], a["p"], a["qs"], a["kv"], tokens, a["tokc"], a["ctx"], a["battn"]]
    scratch = [((width, width), bf16)] + [(v.shape, v.dtype) for v in ins]
    scratch += [
        ((rows // LEN, LEN, width), f32), ((rows // LEN, LEN, width), f32), ((width, SLOTS), bf16),
        ((SLOTS, width), bf16), outs["bkv"], outs["rc"], ((rows // LEN, width, LEN), bf16), ((width, rows), bf16),
        ((width, SLOTS), bf16), ((2, 4 * width, half), bf16), outs["small"], ((2 * SMALL, half), bf16),
    ]
    vmem = pl.BlockSpec(memory_space=pltpu.VMEM)
    smem = pl.BlockSpec(memory_space=pltpu.SMEM)
    hbm = pl.BlockSpec(memory_space=pl.ANY)
    res = pl.pallas_call(
        functools.partial(marked_backward_kernel, pieces=pieces, orders=orders),
        out_shape=[jax.ShapeDtypeStruct(*o) for o in outs.values()],
        in_specs=[smem, vmem, vmem] + [hbm] * 10,
        out_specs=[hbm] * 5,
        scratch_shapes=[pltpu.VMEM(*s) for s in scratch] + [pltpu.SemaphoreType.DMA((24,))],
        compiler_params=params(60),
        cost_estimate=COST,
        name="marked_backward",
    )(where, m8, a["small"], w_qkv, *ins)
    return dict(zip(outs, res))


def attention_rows_kernel(
    which, bq_ref, bo_ref, g1_ref, s1_ref, tok_h, kv_h, wqkv_h, wout_h, hidden_h,
    tok, kv, wq, wout, q, ctx, hidden, vt, sems,
):
    width = wq.shape[1]
    quads = width // QUAD
    tile = 128
    mover = Mover(sems)
    i = which[0]
    r0 = pl.multiple_of(i * LEN, LEN)
    c_tok = mover.start(tok_h.at[pl.ds(r0, LEN), :], tok)
    c_wq = mover.start(wqkv_h.at[:, :width], wq)
    c_kv = mover.start(kv_h.at[i], kv)
    c_wout = mover.start(wout_h, wout)
    c_tok.wait()
    c_wq.wait()
    q[...] = ((mm(tok[...], wq[...]) + bq_ref[...]).astype(bf16).astype(f32) * HEAD_DIM**-0.5).astype(bf16)
    c_kv.wait()
    for g in range(quads):
        vt[g * QUAD : (g + 1) * QUAD, :] = kv[:, width + g * QUAD : width + (g + 1) * QUAD].T
    masks = lane_masks()
    steps = [(t, g) for t in range(LEN // tile) for g in range(quads)]

    def scores(i):
        t, g = steps[i]
        lanes = slice(g * QUAD, (g + 1) * QUAD)
        return mm_nt(kv[:, lanes], spread(q[t * tile : (t + 1) * tile, lanes], masks))

    def probabilities(i, s):
        e, inv = softmax_columns(s)
        return e.astype(bf16), inv

    def values(i, parts):
        t, g = steps[i]
        p, inv = parts
        for h in range(2):
            at = g * QUAD + 128 * h
            z = mm(vt[at : at + 128, :], p[:, h * 2 * tile : (h + 1) * 2 * tile])
            for u in range(2):
                tokens = slice((2 * h + u) * tile, (2 * h + u + 1) * tile)
                ctx[at + u * HEAD_DIM : at + (u + 1) * HEAD_DIM, t * tile : (t + 1) * tile] = (
                    z[u * HEAD_DIM : (u + 1) * HEAD_DIM, u * tile : (u + 1) * tile] * inv[:, tokens]
                ).astype(bf16)

    pipelined(len(steps), scores, probabilities, values)
    c_wout.wait()
    nh, _ = norm_parts(mm(ctx[...].T, wout[...]) + bo_ref[...] + tok[...].astype(f32))
    hid = nh * g1_ref[...] + s1_ref[...]
    hidden[...] = hid
    mover.start(hidden, hidden_h).wait()


def attention_rows(which, tokens, kv, w_qkv, b_query, w_out, b_out, g1, s1):
    width = tokens.shape[1]
    vmem = pl.BlockSpec(memory_space=pltpu.VMEM)
    smem = pl.BlockSpec(memory_space=pltpu.SMEM)
    hbm = pl.BlockSpec(memory_space=pl.ANY)
    scratch = [
        ((LEN, width), bf16), ((LEN, 2 * width), bf16), ((width, width), bf16), (w_out.shape, bf16),
        ((LEN, width), bf16), ((width, LEN), bf16), ((LEN, width), f32), ((width, LEN), bf16),
    ]
    return pl.pallas_call(
        attention_rows_kernel,
        out_shape=jax.ShapeDtypeStruct((LEN, width), f32),
        in_specs=[smem] + [vmem] * 4 + [hbm] * 4,
        out_specs=hbm,
        scratch_shapes=[pltpu.VMEM(*s) for s in scratch] + [pltpu.SemaphoreType.DMA((8,))],
        compiler_params=params(14),
        cost_estimate=COST,
        name="attention_rows",
    )(jnp.full((1,), which, jnp.int32), b_query, b_out, g1, s1, tokens, kv, w_qkv, w_out)


def ffn_rows_kernel(
    which, bi_ref, bb_ref, g2_ref, s2_ref, hidden_h, win_h, wback_h, *rest,
):
    (out_h, win, wback, hl, hidden, act, branch, out, bi, sems) = rest[-10:]
    width, ff = win.shape
    mover = Mover(sems)
    r0 = pl.multiple_of(which[0] * LEN, LEN)
    c_hidden = mover.start(hidden_h, hidden)
    part = ff // 4
    c_win = [mover.start(win_h.at[:, k : k + part], win.at[:, k : k + part]) for k in range(0, ff, part)]
    c_wback = mover.start(wback_h, wback)
    bi[...] = bi_ref[...].reshape(bi.shape)
    c_hidden.wait()
    hl[...] = hidden[...].astype(bf16)
    steps = [(j, m) for j in range(0, ff, 256) for m in range(0, LEN, ROWS)]

    def inner(i):
        j, m = steps[i]
        if j % part == 0 and m == 0:
            c_win[j // part].wait()
        return mm(hl[m : m + ROWS, :], win[:, j : j + 256])

    def gelu(i, v):
        j, m = steps[i]
        v = v + bi[:, j : j + 256]
        h = v * 0.5
        act[m : m + ROWS, j : j + 256] = (h + h * erf_of(v)).astype(bf16)

    pipelined(len(steps), inner, gelu, nothing)
    c_wback.wait()
    for m in range(0, LEN, 256):
        for k in range(0, width, 256):
            branch[m : m + 256, k : k + 256] = mm(act[m : m + 256, :], wback[:, k : k + 256])
    nh2, _ = norm_parts(hidden[...] + branch[...] + bb_ref[...])
    out[...] = (nh2 * g2_ref[...] + s2_ref[...]).astype(bf16)
    mover.start(out, out_h.at[pl.ds(r0, LEN), :]).wait()


def ffn_rows(which, previous, rows, hidden, w_in, b_in, w_back, b_back, g2, s2):
    width, ff = w_in.shape
    vmem = pl.BlockSpec(memory_space=pltpu.VMEM)
    smem = pl.BlockSpec(memory_space=pltpu.SMEM)
    hbm = pl.BlockSpec(memory_space=pl.ANY)
    scratch = [
        (w_in.shape, bf16), (w_back.shape, bf16), ((LEN, width), bf16), ((LEN, width), f32), ((LEN, ff), bf16),
        ((LEN, width), f32), ((LEN, width), bf16), ((1, ff), f32),
    ]
    extra = () if previous is None else (previous,)
    return pl.pallas_call(
        ffn_rows_kernel,
        out_shape=jax.ShapeDtypeStruct((rows, width), bf16),
        in_specs=[smem] + [vmem] * 4 + [hbm] * (3 + len(extra)),
        out_specs=hbm,
        scratch_shapes=[pltpu.VMEM(*s) for s in scratch] + [pltpu.SemaphoreType.DMA((12,))],
        input_output_aliases={8: 0} if extra else {},
        compiler_params=params(22),
        cost_estimate=COST,
        name="ffn_rows",
    )(jnp.full((1,), which, jnp.int32), b_in, b_back, g2, s2, hidden, w_in, w_back, *extra)


def ffn_grads_kernel(
    where, act_h, hl_h, bbr_h, bin_h, x_h, keep1_h, send1_h, keep2_h, send2_h,
    act, hl, bbr, bin_, out1, out2, hlt, sems, *, pieces, orders,
):
    own, core = where[0], where[1]
    slots, ff = act_h.shape
    width = hl_h.shape[1]
    half = width // 2
    mover = Mover(sems)
    up, down = slice(0, slots), slice(slots, 2 * slots)
    mine = lambda n: pl.ds(pl.multiple_of(core * n, n), n)
    c2 = [
        mover.start(hl_h, hl.at[up, :]),
        mover.start(x_h.at[:, ff : ff + width], hl.at[down, :]),
    ]
    c_in = []
    for k in range(0, ff // 2, width):
        lanes = slice(k, k + width)
        there = pl.ds(pl.multiple_of(core * (ff // 2) + k, width), width)
        first = ff + width + half + k
        c_in.append(
            (
                mover.start(bin_h.at[:, there], bin_.at[up, lanes]),
                mover.start(x_h.at[:, first : first + width], bin_.at[down, lanes]),
            )
        )
    c1 = [
        mover.start(bbr_h.at[:, mine(half)], bbr.at[up, :]),
        mover.start(x_h.at[:, ff + width : ff + width + half], bbr.at[down, :]),
    ]
    c_act = []
    for k in range(0, ff, width):
        lanes = slice(k, k + width)
        c_act.append(
            (mover.start(act_h.at[:, lanes], act.at[up, lanes]), mover.start(x_h.at[:, lanes], act.at[down, lanes]))
        )
    size, block = ff // pieces, width // pieces
    for c in c2:
        c.wait()
    hlt[...] = hl[...].T
    for j in range(ff // 2 // width):
        for c in c_in[j]:
            c.wait()
        for m in range(0, width, TALL):
            g = mm(hlt[m : m + TALL, :], bin_[:, j * width : (j + 1) * width]).astype(bf16)
            for c in range(2):
                for k in range(TALL // block):
                    at = place(m // block + k, own, core, orders[1]) * size + (2 * j + c) * block
                    out2[pl.ds(pl.multiple_of(at, block), block), :] = g[
                        k * block : (k + 1) * block, c * half : (c + 1) * half
                    ]
    rows = ff // 2
    outs = [mover.start(out2.at[rows:, :], send2_h), mover.start(out2.at[:rows, :], keep2_h)]
    for c in c1:
        c.wait()
    for j in range(ff // half):
        if j % 2 == 0:
            for c in c_act[j // 2]:
                c.wait()
        g = mm_tn(act[:, j * half : (j + 1) * half], bbr[...]).astype(bf16)
        for k in range(half // size):
            at = place(j * (half // size) + k, own, core, orders[0]) * size
            out1[pl.ds(pl.multiple_of(at, size), size), :] = g[k * size : (k + 1) * size]
    outs += [mover.start(out1.at[rows:, :], send1_h), mover.start(out1.at[:rows, :], keep1_h)]
    for c in outs:
        c.wait()


def ffn_grads(where, a, x, pieces, orders):
    slots, ff = a["act"].shape
    width = a["hl"].shape[1]
    half = width // 2
    smem = pl.BlockSpec(memory_space=pltpu.SMEM)
    hbm = pl.BlockSpec(memory_space=pl.ANY)
    scratch = [
        (2 * slots, ff), (2 * slots, width), (2 * slots, half), (2 * slots, ff // 2), (ff, half), (ff, half),
        (width, 2 * slots),
    ]
    return pl.pallas_call(
        functools.partial(ffn_grads_kernel, pieces=pieces, orders=orders),
        out_shape=[jax.ShapeDtypeStruct((ff // 2, half), bf16)] * 4,
        in_specs=[smem] + [hbm] * 5,
        out_specs=[hbm] * 4,
        scratch_shapes=[pltpu.VMEM(s, bf16) for s in scratch] + [pltpu.SemaphoreType.DMA((24,))],
        compiler_params=params(20),
        cost_estimate=COST,
        name="ffn_grads",
    )(where, a["act"], a["hl"], a["bbr"], a["bin"], x)


def small_sums_kernel(small_ref, *outs):
    at = 0
    for out in outs:
        width = small_ref.shape[1]
        for i in range(out.shape[0] // width):
            out[i * width : (i + 1) * width] = small_ref[at, :]
            at += 1


def small_sums(small, sizes):
    vmem = pl.BlockSpec(memory_space=pltpu.VMEM)
    return pl.pallas_call(
        small_sums_kernel,
        out_shape=[jax.ShapeDtypeStruct((size,), f32) for size in sizes],
        in_specs=[vmem],
        out_specs=[vmem] * len(sizes),
        cost_estimate=COST,
        name="small_sums",
    )(small)


def add_low(a, b):
    return (a.astype(f32) + b.astype(f32)).astype(bf16)


def after(value, *others):
    return lax.optimization_barrier((value, others))[0]


def two_parts(v):
    high = lax.reduce_precision(v, 8, 7)
    return [high.astype(bf16), (v - high).astype(bf16)]


def one_part(v):
    return v[:SMALL].astype(f32) + v[SMALL:].astype(f32)


class Reduction:
    def __init__(self, keep, send, orders, n, small=None):
        self.keep, self.send, self.orders, self.n, self.small = keep, send, orders, n, small
        self.step = 0
        self.start()

    def start(self):
        pairs = [
            (2 * i + core, 2 * (i ^ (1 << self.orders[core][self.step])) + core)
            for i in range(self.n)
            for core in range(2)
        ]
        send = self.send
        if self.small is not None:
            send = jnp.concatenate([send] + two_parts(self.small))
        self.got = lax.ppermute(send, ("dp", "head"), pairs)

    def advance(self, *others):
        keep, got, small = self.keep, self.got, self.small
        if others:
            keep, got, small = after((keep, got, small), *others)
        self.step += 1
        rows = keep.shape[0]
        if small is not None:
            self.small = small + one_part(got[rows:])
            got = got[:rows]
        if self.step == len(self.orders[0]):
            self.share = keep.astype(f32) + got.astype(f32)
            return self.share
        m = rows // 2
        self.send = add_low(keep[m:], got[m:])
        self.start()
        self.keep = add_low(keep[:m], got[:m])
        return self.keep, self.send


def columns(share, count):
    rows = share.shape[0] // count
    return jnp.concatenate([share[i * rows : (i + 1) * rows] for i in range(count)], axis=1)


def body(
    tokens, w_qkv, b_query, b_value, w_out, b_out, gain_attn, shift_attn, w_in, b_in, w_back, b_back,
    gain_out, shift_out, grad_out, masked,
):
    rows, width = tokens.shape
    ff = w_in.shape[1]
    n = lax.axis_size("dp")
    core = lax.axis_index("head")
    steps = n.bit_length() - 1
    halving = n == 1 << steps and width // n % 16 == 0
    if halving:
        own = lax.axis_index("dp")
        rest = tuple(range(3, steps))
        plane_first = ((0, 1, 2) + rest, (1, 0, 2) + rest)
        line_first = ((2, 0, 1) + rest, (2, 1, 0) + rest)
        orders = [plane_first, line_first, plane_first]
        pieces = n
    else:
        own = jnp.int32(0)
        orders = [((3, 2, 1, 0),) * 2] * 3
        pieces = 16
    where = jnp.stack([own, core]).astype(jnp.int32)
    m8 = masked.reshape(-1, 128)
    swap_cores = lambda v: lax.ppermute(v, "head", [(0, 1), (1, 0)])

    a = marked_forward(
        core.reshape(1).astype(jnp.int32), m8, tokens, grad_out, w_qkv, b_query, b_value, w_out, b_out,
        gain_attn, shift_attn, w_in, b_in, w_back, b_back, gain_out,
    )
    x = swap_cores(a["xsend"])
    b = marked_backward(where, m8, tokens, w_qkv, a, pieces, orders[2])
    got3 = swap_cores(b["send"])
    keep1, send1, keep2, send2 = ffn_grads(after(where, b["rc"]), a, x, pieces, orders[:2])
    keep3, got3, small = after((b["keep"], got3, b["small"]), keep1)
    small = small + one_part(got3[4 * width :])
    m = 2 * width
    if halving:
        r1 = Reduction(keep1, send1, orders[0], n, small)
        r2 = Reduction(keep2, send2, orders[1], n)
        r3 = Reduction(
            add_low(keep3[:m], got3[:m]), add_low(keep3[m:], got3[m : 2 * m]), orders[2], n
        )
        done = r3.keep
    else:
        r1 = r2 = r3 = None
        both3 = done = add_low(keep3, got3[: 2 * m])

    def attention(which, done):
        return attention_rows(which, after(tokens, done), a["kv"], w_qkv, b_query, w_out, b_out, gain_attn, shift_attn)

    def ffn(which, previous, hidden, done):
        return ffn_rows(which, previous, rows, after(hidden, done), w_in, b_in, w_back, b_back, gain_out, shift_out)

    def turn(done, *chains):
        if halving:
            return tuple(chain.advance(done) for chain in chains)
        return done

    hidden = attention(0, done)
    done = turn(hidden, r1)
    layer_out = ffn(0, None, hidden, done)
    done = turn(layer_out, r1, r2)
    hidden = attention(1, done)
    done = turn(hidden, r3, r1, r2)
    layer_out = ffn(1, layer_out, hidden, done)
    done = turn(layer_out, r3, r1, r2)
    sel, wkv = after((a["sel"], w_qkv[:, width:]), done)
    grad_tokens = mm_tn(sel, b["rc"]) + mm_nt(b["bkv"], wkv)
    done = turn(grad_tokens, r3, r2)
    turn(done, r3)
    if halving:
        shares = [r1.share, r2.share, r3.share]
        small = r1.small
    else:
        total = lambda v: lax.psum_scatter(v, "dp", scatter_dimension=0, tiled=True).astype(f32)
        natural = lambda v, count: columns_of_blocks(v, count, pieces)
        small = lax.psum(small, "dp")
        shares = [
            total(jnp.concatenate([keep1, send1])),
            total(natural(jnp.concatenate([keep2, send2]), 4)),
            total(natural(both3, 4)),
        ]
    names = (("gain_out", width), ("shift_out", width), ("b_back", width), ("b_in", ff), ("b_out", width),
             ("gain_attn", width), ("shift_attn", width), ("b_query", width), ("b_value", width))
    sums = dict(zip([name for name, _ in names], small_sums(small, [size for _, size in names])))
    if halving:
        shares[1] = columns(shares[1], 4)
        shares[2] = columns(shares[2], 4)
    half3 = 3 * width // 2
    return (
        layer_out, grad_tokens, shares[2][:, :half3], sums["b_query"], sums["b_value"], shares[2][:, half3:],
        sums["b_out"], sums["gain_attn"], sums["shift_attn"], shares[1], sums["b_in"], shares[0],
        sums["b_back"], sums["gain_out"], sums["shift_out"],
    )


def columns_of_blocks(v, count, pieces):
    lanes = v.shape[1]
    v = v.reshape(pieces, count, -1, lanes)
    return jnp.moveaxis(v, 1, 2).reshape(-1, count * lanes)


def solution(mesh):
    rows = P(("dp", "head"), None)
    shard = P("dp", "head")
    return jax.shard_map(
        body,
        mesh=mesh,
        in_specs=(rows,) + (P(),) * 13 + (rows, P(("dp", "head"))),
        out_specs=(rows, rows, shard, P(), P(), shard, P(), P(), P(), shard, P(), shard, P(), P(), P()),
        check_vma=False,
    )
```

```python
import functools

import jax
import jax.numpy as jnp
from jax import lax
from jax.experimental import pallas as pl
from jax.experimental.pallas import tpu as pltpu
from jax.sharding import PartitionSpec as P

HEADS = 12
HEAD_DIM = 64
LEN = 512
CAP = 320
TALL = 384
ROWS = 256
SMALL = 32
TILE = 64
SLOTS = (CAP // TILE + 1) * TILE
QUAD = 4 * HEAD_DIM


def cost(flops):
    return pl.CostEstimate(flops=flops, bytes_accessed=1000, transcendentals=0)


epsilon = 1e-12
bf16 = jnp.bfloat16
f32 = jnp.float32


def params(mib):
    return pltpu.CompilerParams(vmem_limit_bytes=mib * 1024 * 1024)


def mm(a, b):
    return jnp.dot(a, b, preferred_element_type=f32)


def mm_nt(a, b):
    return lax.dot_general(a, b, (((1,), (1,)), ((), ())), preferred_element_type=f32)


def mm_tn(a, b):
    return lax.dot_general(a, b, (((0,), (0,)), ((), ())), preferred_element_type=f32)


def colsum(v):
    return jnp.sum(v, axis=0, keepdims=True)


def rowmean(v):
    return jnp.sum(v, axis=-1, keepdims=True) * (1.0 / v.shape[-1])


def norm_parts(v):
    centred = v - rowmean(v)
    r = lax.rsqrt(rowmean(centred * centred) + epsilon)
    return centred * r, r


def norm_back(cot, nhat, r, gain):
    e = cot * gain
    return r * (e - rowmean(e) - nhat * rowmean(e * nhat))


def erf_of(v):
    return lax.erf(v * 0.7071067811865476)


def lane_masks():
    head = lax.broadcasted_iota(jnp.int32, (1, QUAD), 1) // HEAD_DIM
    return [(head == j).astype(f32).astype(bf16) for j in range(4)]


def spread(x, masks):
    return jnp.concatenate([x * m for m in masks], axis=0)


def softmax_columns(scores):
    e = jnp.exp(scores - jnp.max(scores, axis=0, keepdims=True))
    return e, 1.0 / jnp.sum(e, axis=0, keepdims=True)


def join_tiles(first, second):
    low = lax.broadcasted_iota(jnp.int32, (HEAD_DIM, 2 * TILE), 1) < TILE
    top = jnp.where(low, first[:HEAD_DIM], pltpu.roll(second[:HEAD_DIM], TILE, 1))
    bottom = jnp.where(low, pltpu.roll(first[HEAD_DIM:], TILE, 1), second[HEAD_DIM:])
    return jnp.concatenate([top, bottom], axis=0)


def nothing(i, value):
    pass


def pipelined(count, early, middle, late):
    ahead = early(0)
    waiting = None
    for i in range(count):
        now, ahead = ahead, early(i + 1) if i + 1 < count else None
        if waiting is not None:
            late(i - 1, waiting)
        waiting = middle(i, now)
    late(count - 1, waiting)


class Mover:
    def __init__(self, sems):
        self.sems = sems
        self.count = 0

    def start(self, src, dst):
        copy = pltpu.make_async_copy(src, dst, self.sems.at[self.count])
        self.count += 1
        copy.start()
        return copy


def marked_forward_kernel(
    core_ref, m_ref, bq_ref, bv_ref, bo_ref, g1_ref, s1_ref, bi_ref, bb_ref, g2_ref,
    tok_h, gout_h, wqkv_h, wout_h, win_h, wback_h,
    sel_h, kv_h, tokc_h, qs_h, p_h, ctx_h, hl_h, act_h, bbr_h, bin_h, xsend_h, battn_h, bctx_h, bpre_h, small_ref,
    tok, gout, wqkv, wout, win, wback,
    sel, kv, tokc, gc, qs, prob, ctx, nhat, rr, hidden, hl, act, gp, branch, bbr, bin_, bv, bi, vt,
    battn, bctx, bpre,
    sems,
):
    rows, width = tok.shape
    ff = win.shape[1]
    quads = width // QUAD
    mover = Mover(sems)
    other = 1 - core_ref[0]
    c_tok = mover.start(tok_h, tok)
    c_wqkv = mover.start(wqkv_h, wqkv)
    c_gout = mover.start(gout_h, gout)
    c_wout = mover.start(wout_h, wout)
    c_win = mover.start(win_h, win)
    c_wback = mover.start(wback_h, wback)
    outs = []
    bv[...] = bv_ref[...].reshape(bv.shape)
    bi[...] = bi_ref[...].reshape(bi.shape)
    m8 = m_ref[...].astype(f32)
    groups = m8.shape[0]
    per_seq = LEN // 128
    tri = (
        lax.broadcasted_iota(jnp.int32, (128, 128), 0)
        <= lax.broadcasted_iota(jnp.int32, (128, 128), 1)
    ).astype(f32).astype(bf16)
    within = mm(m8.astype(bf16), tri)
    first = jnp.sum(m8[:per_seq], axis=(0, 1), keepdims=True)
    a0 = jnp.floor((first + (TILE - 1)) * (1.0 / TILE)) * TILE
    offset = jnp.zeros((1, 1), f32)
    slot_iota = lax.broadcasted_iota(jnp.int32, (SLOTS, 128), 0).astype(f32)
    for g in range(groups):
        if g == per_seq:
            offset = a0
        slot = jnp.where(m8[g : g + 1] > 0.0, offset + within[g : g + 1] - 1.0, -1.0)
        sel[:, 128 * g : 128 * (g + 1)] = (slot_iota == slot).astype(f32).astype(bf16)
        offset = offset + within[g : g + 1, 127:128]
    outs.append(mover.start(sel, sel_h))
    a0_scalar = jnp.sum(a0).astype(jnp.int32)

    c_tok.wait()
    tokc[...] = mm(sel[...], tok[...]).astype(bf16)
    outs.append(mover.start(tokc, tokc_h))
    c_wqkv.wait()
    for q in range(rows // LEN):
        for i in range(2 * width // QUAD):
            at = slice(i * QUAD, (i + 1) * QUAD)
            value = mm(tok[q * LEN : (q + 1) * LEN, :], wqkv[:, width + i * QUAD : width + (i + 1) * QUAD])
            if i >= quads:
                low = (value + bv[:, i * QUAD - width : (i + 1) * QUAD - width]).astype(bf16)
                vt[q, i * QUAD - width : (i + 1) * QUAD - width, :] = low.T
                kv[q, :, at] = low
            else:
                kv[q, :, at] = value.astype(bf16)
    outs.append(mover.start(kv, kv_h))
    qs[...] = (
        (mm(tokc[...], wqkv[:, :width]) + bq_ref[...]).astype(bf16).astype(f32) * HEAD_DIM**-0.5
    ).astype(bf16)
    outs.append(mover.start(qs, qs_h))

    masks = lane_masks()
    steps = [(t, g, w) for t in range(SLOTS // (2 * TILE)) for g in range(quads) for w in range(2)]
    kept = {}

    def place_of(i):
        t, g, w = steps[i]
        r0 = (2 * t + w) * TILE
        return r0, (r0 >= a0_scalar).astype(jnp.int32), slice(g * QUAD, (g + 1) * QUAD)

    def scores(i):
        r0, q, lanes = place_of(i)
        return mm_nt(kv[q, :, lanes], spread(qs[r0 : r0 + TILE, lanes], masks))

    def probabilities(i, s):
        t, g, w = steps[i]
        e, inv = softmax_columns(s)
        p = (e * inv).astype(bf16)
        prob[(2 * t + w) * quads + g] = p
        return p

    def values(i, p):
        t, g, w = steps[i]
        r0, q, lanes = place_of(i)
        kept[w] = mm(vt[q, lanes, :], p)
        if w == 1:
            for h in range(2):
                part = slice(128 * h, 128 * (h + 1))
                ctx[g * QUAD + 128 * h : g * QUAD + 128 * (h + 1), 128 * t : 128 * (t + 1)] = join_tiles(
                    kept[0][part, part], kept[1][part, part]
                ).astype(bf16)

    pipelined(len(steps), scores, probabilities, values)
    outs.append(mover.start(prob, p_h))
    outs.append(mover.start(ctx, ctx_h))
    c_wout.wait()
    pre = mm(ctx[...].T, wout[...]) + bo_ref[...] + tokc[...].astype(f32)
    nh, r = norm_parts(pre)
    nhat[...] = nh
    rr[...] = jnp.broadcast_to(r, rr.shape)
    hid = nh * g1_ref[...] + s1_ref[...]
    hidden[...] = hid
    hl[...] = hid.astype(bf16)
    outs.append(mover.start(hl, hl_h))
    outs.append(mover.start(hl, xsend_h.at[:, ff : ff + width]))
    c_gout.wait()
    gc[...] = mm(sel[...], gout[...]).astype(bf16)
    c_win.wait()

    c_wback.wait()
    steps = [(j, m) for j in range(0, ff, 256) for m in range(0, SLOTS, SLOTS)]

    def inner(i):
        j, m = steps[i]
        return mm(hl[m : m + SLOTS, :], win[:, j : j + 256])

    def gelu(i, v):
        j, m = steps[i]
        v = v + bi[:, j : j + 256]
        cdf = 0.5 + 0.5 * erf_of(v)
        act[m : m + SLOTS, j : j + 256] = (v * cdf).astype(bf16)
        phi = jnp.exp2(v * v * (-0.5 * 1.4426950408889634)) * 0.3989422804014327
        gp[m : m + SLOTS, j : j + 256] = cdf + v * phi

    pipelined(len(steps), inner, gelu, nothing)
    outs.append(mover.start(act, act_h))
    outs.append(mover.start(act, xsend_h.at[:, :ff]))
    for m in range(0, SLOTS, SLOTS):
        for k in range(0, width, 256):
            branch[m : m + SLOTS, k : k + 256] = mm(act[m : m + SLOTS, :], wback[:, k : k + 256])
    nh2, r2 = norm_parts(hidden[...] + branch[...] + bb_ref[...])
    cot = gc[...].astype(f32)
    bs = norm_back(cot, nh2, r2, g2_ref[...])
    bl = bs.astype(bf16)
    bbr[...] = bl
    outs.append(mover.start(bbr, bbr_h))
    half = width // 2
    outs.append(
        mover.start(
            bbr.at[:, pl.ds(pl.multiple_of(other * half, half), half)],
            xsend_h.at[:, ff + width : ff + width + half],
        )
    )
    small_ref[:, :width] = colsum(cot * nh2)
    small_ref[:, width : 2 * width] = colsum(cot)
    small_ref[:, 2 * width : 3 * width] = colsum(bl.astype(f32))

    branch[...] = bs

    def back_active(i):
        j, m = steps[i]
        return mm_nt(bbr[m : m + SLOTS, :], wback[j : j + 256, :])

    def back_gelu(i, v):
        j, m = steps[i]
        b = (v * gp[m : m + SLOTS, j : j + 256]).astype(bf16)
        bin_[m : m + SLOTS, j : j + 256] = b
        part = colsum(b.astype(f32))
        at = slice(3 * width + j, 3 * width + j + 256)
        small_ref[:, at] = part if m == 0 else small_ref[:, at] + part

    pipelined(len(steps), back_active, back_gelu, nothing)
    outs.append(mover.start(bin_, bin_h))
    outs.append(
        mover.start(
            bin_.at[:, pl.ds(pl.multiple_of(other * (ff // 2), ff // 2), ff // 2)],
            xsend_h.at[:, ff + width + half :],
        )
    )
    for m in range(0, SLOTS, SLOTS):
        for k in range(0, width, 256):
            branch[m : m + SLOTS, k : k + 256] += mm_nt(bin_[m : m + SLOTS, :], win[k : k + 256, :])
    back_hidden = branch[...]
    nh = nhat[...]
    bp = norm_back(back_hidden, nh, rr[:, :1], g1_ref[...])
    bpre[...] = bp
    outs.append(mover.start(bpre, bpre_h))
    bl = bp.astype(bf16)
    battn[...] = bl
    outs.append(mover.start(battn, battn_h))
    bctx[...] = mm_nt(bl, wout[...]).astype(bf16)
    outs.append(mover.start(bctx, bctx_h))
    at = 3 * width + ff
    small_ref[:, at : at + width] = colsum(bl.astype(f32))
    small_ref[:, at + width : at + 2 * width] = colsum(back_hidden * nh)
    small_ref[:, at + 2 * width : at + 3 * width] = colsum(back_hidden)
    for copy in outs:
        copy.wait()


def marked_forward(core, m8, tokens, gout, w_qkv, b_query, b_value, w_out, b_out, g1, s1, w_in, b_in, w_back, b_back, g2):
    rows, width = tokens.shape
    ff = w_in.shape[1]
    tiles = SLOTS // TILE * (width // QUAD)
    outs = dict(
        sel=((SLOTS, rows), bf16), kv=((rows // LEN, LEN, 2 * width), bf16), tokc=((SLOTS, width), bf16),
        qs=((SLOTS, width), bf16), p=((tiles, LEN, 4 * TILE), bf16), ctx=((width, SLOTS), bf16),
        hl=((SLOTS, width), bf16),
        act=((SLOTS, ff), bf16), bbr=((SLOTS, width), bf16), bin=((SLOTS, ff), bf16),
        xsend=((SLOTS, (ff + width) * 3 // 2), bf16), battn=((SLOTS, width), bf16), bctx=((SLOTS, width), bf16),
        bpre=((SLOTS, width), f32), small=((1, 6 * width + ff), f32),
    )
    scratch = [
        ((rows, width), bf16), ((rows, width), bf16), (w_qkv.shape, bf16), (w_out.shape, bf16),
        (w_in.shape, bf16), (w_back.shape, bf16),
        outs["sel"], outs["kv"], outs["tokc"], ((SLOTS, width), bf16), outs["qs"], outs["p"], outs["ctx"],
        ((SLOTS, width), f32), ((SLOTS, 128), f32), ((SLOTS, width), f32), outs["hl"], outs["act"], ((SLOTS, ff), f32),
        ((SLOTS, width), f32), outs["bbr"], outs["bin"], ((1, width), f32), ((1, ff), f32),
        ((rows // LEN, width, LEN), bf16), outs["battn"], outs["bctx"], outs["bpre"],
    ]
    vmem = pl.BlockSpec(memory_space=pltpu.VMEM)
    smem = pl.BlockSpec(memory_space=pltpu.SMEM)
    hbm = pl.BlockSpec(memory_space=pl.ANY)
    res = pl.pallas_call(
        marked_forward_kernel,
        out_shape=[jax.ShapeDtypeStruct(*o) for o in outs.values()],
        in_specs=[smem] + [vmem] * 9 + [hbm] * 6,
        out_specs=[hbm] * 14 + [vmem],
        scratch_shapes=[pltpu.VMEM(*s) for s in scratch] + [pltpu.SemaphoreType.DMA((32,))],
        compiler_params=params(60),
        cost_estimate=cost(14375000000),
        name="marked_forward",
    )(core, m8, b_query, b_value, b_out, g1, s1, b_in, b_back, g2,
      tokens, gout, w_qkv, w_out, w_in, w_back)
    return dict(zip(outs, res))


def place(piece, own, core, orders):
    bits = piece ^ own
    spots = []
    for order in orders:
        spot = 0
        for step in order:
            spot = spot * 2 + ((bits >> step) & 1)
        spots.append(spot)
    return spots[core] if isinstance(core, int) else spots[0] + core * (spots[1] - spots[0])


def marked_backward_kernel(
    where, m_ref, small_a, wqkv_h, bpre_h, bctx_h, p_h, qs_h, kv_h, tok_h, tokc_h, ctx_h, battn_h,
    bkv_h, rc_h, keep_h, send_h, small_h,
    wq, bpre, bctx, prob, qs, kv, tok, tokc, ctx, battn, dk, dv, bqt, bq, bkv, rc, kt, tokt, short, out, small, low,
    sems, *, pieces, orders,
):
    slots, width = qs.shape
    rows = tok.shape[0]
    quads = width // QUAD
    half = width // 2
    own, core = where[0], where[1]
    block = width // pieces
    size = 4 * block
    mover = Mover(sems)
    c_first = [mover.start(ctx_h, ctx), mover.start(battn_h, battn)]
    c_kv = [mover.start(kv_h, kv), mover.start(bctx_h, bctx), mover.start(qs_h, qs)]
    group = 2 * quads
    c_p = [
        mover.start(p_h.at[i : i + group], prob.at[i : i + group]) for i in range(0, prob.shape[0], group)
    ]
    c_tok = [mover.start(tok_h, tok), mover.start(tokc_h, tokc)]
    c_wq = mover.start(wqkv_h.at[:, :width], wq)
    c_bpre = mover.start(bpre_h, bpre)
    per_seq = LEN // 128
    first = jnp.sum(m_ref[:per_seq].astype(f32), axis=(0, 1), keepdims=True)
    a0_scalar = jnp.sum(jnp.floor((first + (TILE - 1)) * (1.0 / TILE)) * TILE).astype(jnp.int32)
    dk[...] = jnp.zeros_like(dk)
    dv[...] = jnp.zeros_like(dv)

    def products(left, right, chunks):
        for m in range(0, width, half):
            g = mm(left[m : m + half, :], right).astype(bf16)
            for c, (owner, chunk) in enumerate(chunks):
                for k in range(half // block):
                    at = place(m // block + k, own, owner, orders) * size + chunk * block
                    out[owner ^ core, pl.ds(pl.multiple_of(at, block), block), :] = g[
                        k * block : (k + 1) * block, c * half : (c + 1) * half
                    ]

    for c in c_first:
        c.wait()
    products(ctx, battn[...], ((0, 3), (1, 3)))
    for c in c_kv:
        c.wait()
    for q in range(kv.shape[0]):
        for g in range(quads):
            lanes = slice(g * QUAD, (g + 1) * QUAD)
            kt[q, lanes, :] = kv[q, :, lanes].T
    masks = lane_masks()
    steps = [(t, g, w) for t in range(slots // (2 * TILE)) for g in range(quads) for w in range(2)]
    kept = {}

    def place_of(i):
        t, g, w = steps[i]
        r0 = (2 * t + w) * TILE
        return r0, (r0 >= a0_scalar).astype(jnp.int32), slice(g * QUAD, (g + 1) * QUAD)

    def back_probs(i):
        t, g, w = steps[i]
        if g == 0 and w == 0:
            c_p[t].wait()
        r0, q, lanes = place_of(i)
        d4 = spread(bctx[r0 : r0 + TILE, lanes], masks)
        dp = mm_nt(kv[q, :, width + g * QUAD : width + (g + 1) * QUAD], d4)
        dv[q, :, lanes] += mm(prob[(2 * t + w) * quads + g], d4)
        return dp

    def back_scores(i, dp):
        t, g, w = steps[i]
        p = prob[(2 * t + w) * quads + g].astype(f32)
        weighted = p * dp
        return (weighted - p * colsum(weighted)).astype(bf16)

    def back_query_key(i, ds):
        t, g, w = steps[i]
        r0, q, lanes = place_of(i)
        dk[q, :, lanes] += mm(ds, spread(qs[r0 : r0 + TILE, lanes], masks))
        kept[w] = mm(kt[q, lanes, :], ds)
        if w == 1:
            for h in range(2):
                part = slice(128 * h, 128 * (h + 1))
                bqt[g * QUAD + 128 * h : g * QUAD + 128 * (h + 1), 128 * t : 128 * (t + 1)] = (
                    join_tiles(kept[0][part, part], kept[1][part, part]) * HEAD_DIM**-0.5
                ).astype(bf16)

    pipelined(len(steps), back_probs, back_scores, back_query_key)
    for q in range(kv.shape[0]):
        at = slice(q * LEN, (q + 1) * LEN)
        bkv[at, :width] = dk[q].astype(bf16)
        bkv[at, width:] = dv[q].astype(bf16)
    outs = [mover.start(bkv, bkv_h)]
    bq[...] = bqt[...].T
    for c in c_tok:
        c.wait()
    tokt[...] = tok[...].T
    short[...] = tokc[...].T
    products(short, bq[...], ((0, 0), (0, 1)))
    products(tokt, bkv[:, :width], ((0, 2), (1, 0)))
    products(tokt, bkv[:, width:], ((1, 1), (1, 2)))
    first_rows = small_a.shape[1] // half
    small[...] = jnp.zeros_like(small)
    for i in range(first_rows):
        small[i : i + 1, :] = small_a[:, i * half : (i + 1) * half]
    for i, lanes in enumerate((slice(0, half), slice(half, width))):
        small[first_rows + i : first_rows + i + 1, :] = colsum(bq[:, lanes].astype(f32))
        small[first_rows + 2 + i : first_rows + 3 + i, :] = colsum(
            bkv[:, width + i * half : width + (i + 1) * half].astype(f32)
        )
    high = small[...].astype(bf16)
    low[:SMALL] = high
    low[SMALL:] = (small[...] - high.astype(f32)).astype(bf16)
    outs += [
        mover.start(out.at[1], send_h.at[: 4 * width, :]),
        mover.start(low, send_h.at[4 * width :, :]),
        mover.start(out.at[0], keep_h),
        mover.start(small, small_h),
    ]
    c_wq.wait()
    c_bpre.wait()
    rc[...] = (bpre[...] + mm_nt(bq[...], wq[...])).astype(bf16)
    outs.append(mover.start(rc, rc_h))
    for copy in outs:
        copy.wait()


def marked_backward(where, m8, tokens, w_qkv, a, pieces, orders):
    rows, width = tokens.shape
    half = width // 2
    outs = dict(
        bkv=((rows, 2 * width), bf16), rc=((SLOTS, width), bf16), keep=((4 * width, half), bf16),
        send=((4 * width + 2 * SMALL, half), bf16), small=((SMALL, half), f32),
    )
    ins = [a["bpre"], a["bctx"], a["p"], a["qs"], a["kv"], tokens, a["tokc"], a["ctx"], a["battn"]]
    scratch = [((width, width), bf16)] + [(v.shape, v.dtype) for v in ins]
    scratch += [
        ((rows // LEN, LEN, width), f32), ((rows // LEN, LEN, width), f32), ((width, SLOTS), bf16),
        ((SLOTS, width), bf16), outs["bkv"], outs["rc"], ((rows // LEN, width, LEN), bf16), ((width, rows), bf16),
        ((width, SLOTS), bf16), ((2, 4 * width, half), bf16), outs["small"], ((2 * SMALL, half), bf16),
    ]
    vmem = pl.BlockSpec(memory_space=pltpu.VMEM)
    smem = pl.BlockSpec(memory_space=pltpu.SMEM)
    hbm = pl.BlockSpec(memory_space=pl.ANY)
    res = pl.pallas_call(
        functools.partial(marked_backward_kernel, pieces=pieces, orders=orders),
        out_shape=[jax.ShapeDtypeStruct(*o) for o in outs.values()],
        in_specs=[smem, vmem, vmem] + [hbm] * 10,
        out_specs=[hbm] * 5,
        scratch_shapes=[pltpu.VMEM(*s) for s in scratch] + [pltpu.SemaphoreType.DMA((24,))],
        compiler_params=params(60),
        cost_estimate=cost(9775000000),
        name="marked_backward",
    )(where, m8, a["small"], w_qkv, *ins)
    return dict(zip(outs, res))


def attention_rows_kernel(
    which, bq_ref, bo_ref, g1_ref, s1_ref, tok_h, kv_h, wqkv_h, wout_h, hidden_h,
    tok, kv, wq, wout, q, ctx, hidden, vt, sems,
):
    width = wq.shape[1]
    quads = width // QUAD
    tile = 128
    mover = Mover(sems)
    i = which[0]
    r0 = pl.multiple_of(i * LEN, LEN)
    c_tok = mover.start(tok_h.at[pl.ds(r0, LEN), :], tok)
    c_wq = mover.start(wqkv_h.at[:, :width], wq)
    c_kv = mover.start(kv_h.at[i], kv)
    c_wout = mover.start(wout_h, wout)
    c_tok.wait()
    c_wq.wait()
    q[...] = ((mm(tok[...], wq[...]) + bq_ref[...]).astype(bf16).astype(f32) * HEAD_DIM**-0.5).astype(bf16)
    c_kv.wait()
    for g in range(quads):
        vt[g * QUAD : (g + 1) * QUAD, :] = kv[:, width + g * QUAD : width + (g + 1) * QUAD].T
    masks = lane_masks()
    steps = [(t, g) for t in range(LEN // tile) for g in range(quads)]

    def scores(i):
        t, g = steps[i]
        lanes = slice(g * QUAD, (g + 1) * QUAD)
        return mm_nt(kv[:, lanes], spread(q[t * tile : (t + 1) * tile, lanes], masks))

    def probabilities(i, s):
        e, inv = softmax_columns(s)
        return e.astype(bf16), inv

    def values(i, parts):
        t, g = steps[i]
        p, inv = parts
        for h in range(2):
            at = g * QUAD + 128 * h
            z = mm(vt[at : at + 128, :], p[:, h * 2 * tile : (h + 1) * 2 * tile])
            for u in range(2):
                tokens = slice((2 * h + u) * tile, (2 * h + u + 1) * tile)
                ctx[at + u * HEAD_DIM : at + (u + 1) * HEAD_DIM, t * tile : (t + 1) * tile] = (
                    z[u * HEAD_DIM : (u + 1) * HEAD_DIM, u * tile : (u + 1) * tile] * inv[:, tokens]
                ).astype(bf16)

    pipelined(len(steps), scores, probabilities, values)
    c_wout.wait()
    nh, _ = norm_parts(mm(ctx[...].T, wout[...]) + bo_ref[...] + tok[...].astype(f32))
    hid = nh * g1_ref[...] + s1_ref[...]
    hidden[...] = hid
    mover.start(hidden, hidden_h).wait()


def attention_rows(which, tokens, kv, w_qkv, b_query, w_out, b_out, g1, s1):
    width = tokens.shape[1]
    vmem = pl.BlockSpec(memory_space=pltpu.VMEM)
    smem = pl.BlockSpec(memory_space=pltpu.SMEM)
    hbm = pl.BlockSpec(memory_space=pl.ANY)
    scratch = [
        ((LEN, width), bf16), ((LEN, 2 * width), bf16), ((width, width), bf16), (w_out.shape, bf16),
        ((LEN, width), bf16), ((width, LEN), bf16), ((LEN, width), f32), ((width, LEN), bf16),
    ]
    return pl.pallas_call(
        attention_rows_kernel,
        out_shape=jax.ShapeDtypeStruct((LEN, width), f32),
        in_specs=[smem] + [vmem] * 4 + [hbm] * 4,
        out_specs=hbm,
        scratch_shapes=[pltpu.VMEM(*s) for s in scratch] + [pltpu.SemaphoreType.DMA((8,))],
        compiler_params=params(14),
        cost_estimate=cost(4025000000),
        name="attention_rows",
    )(jnp.full((1,), which, jnp.int32), b_query, b_out, g1, s1, tokens, kv, w_qkv, w_out)


def ffn_rows_kernel(
    which, bi_ref, bb_ref, g2_ref, s2_ref, hidden_h, win_h, wback_h, *rest,
):
    (out_h, win, wback, hl, hidden, act, branch, out, bi, sems) = rest[-10:]
    width, ff = win.shape
    mover = Mover(sems)
    r0 = pl.multiple_of(which[0] * LEN, LEN)
    c_hidden = mover.start(hidden_h, hidden)
    part = ff // 4
    c_win = [mover.start(win_h.at[:, k : k + part], win.at[:, k : k + part]) for k in range(0, ff, part)]
    c_wback = mover.start(wback_h, wback)
    bi[...] = bi_ref[...].reshape(bi.shape)
    c_hidden.wait()
    hl[...] = hidden[...].astype(bf16)
    steps = [(j, m) for j in range(0, ff, 256) for m in range(0, LEN, ROWS)]

    def inner(i):
        j, m = steps[i]
        if j % part == 0 and m == 0:
            c_win[j // part].wait()
        return mm(hl[m : m + ROWS, :], win[:, j : j + 256])

    def gelu(i, v):
        j, m = steps[i]
        v = v + bi[:, j : j + 256]
        h = v * 0.5
        act[m : m + ROWS, j : j + 256] = (h + h * erf_of(v)).astype(bf16)

    pipelined(len(steps), inner, gelu, nothing)
    c_wback.wait()
    for m in range(0, LEN, 256):
        for k in range(0, width, 256):
            branch[m : m + 256, k : k + 256] = mm(act[m : m + 256, :], wback[:, k : k + 256])
    nh2, _ = norm_parts(hidden[...] + branch[...] + bb_ref[...])
    out[...] = (nh2 * g2_ref[...] + s2_ref[...]).astype(bf16)
    mover.start(out, out_h.at[pl.ds(r0, LEN), :]).wait()


def ffn_rows(which, previous, rows, hidden, w_in, b_in, w_back, b_back, g2, s2):
    width, ff = w_in.shape
    vmem = pl.BlockSpec(memory_space=pltpu.VMEM)
    smem = pl.BlockSpec(memory_space=pltpu.SMEM)
    hbm = pl.BlockSpec(memory_space=pl.ANY)
    scratch = [
        (w_in.shape, bf16), (w_back.shape, bf16), ((LEN, width), bf16), ((LEN, width), f32), ((LEN, ff), bf16),
        ((LEN, width), f32), ((LEN, width), bf16), ((1, ff), f32),
    ]
    extra = () if previous is None else (previous,)
    return pl.pallas_call(
        ffn_rows_kernel,
        out_shape=jax.ShapeDtypeStruct((rows, width), bf16),
        in_specs=[smem] + [vmem] * 4 + [hbm] * (3 + len(extra)),
        out_specs=hbm,
        scratch_shapes=[pltpu.VMEM(*s) for s in scratch] + [pltpu.SemaphoreType.DMA((12,))],
        input_output_aliases={8: 0} if extra else {},
        compiler_params=params(22),
        cost_estimate=cost(5175000000),
        name="ffn_rows",
    )(jnp.full((1,), which, jnp.int32), b_in, b_back, g2, s2, hidden, w_in, w_back, *extra)


def ffn_grads_kernel(
    where, act_h, hl_h, bbr_h, bin_h, x_h, keep1_h, send1_h, keep2_h, send2_h,
    act, hl, bbr, bin_, out1, out2, hlt, sems, *, pieces, orders,
):
    own, core = where[0], where[1]
    slots, ff = act_h.shape
    width = hl_h.shape[1]
    half = width // 2
    mover = Mover(sems)
    up, down = slice(0, slots), slice(slots, 2 * slots)
    mine = lambda n: pl.ds(pl.multiple_of(core * n, n), n)
    c2 = [
        mover.start(hl_h, hl.at[up, :]),
        mover.start(x_h.at[:, ff : ff + width], hl.at[down, :]),
    ]
    c_in = []
    for k in range(0, ff // 2, width):
        lanes = slice(k, k + width)
        there = pl.ds(pl.multiple_of(core * (ff // 2) + k, width), width)
        first = ff + width + half + k
        c_in.append(
            (
                mover.start(bin_h.at[:, there], bin_.at[up, lanes]),
                mover.start(x_h.at[:, first : first + width], bin_.at[down, lanes]),
            )
        )
    c1 = [
        mover.start(bbr_h.at[:, mine(half)], bbr.at[up, :]),
        mover.start(x_h.at[:, ff + width : ff + width + half], bbr.at[down, :]),
    ]
    c_act = []
    for k in range(0, ff, width):
        lanes = slice(k, k + width)
        c_act.append(
            (mover.start(act_h.at[:, lanes], act.at[up, lanes]), mover.start(x_h.at[:, lanes], act.at[down, lanes]))
        )
    size, block = ff // pieces, width // pieces
    for c in c2:
        c.wait()
    hlt[...] = hl[...].T
    for j in range(ff // 2 // width):
        for c in c_in[j]:
            c.wait()
        for m in range(0, width, TALL):
            g = mm(hlt[m : m + TALL, :], bin_[:, j * width : (j + 1) * width]).astype(bf16)
            for c in range(2):
                for k in range(TALL // block):
                    at = place(m // block + k, own, core, orders[1]) * size + (2 * j + c) * block
                    out2[pl.ds(pl.multiple_of(at, block), block), :] = g[
                        k * block : (k + 1) * block, c * half : (c + 1) * half
                    ]
    rows = ff // 2
    outs = [mover.start(out2.at[rows:, :], send2_h), mover.start(out2.at[:rows, :], keep2_h)]
    for c in c1:
        c.wait()
    for j in range(ff // half):
        if j % 2 == 0:
            for c in c_act[j // 2]:
                c.wait()
        g = mm_tn(act[:, j * half : (j + 1) * half], bbr[...]).astype(bf16)
        for k in range(half // size):
            at = place(j * (half // size) + k, own, core, orders[0]) * size
            out1[pl.ds(pl.multiple_of(at, size), size), :] = g[k * size : (k + 1) * size]
    outs += [mover.start(out1.at[rows:, :], send1_h), mover.start(out1.at[:rows, :], keep1_h)]
    for c in outs:
        c.wait()


def ffn_grads(where, a, x, pieces, orders):
    slots, ff = a["act"].shape
    width = a["hl"].shape[1]
    half = width // 2
    smem = pl.BlockSpec(memory_space=pltpu.SMEM)
    hbm = pl.BlockSpec(memory_space=pl.ANY)
    scratch = [
        (2 * slots, ff), (2 * slots, width), (2 * slots, half), (2 * slots, ff // 2), (ff, half), (ff, half),
        (width, 2 * slots),
    ]
    return pl.pallas_call(
        functools.partial(ffn_grads_kernel, pieces=pieces, orders=orders),
        out_shape=[jax.ShapeDtypeStruct((ff // 2, half), bf16)] * 4,
        in_specs=[smem] + [hbm] * 5,
        out_specs=[hbm] * 4,
        scratch_shapes=[pltpu.VMEM(s, bf16) for s in scratch] + [pltpu.SemaphoreType.DMA((24,))],
        compiler_params=params(20),
        cost_estimate=cost(5175000000),
        name="ffn_grads",
    )(where, a["act"], a["hl"], a["bbr"], a["bin"], x)


def small_sums_kernel(small_ref, *outs):
    at = 0
    for out in outs:
        width = small_ref.shape[1]
        for i in range(out.shape[0] // width):
            out[i * width : (i + 1) * width] = small_ref[at, :]
            at += 1


def small_sums(small, sizes):
    vmem = pl.BlockSpec(memory_space=pltpu.VMEM)
    return pl.pallas_call(
        small_sums_kernel,
        out_shape=[jax.ShapeDtypeStruct((size,), f32) for size in sizes],
        in_specs=[vmem],
        out_specs=[vmem] * len(sizes),
        cost_estimate=cost(575000000),
        name="small_sums",
    )(small)


def add_low(a, b):
    return (a.astype(f32) + b.astype(f32)).astype(bf16)


def after(value, *others):
    return lax.optimization_barrier((value, others))[0]


def two_parts(v):
    high = lax.reduce_precision(v, 8, 7)
    return [high.astype(bf16), (v - high).astype(bf16)]


def one_part(v):
    return v[:SMALL].astype(f32) + v[SMALL:].astype(f32)


def total(parts, first, last):
    return sum(part[first:last].astype(f32) for part in parts)


class Reduction:
    def __init__(self, keep, send, orders, n, small=None):
        self.parts, self.send, self.orders, self.n, self.small = [keep], send, orders, n, small
        self.rows = keep.shape[0]
        self.step = 0
        self.start()

    def start(self):
        pairs = self.pairs()
        send = self.send
        if self.small is not None:
            send = jnp.concatenate([send] + two_parts(self.small))
        self.got = lax.ppermute(send, ("dp", "head"), pairs)

    def pairs(self):
        return [
            (2 * i + core, 2 * (i ^ (1 << self.orders[core][self.step])) + core)
            for i in range(self.n)
            for core in range(2)
        ]

    def advance(self, *others, go=True):
        parts, got, small = after((self.parts, self.got, self.small), *others)
        self.step += 1
        if small is not None:
            self.small = small + one_part(got[self.rows :])
        self.parts = parts + [got]
        if self.step == len(self.orders[0]):
            self.share = total(self.parts, 0, self.rows)
            return self.share
        self.rows //= 2
        self.send = total(self.parts, self.rows, 2 * self.rows).astype(bf16)
        if go:
            self.start()
        return self.send


def columns(share, count):
    rows = share.shape[0] // count
    return jnp.concatenate([share[i * rows : (i + 1) * rows] for i in range(count)], axis=1)


def body(
    tokens, w_qkv, b_query, b_value, w_out, b_out, gain_attn, shift_attn, w_in, b_in, w_back, b_back,
    gain_out, shift_out, grad_out, masked,
):
    rows, width = tokens.shape
    ff = w_in.shape[1]
    n = lax.axis_size("dp")
    core = lax.axis_index("head")
    steps = n.bit_length() - 1
    halving = n == 1 << steps and width // n % 16 == 0
    if halving:
        own = lax.axis_index("dp")
        rest = tuple(range(3, steps))
        plane_first = ((0, 1, 2) + rest, (1, 0, 2) + rest)
        line_first = ((2, 0, 1) + rest, (2, 1, 0) + rest)
        orders = [plane_first, line_first, plane_first]
        pieces = n
    else:
        own = jnp.int32(0)
        orders = [((3, 2, 1, 0),) * 2] * 3
        pieces = 16
    where = jnp.stack([own, core]).astype(jnp.int32)
    m8 = masked.reshape(-1, 128)
    swap_cores = lambda v: lax.ppermute(v, "head", [(0, 1), (1, 0)])

    a = marked_forward(
        core.reshape(1).astype(jnp.int32), m8, tokens, grad_out, w_qkv, b_query, b_value, w_out, b_out,
        gain_attn, shift_attn, w_in, b_in, w_back, b_back, gain_out,
    )
    x = swap_cores(a["xsend"])
    b = marked_backward(where, m8, tokens, w_qkv, a, pieces, orders[2])
    got3 = swap_cores(b["send"])
    keep1, send1, keep2, send2 = ffn_grads(after(where, b["rc"]), a, x, pieces, orders[:2])
    keep3, got3, small = after((b["keep"], got3, b["small"]), keep1)
    small = small + one_part(got3[4 * width :])
    m = 2 * width
    if halving:
        r1 = Reduction(keep1, send1, orders[0], n, small)
        r2 = Reduction(keep2, send2, orders[1], n)
        r3 = Reduction(
            add_low(keep3[:m], got3[:m]), add_low(keep3[m:], got3[m : 2 * m]), orders[2], n
        )
        done = r3.send
    else:
        r1 = r2 = r3 = None
        both3 = done = add_low(keep3, got3[: 2 * m])

    def attention(which, done):
        return attention_rows(which, after(tokens, done), a["kv"], w_qkv, b_query, w_out, b_out, gain_attn, shift_attn)

    def ffn(which, previous, hidden, done):
        return ffn_rows(which, previous, rows, after(hidden, done), w_in, b_in, w_back, b_back, gain_out, shift_out)

    def turn(done, *chains):
        if halving:
            sent = ()
            for chain in chains:
                sent += (chain.advance(done, *sent),)
            return sent
        return done

    hidden = attention(0, done)
    done = turn(hidden, r1)
    layer_out = ffn(0, None, hidden, done)
    done = turn(layer_out, r1, r2, r3)
    hidden = attention(1, done)
    done = turn(hidden, r1, r2, r3)
    layer_out = ffn(1, layer_out, hidden, done)
    if halving:
        done = (r2.advance(layer_out, go=False), r3.advance(layer_out, go=False))
        got = lax.ppermute(jnp.concatenate(done), ("dp", "head"), r2.pairs())
        r2.got, r3.got = got[: r2.rows], got[r2.rows :]
        done += (r1.advance(layer_out, *done),)
    else:
        done = (layer_out,)
    sel, wkv = after((a["sel"], w_qkv[:, width:]), done)
    grad_tokens = mm_tn(sel, b["rc"]) + mm_nt(b["bkv"], wkv)
    turn(grad_tokens, r2, r3)
    if halving:
        shares = [r1.share, r2.share, r3.share]
        small = r1.small
    else:
        spread_out = lambda v: lax.psum_scatter(v, "dp", scatter_dimension=0, tiled=True).astype(f32)
        natural = lambda v, count: columns_of_blocks(v, count, pieces)
        small = lax.psum(small, "dp")
        shares = [
            spread_out(jnp.concatenate([keep1, send1])),
            spread_out(natural(jnp.concatenate([keep2, send2]), 4)),
            spread_out(natural(both3, 4)),
        ]
    names = (("gain_out", width), ("shift_out", width), ("b_back", width), ("b_in", ff), ("b_out", width),
             ("gain_attn", width), ("shift_attn", width), ("b_query", width), ("b_value", width))
    sums = dict(zip([name for name, _ in names], small_sums(small, [size for _, size in names])))
    if halving:
        shares[1] = columns(shares[1], 4)
        shares[2] = columns(shares[2], 4)
    half3 = 3 * width // 2
    return (
        layer_out, grad_tokens, shares[2][:, :half3], sums["b_query"], sums["b_value"], shares[2][:, half3:],
        sums["b_out"], sums["gain_attn"], sums["shift_attn"], shares[1], sums["b_in"], shares[0],
        sums["b_back"], sums["gain_out"], sums["shift_out"],
    )


def columns_of_blocks(v, count, pieces):
    lanes = v.shape[1]
    v = v.reshape(pieces, count, -1, lanes)
    return jnp.moveaxis(v, 1, 2).reshape(-1, count * lanes)


def solution(mesh):
    rows = P(("dp", "head"), None)
    shard = P("dp", "head")
    return jax.shard_map(
        body,
        mesh=mesh,
        in_specs=(rows,) + (P(),) * 13 + (rows, P(("dp", "head"))),
        out_specs=(rows, rows, shard, P(), P(), shard, P(), P(), P(), shard, P(), shard, P(), P(), P()),
        check_vma=False,
    )
```

```python
import functools

import jax
import jax.numpy as jnp
from jax import lax
from jax.experimental import pallas as pl
from jax.experimental.pallas import tpu as pltpu
from jax.sharding import PartitionSpec as P

HEADS = 12
HEAD_DIM = 64
LEN = 512
CAP = 320
TALL = 384
ROWS = 256
SMALL = 32
TILE = 64
SLOTS = (CAP // TILE + 1) * TILE
QUAD = 4 * HEAD_DIM


def cost(flops):
    return pl.CostEstimate(flops=flops, bytes_accessed=1000, transcendentals=0)


epsilon = 1e-12
bf16 = jnp.bfloat16
f32 = jnp.float32


def params(mib):
    return pltpu.CompilerParams(vmem_limit_bytes=mib * 1024 * 1024)


def mm(a, b):
    return jnp.dot(a, b, preferred_element_type=f32)


def mm_nt(a, b):
    return lax.dot_general(a, b, (((1,), (1,)), ((), ())), preferred_element_type=f32)


def mm_tn(a, b):
    return lax.dot_general(a, b, (((0,), (0,)), ((), ())), preferred_element_type=f32)


def colsum(v):
    return jnp.sum(v, axis=0, keepdims=True)


def rowmean(v):
    return jnp.sum(v, axis=-1, keepdims=True) * (1.0 / v.shape[-1])


def norm_parts(v):
    centred = v - rowmean(v)
    r = lax.rsqrt(rowmean(centred * centred) + epsilon)
    return centred * r, r


def norm_back(cot, nhat, r, gain):
    e = cot * gain
    return r * (e - rowmean(e) - nhat * rowmean(e * nhat))


def erf_of(v):
    return lax.erf(v * 0.7071067811865476)


def lane_masks():
    head = lax.broadcasted_iota(jnp.int32, (1, QUAD), 1) // HEAD_DIM
    return [(head == j).astype(f32).astype(bf16) for j in range(4)]


def spread(x, masks):
    return jnp.concatenate([x * m for m in masks], axis=0)


def softmax_columns(scores):
    e = jnp.exp(scores - jnp.max(scores, axis=0, keepdims=True))
    return e, 1.0 / jnp.sum(e, axis=0, keepdims=True)


def join_tiles(first, second):
    low = lax.broadcasted_iota(jnp.int32, (HEAD_DIM, 2 * TILE), 1) < TILE
    top = jnp.where(low, first[:HEAD_DIM], pltpu.roll(second[:HEAD_DIM], TILE, 1))
    bottom = jnp.where(low, pltpu.roll(first[HEAD_DIM:], TILE, 1), second[HEAD_DIM:])
    return jnp.concatenate([top, bottom], axis=0)


def nothing(i, value):
    pass


def pipelined(count, early, middle, late):
    ahead = early(0)
    waiting = None
    for i in range(count):
        now, ahead = ahead, early(i + 1) if i + 1 < count else None
        if waiting is not None:
            late(i - 1, waiting)
        waiting = middle(i, now)
    late(count - 1, waiting)


class Mover:
    def __init__(self, sems):
        self.sems = sems
        self.count = 0

    def start(self, src, dst):
        copy = pltpu.make_async_copy(src, dst, self.sems.at[self.count])
        self.count += 1
        copy.start()
        return copy


def marked_forward_kernel(
    core_ref, m_ref, bq_ref, bv_ref, bo_ref, g1_ref, s1_ref, bi_ref, bb_ref, g2_ref,
    tok_h, gout_h, wqkv_h, wout_h, win_h, wback_h,
    sel_h, kv_h, tokc_h, qs_h, p_h, ctx_h, hl_h, act_h, bbr_h, bin_h, xsend_h, battn_h, bctx_h, bpre_h, small_ref,
    tok, gout, wqkv, wout, win, wback,
    sel, kv, tokc, gc, qs, prob, ctx, nhat, rr, hidden, hl, act, gp, branch, bbr, bin_, bv, bi, vt,
    battn, bctx, bpre,
    sems,
):
    rows, width = tok.shape
    ff = win.shape[1]
    quads = width // QUAD
    mover = Mover(sems)
    other = 1 - core_ref[0]
    c_tok = mover.start(tok_h, tok)
    c_wqkv = mover.start(wqkv_h, wqkv)
    c_gout = mover.start(gout_h, gout)
    c_wout = mover.start(wout_h, wout)
    c_win = mover.start(win_h, win)
    c_wback = mover.start(wback_h, wback)
    outs = []
    bv[...] = bv_ref[...].reshape(bv.shape)
    bi[...] = bi_ref[...].reshape(bi.shape)
    m8 = m_ref[...].astype(f32)
    groups = m8.shape[0]
    per_seq = LEN // 128
    tri = (
        lax.broadcasted_iota(jnp.int32, (128, 128), 0)
        <= lax.broadcasted_iota(jnp.int32, (128, 128), 1)
    ).astype(f32).astype(bf16)
    within = mm(m8.astype(bf16), tri)
    first = jnp.sum(m8[:per_seq], axis=(0, 1), keepdims=True)
    a0 = jnp.floor((first + (TILE - 1)) * (1.0 / TILE)) * TILE
    offset = jnp.zeros((1, 1), f32)
    slot_iota = lax.broadcasted_iota(jnp.int32, (SLOTS, 128), 0).astype(f32)
    for g in range(groups):
        if g == per_seq:
            offset = a0
        slot = jnp.where(m8[g : g + 1] > 0.0, offset + within[g : g + 1] - 1.0, -1.0)
        sel[:, 128 * g : 128 * (g + 1)] = (slot_iota == slot).astype(f32).astype(bf16)
        offset = offset + within[g : g + 1, 127:128]
    outs.append(mover.start(sel, sel_h))
    a0_scalar = jnp.sum(a0).astype(jnp.int32)

    c_tok.wait()
    tokc[...] = mm(sel[...], tok[...]).astype(bf16)
    outs.append(mover.start(tokc, tokc_h))
    c_wqkv.wait()
    for q in range(rows // LEN):
        for i in range(2 * width // QUAD):
            at = slice(i * QUAD, (i + 1) * QUAD)
            value = mm(tok[q * LEN : (q + 1) * LEN, :], wqkv[:, width + i * QUAD : width + (i + 1) * QUAD])
            if i >= quads:
                low = (value + bv[:, i * QUAD - width : (i + 1) * QUAD - width]).astype(bf16)
                vt[q, i * QUAD - width : (i + 1) * QUAD - width, :] = low.T
                kv[q, :, at] = low
            else:
                kv[q, :, at] = value.astype(bf16)
    outs.append(mover.start(kv, kv_h))
    qs[...] = (
        (mm(tokc[...], wqkv[:, :width]) + bq_ref[...]).astype(bf16).astype(f32) * HEAD_DIM**-0.5
    ).astype(bf16)
    outs.append(mover.start(qs, qs_h))

    masks = lane_masks()
    steps = [(t, g, w) for t in range(SLOTS // (2 * TILE)) for g in range(quads) for w in range(2)]
    kept = {}

    def place_of(i):
        t, g, w = steps[i]
        r0 = (2 * t + w) * TILE
        return r0, (r0 >= a0_scalar).astype(jnp.int32), slice(g * QUAD, (g + 1) * QUAD)

    def scores(i):
        r0, q, lanes = place_of(i)
        return mm_nt(kv[q, :, lanes], spread(qs[r0 : r0 + TILE, lanes], masks))

    def probabilities(i, s):
        t, g, w = steps[i]
        e, inv = softmax_columns(s)
        p = (e * inv).astype(bf16)
        prob[(2 * t + w) * quads + g] = p
        return p

    def values(i, p):
        t, g, w = steps[i]
        r0, q, lanes = place_of(i)
        kept[w] = mm(vt[q, lanes, :], p)
        if w == 1:
            for h in range(2):
                part = slice(128 * h, 128 * (h + 1))
                ctx[g * QUAD + 128 * h : g * QUAD + 128 * (h + 1), 128 * t : 128 * (t + 1)] = join_tiles(
                    kept[0][part, part], kept[1][part, part]
                ).astype(bf16)

    pipelined(len(steps), scores, probabilities, values)
    outs.append(mover.start(prob, p_h))
    outs.append(mover.start(ctx, ctx_h))
    c_wout.wait()
    pre = mm(ctx[...].T, wout[...]) + bo_ref[...] + tokc[...].astype(f32)
    nh, r = norm_parts(pre)
    nhat[...] = nh
    rr[...] = jnp.broadcast_to(r, rr.shape)
    hid = nh * g1_ref[...] + s1_ref[...]
    hidden[...] = hid
    hl[...] = hid.astype(bf16)
    outs.append(mover.start(hl, hl_h))
    outs.append(mover.start(hl, xsend_h.at[:, ff : ff + width]))
    c_gout.wait()
    gc[...] = mm(sel[...], gout[...]).astype(bf16)
    c_win.wait()

    c_wback.wait()
    forward = [(j, m) for j in range(0, ff, 256) for m in range(0, SLOTS, 128)]

    def inner(i):
        j, m = forward[i]
        return mm(hl[m : m + 128, :], win[:, j : j + 256])

    def gelu(i, v):
        j, m = forward[i]
        v = v + bi[:, j : j + 256]
        cdf = 0.5 + 0.5 * erf_of(v)
        act[m : m + 128, j : j + 256] = (v * cdf).astype(bf16)
        phi = jnp.exp2(v * v * (-0.5 * 1.4426950408889634)) * 0.3989422804014327
        gp[m : m + 128, j : j + 256] = cdf + v * phi

    pipelined(len(forward), inner, gelu, nothing)
    outs.append(mover.start(act, act_h))
    outs.append(mover.start(act, xsend_h.at[:, :ff]))
    for m in range(0, SLOTS, 128):
        for k in range(0, width, 256):
            branch[m : m + 128, k : k + 256] = mm(act[m : m + 128, :], wback[:, k : k + 256])
    steps = [(j, 0) for j in range(0, ff, 256)]
    nh2, r2 = norm_parts(hidden[...] + branch[...] + bb_ref[...])
    cot = gc[...].astype(f32)
    bs = norm_back(cot, nh2, r2, g2_ref[...])
    bl = bs.astype(bf16)
    bbr[...] = bl
    outs.append(mover.start(bbr, bbr_h))
    half = width // 2
    outs.append(
        mover.start(
            bbr.at[:, pl.ds(pl.multiple_of(other * half, half), half)],
            xsend_h.at[:, ff + width : ff + width + half],
        )
    )
    small_ref[:, :width] = colsum(cot * nh2)
    small_ref[:, width : 2 * width] = colsum(cot)
    small_ref[:, 2 * width : 3 * width] = colsum(bl.astype(f32))

    branch[...] = bs

    def back_active(i):
        j, m = steps[i]
        return mm_nt(bbr[m : m + SLOTS, :], wback[j : j + 256, :])

    def back_gelu(i, v):
        j, m = steps[i]
        b = (v * gp[m : m + SLOTS, j : j + 256]).astype(bf16)
        bin_[m : m + SLOTS, j : j + 256] = b
        part = colsum(b.astype(f32))
        at = slice(3 * width + j, 3 * width + j + 256)
        small_ref[:, at] = part if m == 0 else small_ref[:, at] + part

    pipelined(len(steps), back_active, back_gelu, nothing)
    outs.append(mover.start(bin_, bin_h))
    outs.append(
        mover.start(
            bin_.at[:, pl.ds(pl.multiple_of(other * (ff // 2), ff // 2), ff // 2)],
            xsend_h.at[:, ff + width + half :],
        )
    )
    for m in range(0, SLOTS, SLOTS):
        for k in range(0, width, 256):
            branch[m : m + SLOTS, k : k + 256] += mm_nt(bin_[m : m + SLOTS, :], win[k : k + 256, :])
    back_hidden = branch[...]
    nh = nhat[...]
    bp = norm_back(back_hidden, nh, rr[:, :1], g1_ref[...])
    bpre[...] = bp
    outs.append(mover.start(bpre, bpre_h))
    bl = bp.astype(bf16)
    battn[...] = bl
    outs.append(mover.start(battn, battn_h))
    bctx[...] = mm_nt(bl, wout[...]).astype(bf16)
    outs.append(mover.start(bctx, bctx_h))
    at = 3 * width + ff
    small_ref[:, at : at + width] = colsum(bl.astype(f32))
    small_ref[:, at + width : at + 2 * width] = colsum(back_hidden * nh)
    small_ref[:, at + 2 * width : at + 3 * width] = colsum(back_hidden)
    for copy in outs:
        copy.wait()


def marked_forward(core, m8, tokens, gout, w_qkv, b_query, b_value, w_out, b_out, g1, s1, w_in, b_in, w_back, b_back, g2):
    rows, width = tokens.shape
    ff = w_in.shape[1]
    tiles = SLOTS // TILE * (width // QUAD)
    outs = dict(
        sel=((SLOTS, rows), bf16), kv=((rows // LEN, LEN, 2 * width), bf16), tokc=((SLOTS, width), bf16),
        qs=((SLOTS, width), bf16), p=((tiles, LEN, 4 * TILE), bf16), ctx=((width, SLOTS), bf16),
        hl=((SLOTS, width), bf16),
        act=((SLOTS, ff), bf16), bbr=((SLOTS, width), bf16), bin=((SLOTS, ff), bf16),
        xsend=((SLOTS, (ff + width) * 3 // 2), bf16), battn=((SLOTS, width), bf16), bctx=((SLOTS, width), bf16),
        bpre=((SLOTS, width), f32), small=((1, 6 * width + ff), f32),
    )
    scratch = [
        ((rows, width), bf16), ((rows, width), bf16), (w_qkv.shape, bf16), (w_out.shape, bf16),
        (w_in.shape, bf16), (w_back.shape, bf16),
        outs["sel"], outs["kv"], outs["tokc"], ((SLOTS, width), bf16), outs["qs"], outs["p"], outs["ctx"],
        ((SLOTS, width), f32), ((SLOTS, 128), f32), ((SLOTS, width), f32), outs["hl"], outs["act"], ((SLOTS, ff), f32),
        ((SLOTS, width), f32), outs["bbr"], outs["bin"], ((1, width), f32), ((1, ff), f32),
        ((rows // LEN, width, LEN), bf16), outs["battn"], outs["bctx"], outs["bpre"],
    ]
    vmem = pl.BlockSpec(memory_space=pltpu.VMEM)
    smem = pl.BlockSpec(memory_space=pltpu.SMEM)
    hbm = pl.BlockSpec(memory_space=pl.ANY)
    res = pl.pallas_call(
        marked_forward_kernel,
        out_shape=[jax.ShapeDtypeStruct(*o) for o in outs.values()],
        in_specs=[smem] + [vmem] * 9 + [hbm] * 6,
        out_specs=[hbm] * 14 + [vmem],
        scratch_shapes=[pltpu.VMEM(*s) for s in scratch] + [pltpu.SemaphoreType.DMA((32,))],
        compiler_params=params(60),
        cost_estimate=cost(14375000000),
        name="marked_forward",
    )(core, m8, b_query, b_value, b_out, g1, s1, b_in, b_back, g2,
      tokens, gout, w_qkv, w_out, w_in, w_back)
    return dict(zip(outs, res))


def place(piece, own, core, orders):
    bits = piece ^ own
    spots = []
    for order in orders:
        spot = 0
        for step in order:
            spot = spot * 2 + ((bits >> step) & 1)
        spots.append(spot)
    return spots[core] if isinstance(core, int) else spots[0] + core * (spots[1] - spots[0])


def marked_backward_kernel(
    where, m_ref, small_a, wqkv_h, bpre_h, bctx_h, p_h, qs_h, kv_h, tok_h, tokc_h, ctx_h, battn_h,
    bkv_h, rc_h, keep_h, send_h, small_h,
    wq, bpre, bctx, prob, qs, kv, tok, tokc, ctx, battn, dk, dv, bqt, bq, bkv, rc, kt, tokt, short, out, small, low,
    sems, *, pieces, orders,
):
    slots, width = qs.shape
    rows = tok.shape[0]
    quads = width // QUAD
    half = width // 2
    own, core = where[0], where[1]
    block = width // pieces
    size = 4 * block
    mover = Mover(sems)
    c_first = [mover.start(ctx_h, ctx), mover.start(battn_h, battn)]
    c_kv = [mover.start(kv_h, kv), mover.start(bctx_h, bctx), mover.start(qs_h, qs)]
    group = 2 * quads
    c_p = [
        mover.start(p_h.at[i : i + group], prob.at[i : i + group]) for i in range(0, prob.shape[0], group)
    ]
    c_tok = [mover.start(tok_h, tok), mover.start(tokc_h, tokc)]
    c_wq = mover.start(wqkv_h.at[:, :width], wq)
    c_bpre = mover.start(bpre_h, bpre)
    per_seq = LEN // 128
    first = jnp.sum(m_ref[:per_seq].astype(f32), axis=(0, 1), keepdims=True)
    a0_scalar = jnp.sum(jnp.floor((first + (TILE - 1)) * (1.0 / TILE)) * TILE).astype(jnp.int32)
    dk[...] = jnp.zeros_like(dk)
    dv[...] = jnp.zeros_like(dv)

    def products(left, right, chunks):
        for m in range(0, width, half):
            g = mm(left[m : m + half, :], right).astype(bf16)
            for c, (owner, chunk) in enumerate(chunks):
                for k in range(half // block):
                    at = place(m // block + k, own, owner, orders) * size + chunk * block
                    out[owner ^ core, pl.ds(pl.multiple_of(at, block), block), :] = g[
                        k * block : (k + 1) * block, c * half : (c + 1) * half
                    ]

    for c in c_first:
        c.wait()
    products(ctx, battn[...], ((0, 3), (1, 3)))
    for c in c_kv:
        c.wait()
    for q in range(kv.shape[0]):
        for g in range(quads):
            lanes = slice(g * QUAD, (g + 1) * QUAD)
            kt[q, lanes, :] = kv[q, :, lanes].T
    masks = lane_masks()
    steps = [(t, g, w) for t in range(slots // (2 * TILE)) for g in range(quads) for w in range(2)]
    kept = {}

    def place_of(i):
        t, g, w = steps[i]
        r0 = (2 * t + w) * TILE
        return r0, (r0 >= a0_scalar).astype(jnp.int32), slice(g * QUAD, (g + 1) * QUAD)

    def back_probs(i):
        t, g, w = steps[i]
        if g == 0 and w == 0:
            c_p[t].wait()
        r0, q, lanes = place_of(i)
        d4 = spread(bctx[r0 : r0 + TILE, lanes], masks)
        dp = mm_nt(kv[q, :, width + g * QUAD : width + (g + 1) * QUAD], d4)
        dv[q, :, lanes] += mm(prob[(2 * t + w) * quads + g], d4)
        return dp

    def back_scores(i, dp):
        t, g, w = steps[i]
        p = prob[(2 * t + w) * quads + g].astype(f32)
        weighted = p * dp
        return (weighted - p * colsum(weighted)).astype(bf16)

    def back_query_key(i, ds):
        t, g, w = steps[i]
        r0, q, lanes = place_of(i)
        dk[q, :, lanes] += mm(ds, spread(qs[r0 : r0 + TILE, lanes], masks))
        kept[w] = mm(kt[q, lanes, :], ds)
        if w == 1:
            for h in range(2):
                part = slice(128 * h, 128 * (h + 1))
                bqt[g * QUAD + 128 * h : g * QUAD + 128 * (h + 1), 128 * t : 128 * (t + 1)] = (
                    join_tiles(kept[0][part, part], kept[1][part, part]) * HEAD_DIM**-0.5
                ).astype(bf16)

    pipelined(len(steps), back_probs, back_scores, back_query_key)
    for q in range(kv.shape[0]):
        at = slice(q * LEN, (q + 1) * LEN)
        bkv[at, :width] = dk[q].astype(bf16)
        bkv[at, width:] = dv[q].astype(bf16)
    outs = [mover.start(bkv, bkv_h)]
    bq[...] = bqt[...].T
    for c in c_tok:
        c.wait()
    tokt[...] = tok[...].T
    short[...] = tokc[...].T
    products(short, bq[...], ((0, 0), (0, 1)))
    products(tokt, bkv[:, :width], ((0, 2), (1, 0)))
    products(tokt, bkv[:, width:], ((1, 1), (1, 2)))
    first_rows = small_a.shape[1] // half
    small[...] = jnp.zeros_like(small)
    for i in range(first_rows):
        small[i : i + 1, :] = small_a[:, i * half : (i + 1) * half]
    for i, lanes in enumerate((slice(0, half), slice(half, width))):
        small[first_rows + i : first_rows + i + 1, :] = colsum(bq[:, lanes].astype(f32))
        small[first_rows + 2 + i : first_rows + 3 + i, :] = colsum(
            bkv[:, width + i * half : width + (i + 1) * half].astype(f32)
        )
    high = small[...].astype(bf16)
    low[:SMALL] = high
    low[SMALL:] = (small[...] - high.astype(f32)).astype(bf16)
    outs += [
        mover.start(out.at[1], send_h.at[: 4 * width, :]),
        mover.start(low, send_h.at[4 * width :, :]),
        mover.start(out.at[0], keep_h),
        mover.start(small, small_h),
    ]
    c_wq.wait()
    c_bpre.wait()
    rc[...] = (bpre[...] + mm_nt(bq[...], wq[...])).astype(bf16)
    outs.append(mover.start(rc, rc_h))
    for copy in outs:
        copy.wait()


def marked_backward(where, m8, tokens, w_qkv, a, pieces, orders):
    rows, width = tokens.shape
    half = width // 2
    outs = dict(
        bkv=((rows, 2 * width), bf16), rc=((SLOTS, width), bf16), keep=((4 * width, half), bf16),
        send=((4 * width + 2 * SMALL, half), bf16), small=((SMALL, half), f32),
    )
    ins = [a["bpre"], a["bctx"], a["p"], a["qs"], a["kv"], tokens, a["tokc"], a["ctx"], a["battn"]]
    scratch = [((width, width), bf16)] + [(v.shape, v.dtype) for v in ins]
    scratch += [
        ((rows // LEN, LEN, width), f32), ((rows // LEN, LEN, width), f32), ((width, SLOTS), bf16),
        ((SLOTS, width), bf16), outs["bkv"], outs["rc"], ((rows // LEN, width, LEN), bf16), ((width, rows), bf16),
        ((width, SLOTS), bf16), ((2, 4 * width, half), bf16), outs["small"], ((2 * SMALL, half), bf16),
    ]
    vmem = pl.BlockSpec(memory_space=pltpu.VMEM)
    smem = pl.BlockSpec(memory_space=pltpu.SMEM)
    hbm = pl.BlockSpec(memory_space=pl.ANY)
    res = pl.pallas_call(
        functools.partial(marked_backward_kernel, pieces=pieces, orders=orders),
        out_shape=[jax.ShapeDtypeStruct(*o) for o in outs.values()],
        in_specs=[smem, vmem, vmem] + [hbm] * 10,
        out_specs=[hbm] * 5,
        scratch_shapes=[pltpu.VMEM(*s) for s in scratch] + [pltpu.SemaphoreType.DMA((24,))],
        compiler_params=params(60),
        cost_estimate=cost(9775000000),
        name="marked_backward",
    )(where, m8, a["small"], w_qkv, *ins)
    return dict(zip(outs, res))


def attention_rows_kernel(
    which, bq_ref, bo_ref, g1_ref, s1_ref, tok_h, kv_h, wqkv_h, wout_h, hidden_h,
    tok, kv, wq, wout, q, ctx, hidden, vt, sems,
):
    width = wq.shape[1]
    quads = width // QUAD
    tile = 128
    mover = Mover(sems)
    i = which[0]
    r0 = pl.multiple_of(i * LEN, LEN)
    c_tok = mover.start(tok_h.at[pl.ds(r0, LEN), :], tok)
    c_wq = mover.start(wqkv_h.at[:, :width], wq)
    c_kv = mover.start(kv_h.at[i], kv)
    c_wout = mover.start(wout_h, wout)
    c_tok.wait()
    c_wq.wait()
    q[...] = ((mm(tok[...], wq[...]) + bq_ref[...]).astype(bf16).astype(f32) * HEAD_DIM**-0.5).astype(bf16)
    c_kv.wait()
    for g in range(quads):
        vt[g * QUAD : (g + 1) * QUAD, :] = kv[:, width + g * QUAD : width + (g + 1) * QUAD].T
    masks = lane_masks()
    steps = [(t, g) for t in range(LEN // tile) for g in range(quads)]

    def scores(i):
        t, g = steps[i]
        lanes = slice(g * QUAD, (g + 1) * QUAD)
        return mm_nt(kv[:, lanes], spread(q[t * tile : (t + 1) * tile, lanes], masks))

    def probabilities(i, s):
        e, inv = softmax_columns(s)
        return e.astype(bf16), inv

    def values(i, parts):
        t, g = steps[i]
        p, inv = parts
        for h in range(2):
            at = g * QUAD + 128 * h
            z = mm(vt[at : at + 128, :], p[:, h * 2 * tile : (h + 1) * 2 * tile])
            for u in range(2):
                tokens = slice((2 * h + u) * tile, (2 * h + u + 1) * tile)
                ctx[at + u * HEAD_DIM : at + (u + 1) * HEAD_DIM, t * tile : (t + 1) * tile] = (
                    z[u * HEAD_DIM : (u + 1) * HEAD_DIM, u * tile : (u + 1) * tile] * inv[:, tokens]
                ).astype(bf16)

    pipelined(len(steps), scores, probabilities, values)
    c_wout.wait()
    nh, _ = norm_parts(mm(ctx[...].T, wout[...]) + bo_ref[...] + tok[...].astype(f32))
    hid = nh * g1_ref[...] + s1_ref[...]
    hidden[...] = hid
    mover.start(hidden, hidden_h).wait()


def attention_rows(which, tokens, kv, w_qkv, b_query, w_out, b_out, g1, s1):
    width = tokens.shape[1]
    vmem = pl.BlockSpec(memory_space=pltpu.VMEM)
    smem = pl.BlockSpec(memory_space=pltpu.SMEM)
    hbm = pl.BlockSpec(memory_space=pl.ANY)
    scratch = [
        ((LEN, width), bf16), ((LEN, 2 * width), bf16), ((width, width), bf16), (w_out.shape, bf16),
        ((LEN, width), bf16), ((width, LEN), bf16), ((LEN, width), f32), ((width, LEN), bf16),
    ]
    return pl.pallas_call(
        attention_rows_kernel,
        out_shape=jax.ShapeDtypeStruct((LEN, width), f32),
        in_specs=[smem] + [vmem] * 4 + [hbm] * 4,
        out_specs=hbm,
        scratch_shapes=[pltpu.VMEM(*s) for s in scratch] + [pltpu.SemaphoreType.DMA((8,))],
        compiler_params=params(14),
        cost_estimate=cost(4025000000),
        name="attention_rows",
    )(jnp.full((1,), which, jnp.int32), b_query, b_out, g1, s1, tokens, kv, w_qkv, w_out)


def ffn_rows_kernel(
    which, bi_ref, bb_ref, g2_ref, s2_ref, hidden_h, win_h, wback_h, *rest,
):
    (out_h, win, wback, hl, hidden, act, branch, out, bi, sems) = rest[-10:]
    width, ff = win.shape
    mover = Mover(sems)
    r0 = pl.multiple_of(which[0] * LEN, LEN)
    c_hidden = mover.start(hidden_h, hidden)
    part = ff // 4
    c_win = [mover.start(win_h.at[:, k : k + part], win.at[:, k : k + part]) for k in range(0, ff, part)]
    c_wback = mover.start(wback_h, wback)
    bi[...] = bi_ref[...].reshape(bi.shape)
    c_hidden.wait()
    hl[...] = hidden[...].astype(bf16)
    steps = [(j, m) for j in range(0, ff, 256) for m in range(0, LEN, ROWS)]

    def inner(i):
        j, m = steps[i]
        if j % part == 0 and m == 0:
            c_win[j // part].wait()
        return mm(hl[m : m + ROWS, :], win[:, j : j + 256])

    def gelu(i, v):
        j, m = steps[i]
        v = v + bi[:, j : j + 256]
        h = v * 0.5
        act[m : m + ROWS, j : j + 256] = (h + h * erf_of(v)).astype(bf16)

    pipelined(len(steps), inner, gelu, nothing)
    c_wback.wait()
    for m in range(0, LEN, 256):
        for k in range(0, width, 256):
            branch[m : m + 256, k : k + 256] = mm(act[m : m + 256, :], wback[:, k : k + 256])
    nh2, _ = norm_parts(hidden[...] + branch[...] + bb_ref[...])
    out[...] = (nh2 * g2_ref[...] + s2_ref[...]).astype(bf16)
    mover.start(out, out_h.at[pl.ds(r0, LEN), :]).wait()


def ffn_rows(which, previous, rows, hidden, w_in, b_in, w_back, b_back, g2, s2):
    width, ff = w_in.shape
    vmem = pl.BlockSpec(memory_space=pltpu.VMEM)
    smem = pl.BlockSpec(memory_space=pltpu.SMEM)
    hbm = pl.BlockSpec(memory_space=pl.ANY)
    scratch = [
        (w_in.shape, bf16), (w_back.shape, bf16), ((LEN, width), bf16), ((LEN, width), f32), ((LEN, ff), bf16),
        ((LEN, width), f32), ((LEN, width), bf16), ((1, ff), f32),
    ]
    extra = () if previous is None else (previous,)
    return pl.pallas_call(
        ffn_rows_kernel,
        out_shape=jax.ShapeDtypeStruct((rows, width), bf16),
        in_specs=[smem] + [vmem] * 4 + [hbm] * (3 + len(extra)),
        out_specs=hbm,
        scratch_shapes=[pltpu.VMEM(*s) for s in scratch] + [pltpu.SemaphoreType.DMA((12,))],
        input_output_aliases={8: 0} if extra else {},
        compiler_params=params(22),
        cost_estimate=cost(5175000000),
        name="ffn_rows",
    )(jnp.full((1,), which, jnp.int32), b_in, b_back, g2, s2, hidden, w_in, w_back, *extra)


def ffn_grads_kernel(
    where, act_h, hl_h, bbr_h, bin_h, x_h, keep1_h, send1_h, keep2_h, send2_h,
    act, hl, bbr, bin_, out1, out2, hlt, sems, *, pieces, orders,
):
    own, core = where[0], where[1]
    slots, ff = act_h.shape
    width = hl_h.shape[1]
    half = width // 2
    mover = Mover(sems)
    up, down = slice(0, slots), slice(slots, 2 * slots)
    mine = lambda n: pl.ds(pl.multiple_of(core * n, n), n)
    c2 = [
        mover.start(hl_h, hl.at[up, :]),
        mover.start(x_h.at[:, ff : ff + width], hl.at[down, :]),
    ]
    c_in = []
    for k in range(0, ff // 2, width):
        lanes = slice(k, k + width)
        there = pl.ds(pl.multiple_of(core * (ff // 2) + k, width), width)
        first = ff + width + half + k
        c_in.append(
            (
                mover.start(bin_h.at[:, there], bin_.at[up, lanes]),
                mover.start(x_h.at[:, first : first + width], bin_.at[down, lanes]),
            )
        )
    c1 = [
        mover.start(bbr_h.at[:, mine(half)], bbr.at[up, :]),
        mover.start(x_h.at[:, ff + width : ff + width + half], bbr.at[down, :]),
    ]
    c_act = []
    for k in range(0, ff, width):
        lanes = slice(k, k + width)
        c_act.append(
            (mover.start(act_h.at[:, lanes], act.at[up, lanes]), mover.start(x_h.at[:, lanes], act.at[down, lanes]))
        )
    size, block = ff // pieces, width // pieces
    for c in c2:
        c.wait()
    hlt[...] = hl[...].T
    for j in range(ff // 2 // width):
        for c in c_in[j]:
            c.wait()
        for m in range(0, width, TALL):
            g = mm(hlt[m : m + TALL, :], bin_[:, j * width : (j + 1) * width]).astype(bf16)
            for c in range(2):
                for k in range(TALL // block):
                    at = place(m // block + k, own, core, orders[1]) * size + (2 * j + c) * block
                    out2[pl.ds(pl.multiple_of(at, block), block), :] = g[
                        k * block : (k + 1) * block, c * half : (c + 1) * half
                    ]
    rows = ff // 2
    outs = [mover.start(out2.at[rows:, :], send2_h), mover.start(out2.at[:rows, :], keep2_h)]
    for c in c1:
        c.wait()
    for j in range(ff // half):
        if j % 2 == 0:
            for c in c_act[j // 2]:
                c.wait()
        g = mm_tn(act[:, j * half : (j + 1) * half], bbr[...]).astype(bf16)
        for k in range(half // size):
            at = place(j * (half // size) + k, own, core, orders[0]) * size
            out1[pl.ds(pl.multiple_of(at, size), size), :] = g[k * size : (k + 1) * size]
    outs += [mover.start(out1.at[rows:, :], send1_h), mover.start(out1.at[:rows, :], keep1_h)]
    for c in outs:
        c.wait()


def ffn_grads(where, a, x, pieces, orders):
    slots, ff = a["act"].shape
    width = a["hl"].shape[1]
    half = width // 2
    smem = pl.BlockSpec(memory_space=pltpu.SMEM)
    hbm = pl.BlockSpec(memory_space=pl.ANY)
    scratch = [
        (2 * slots, ff), (2 * slots, width), (2 * slots, half), (2 * slots, ff // 2), (ff, half), (ff, half),
        (width, 2 * slots),
    ]
    return pl.pallas_call(
        functools.partial(ffn_grads_kernel, pieces=pieces, orders=orders),
        out_shape=[jax.ShapeDtypeStruct((ff // 2, half), bf16)] * 4,
        in_specs=[smem] + [hbm] * 5,
        out_specs=[hbm] * 4,
        scratch_shapes=[pltpu.VMEM(s, bf16) for s in scratch] + [pltpu.SemaphoreType.DMA((24,))],
        compiler_params=params(20),
        cost_estimate=cost(5175000000),
        name="ffn_grads",
    )(where, a["act"], a["hl"], a["bbr"], a["bin"], x)


def small_sums_kernel(small_ref, *outs):
    at = 0
    for out in outs:
        width = small_ref.shape[1]
        for i in range(out.shape[0] // width):
            out[i * width : (i + 1) * width] = small_ref[at, :]
            at += 1


def small_sums(small, sizes):
    vmem = pl.BlockSpec(memory_space=pltpu.VMEM)
    return pl.pallas_call(
        small_sums_kernel,
        out_shape=[jax.ShapeDtypeStruct((size,), f32) for size in sizes],
        in_specs=[vmem],
        out_specs=[vmem] * len(sizes),
        cost_estimate=cost(575000000),
        name="small_sums",
    )(small)


def add_low(a, b):
    return (a.astype(f32) + b.astype(f32)).astype(bf16)


def after(value, *others):
    return lax.optimization_barrier((value, others))[0]


def two_parts(v):
    high = lax.reduce_precision(v, 8, 7)
    return [high.astype(bf16), (v - high).astype(bf16)]


def one_part(v):
    return v[:SMALL].astype(f32) + v[SMALL:].astype(f32)


def total(parts, first, last):
    return sum(part[first:last].astype(f32) for part in parts)


class Reduction:
    def __init__(self, keep, send, orders, n, small=None):
        self.parts, self.send, self.orders, self.n, self.small = [keep], send, orders, n, small
        self.rows = keep.shape[0]
        self.step = 0
        self.start()

    def start(self):
        pairs = self.pairs()
        send = self.send
        if self.small is not None:
            send = jnp.concatenate([send] + two_parts(self.small))
        self.got = lax.ppermute(send, ("dp", "head"), pairs)

    def pairs(self):
        return [
            (2 * i + core, 2 * (i ^ (1 << self.orders[core][self.step])) + core)
            for i in range(self.n)
            for core in range(2)
        ]

    def advance(self, *others, go=True):
        parts, got, small = after((self.parts, self.got, self.small), *others)
        self.step += 1
        if small is not None:
            self.small = small + one_part(got[self.rows :])
        self.parts = parts + [got]
        if self.step == len(self.orders[0]):
            self.share = total(self.parts, 0, self.rows)
            return self.share
        self.rows //= 2
        self.send = total(self.parts, self.rows, 2 * self.rows).astype(bf16)
        if go:
            self.start()
        return self.send


def columns(share, count):
    rows = share.shape[0] // count
    return jnp.concatenate([share[i * rows : (i + 1) * rows] for i in range(count)], axis=1)


def body(
    tokens, w_qkv, b_query, b_value, w_out, b_out, gain_attn, shift_attn, w_in, b_in, w_back, b_back,
    gain_out, shift_out, grad_out, masked,
):
    rows, width = tokens.shape
    ff = w_in.shape[1]
    n = lax.axis_size("dp")
    core = lax.axis_index("head")
    steps = n.bit_length() - 1
    halving = n == 1 << steps and width // n % 16 == 0
    if halving:
        own = lax.axis_index("dp")
        rest = tuple(range(3, steps))
        plane_first = ((0, 1, 2) + rest, (1, 0, 2) + rest)
        line_first = ((2, 0, 1) + rest, (2, 1, 0) + rest)
        orders = [plane_first, line_first, plane_first]
        pieces = n
    else:
        own = jnp.int32(0)
        orders = [((3, 2, 1, 0),) * 2] * 3
        pieces = 16
    where = jnp.stack([own, core]).astype(jnp.int32)
    m8 = masked.reshape(-1, 128)
    swap_cores = lambda v: lax.ppermute(v, "head", [(0, 1), (1, 0)])

    a = marked_forward(
        core.reshape(1).astype(jnp.int32), m8, tokens, grad_out, w_qkv, b_query, b_value, w_out, b_out,
        gain_attn, shift_attn, w_in, b_in, w_back, b_back, gain_out,
    )
    x = swap_cores(a["xsend"])
    b = marked_backward(where, m8, tokens, w_qkv, a, pieces, orders[2])
    got3 = swap_cores(b["send"])
    keep1, send1, keep2, send2 = ffn_grads(after(where, b["rc"]), a, x, pieces, orders[:2])
    keep3, got3, small = after((b["keep"], got3, b["small"]), keep1)
    small = small + one_part(got3[4 * width :])
    m = 2 * width
    if halving:
        r1 = Reduction(keep1, send1, orders[0], n, small)
        r2 = Reduction(keep2, send2, orders[1], n)
        r3 = Reduction(
            add_low(keep3[:m], got3[:m]), add_low(keep3[m:], got3[m : 2 * m]), orders[2], n
        )
        done = r3.send
    else:
        r1 = r2 = r3 = None
        both3 = done = add_low(keep3, got3[: 2 * m])

    def attention(which, done):
        return attention_rows(which, after(tokens, done), a["kv"], w_qkv, b_query, w_out, b_out, gain_attn, shift_attn)

    def ffn(which, previous, hidden, done):
        return ffn_rows(which, previous, rows, after(hidden, done), w_in, b_in, w_back, b_back, gain_out, shift_out)

    def turn(done, *chains):
        if halving:
            sent = ()
            for chain in chains:
                sent += (chain.advance(done, *sent),)
            return sent
        return done

    hidden = attention(0, done)
    done = turn(hidden, r1)
    layer_out = ffn(0, None, hidden, done)
    done = turn(layer_out, r1, r2, r3)
    hidden = attention(1, done)
    done = turn(hidden, r1, r2, r3)
    layer_out = ffn(1, layer_out, hidden, done)
    if halving:
        done = (r2.advance(layer_out, go=False), r3.advance(layer_out, go=False))
        got = lax.ppermute(jnp.concatenate(done), ("dp", "head"), r2.pairs())
        r2.got, r3.got = got[: r2.rows], got[r2.rows :]
        done += (r1.advance(layer_out, *done),)
    else:
        done = (layer_out,)
    sel, wkv = after((a["sel"], w_qkv[:, width:]), done)
    grad_tokens = mm_tn(sel, b["rc"]) + mm_nt(b["bkv"], wkv)
    turn(grad_tokens, r2, r3)
    if halving:
        shares = [r1.share, r2.share, r3.share]
        small = r1.small
    else:
        spread_out = lambda v: lax.psum_scatter(v, "dp", scatter_dimension=0, tiled=True).astype(f32)
        natural = lambda v, count: columns_of_blocks(v, count, pieces)
        small = lax.psum(small, "dp")
        shares = [
            spread_out(jnp.concatenate([keep1, send1])),
            spread_out(natural(jnp.concatenate([keep2, send2]), 4)),
            spread_out(natural(both3, 4)),
        ]
    names = (("gain_out", width), ("shift_out", width), ("b_back", width), ("b_in", ff), ("b_out", width),
             ("gain_attn", width), ("shift_attn", width), ("b_query", width), ("b_value", width))
    sums = dict(zip([name for name, _ in names], small_sums(small, [size for _, size in names])))
    if halving:
        shares[1] = columns(shares[1], 4)
        shares[2] = columns(shares[2], 4)
    half3 = 3 * width // 2
    return (
        layer_out, grad_tokens, shares[2][:, :half3], sums["b_query"], sums["b_value"], shares[2][:, half3:],
        sums["b_out"], sums["gain_attn"], sums["shift_attn"], shares[1], sums["b_in"], shares[0],
        sums["b_back"], sums["gain_out"], sums["shift_out"],
    )


def columns_of_blocks(v, count, pieces):
    lanes = v.shape[1]
    v = v.reshape(pieces, count, -1, lanes)
    return jnp.moveaxis(v, 1, 2).reshape(-1, count * lanes)


def solution(mesh):
    rows = P(("dp", "head"), None)
    shard = P("dp", "head")
    return jax.shard_map(
        body,
        mesh=mesh,
        in_specs=(rows,) + (P(),) * 13 + (rows, P(("dp", "head"))),
        out_specs=(rows, rows, shard, P(), P(), shard, P(), P(), P(), shard, P(), shard, P(), P(), P()),
        check_vma=False,
    )
```
